32 devices in a mesh: tensor: 4 (over x, core), dp: 2 (over y), context: 4 (over z).
Axes of the slice: x: 2, y: 2, z: 4, core: 2. Of those that a mesh axis runs over, the one named last changes fastest.
Arguments:
- tokens: bfloat16 [2, 2048, 2048], P('dp', 'context'), may hold values from -6 to 6
- segments: int32 [2, 2048], P('dp', 'context'), may hold values from 0 to 2047, as said below
- gain_one: float32 [2048], replicated, may hold values from 0.1 to 1.9
- w_query: bfloat16 [2048, 2048], P(None, 'tensor'), may hold values from -0.125 to 0.125
- w_keyval: bfloat16 [2048, 4, 128], P(None, 'tensor'), may hold values from -0.125 to 0.125
- w_out: bfloat16 [2048, 2048], P('tensor'), may hold values from -1 to 1
- gain_two: float32 [2048], replicated, may hold values from 0.1 to 1.9
- w_gateup: bfloat16 [2048, 2, 5632], P(None, None, 'tensor'), may hold values from -0.125 to 0.125
- w_down: bfloat16 [5632, 2048], P('tensor'), may hold values from -0.078125 to 0.078125
- cotangent: bfloat16 [2, 2048, 2048], P('dp', 'context'), may hold values from -6 to 6
Outputs:
- mixed: bfloat16 [2, 2048, 2048], P('dp', 'context')
- grad_tokens: float32 [2, 2048, 2048], P('dp', 'context')
- grad_gain_one: float32 [2048], P(('dp', 'context'))
- grad_wquery: float32 [2048, 2048], P(('dp', 'context'), 'tensor')
- grad_wkeyval: float32 [2048, 4, 128], P(('dp', 'context'), 'tensor')
- grad_wout: float32 [2048, 2048], P('tensor', ('dp', 'context'))
- grad_gain_two: float32 [2048], P(('dp', 'context'))
- grad_wgateup: float32 [2048, 2, 5632], P(('dp', 'context'), None, 'tensor')
- grad_wdown: float32 [5632, 2048], P('tensor', ('dp', 'context'))
The draws below stay inside these ranges and needn't reach their ends.
Inputs may be any that keep to these rules, and one draw needn't show every extreme that they name: `segments`: each token holds the index, within its sequence, of its document's first token, so values never fall along a sequence. In each sequence one document begins among the first 512 tokens and ends among the last 512, and the last token begins a document of its own.
All inputs are finite; a program needn't handle non-finite values.
Results may differ from the reference program's by a relative error of at most 0.024.
Values may be sent and summed in bfloat16 or wider, within the bound.
A program may use at most 256 MiB of HBM per device.

```python
import math
import jax
import jax.numpy as jnp
from jax import lax

D = 2048
FF = 5632
HQ = 32
HK = 4
HD = 64
TOK_CTX = 512
LEN = 2048
SEQS = 2


def draw_segments(key, part):
    key = jax.random.fold_in(key, 7)
    key_start, key_stop, key_marks = jax.random.split(key, 3)
    begin = jax.random.randint(key_start, (SEQS, 1), 1, TOK_CTX)
    finish = LEN - jax.random.randint(key_stop, (SEQS, 1), 1, TOK_CTX)
    marks = jax.random.randint(key_marks, (SEQS, LEN), 0, 96)
    places = jnp.arange(LEN, dtype=jnp.int32)[None, :]
    outside = (places < begin) | (places > finish)
    boundary = (places == begin) | (places == finish) | (places == LEN - 1) | (marks == 0) & outside
    starts = jnp.where(boundary, places, 0).astype(jnp.int32)
    return lax.cummax(starts, axis=1).astype(jnp.int32)


def shard_levels(own_key, dims, cuts, low, top_value):
    level = 1.0
    for position, blocks in cuts:
        steps = jax.random.uniform(jax.random.fold_in(jax.random.fold_in(own_key, 6), position), (blocks,), jnp.float32, low / len(cuts), top_value / len(cuts))
        level = level * jnp.repeat(jnp.exp(steps), dims[position] // blocks).reshape((-1,) + (1,) * (len(dims) - 1 - position))
    return level


def noise(own_key, shape, deviation, bound, cuts=(), kind=jnp.bfloat16):
    values = jax.random.normal(own_key, shape, jnp.float32) * deviation
    if len(cuts) > 0:
        values = shard_levels(own_key, shape, cuts, -0.22, 0.18) * values
    return jnp.clip(values, min=-bound, max=bound).astype(kind)


def setup_inputs(seed: int = 0) -> dict:
    key_of = jax.random.split(jax.random.key(seed), 11)
    return {
        "tokens": noise(key_of[0], (SEQS, LEN, D), 1.0, 6.0, ((0, 2), (1, 4))),
        "segments": draw_segments(jax.random.fold_in(key_of[10], 71), 0),
        "gain_one": jnp.clip(1.0 + 0.18 * jax.random.normal(key_of[2], (D,), jnp.float32), 0.1, 1.9),
        "w_query": noise(key_of[3], (D, HQ * HD), D ** -0.5, 0.125, ((1, 4),)),
        "w_keyval": noise(key_of[4], (D, HK, 2 * HD), D ** -0.5, 0.125, ((1, 4),)),
        "w_out": noise(key_of[5], (HQ * HD, D), (HQ * HD // 64) ** -0.5, 1.0, ((0, 4),)),
        "gain_two": jnp.clip(1.0 + 0.18 * jax.random.normal(key_of[6], (D,), jnp.float32), 0.1, 1.9),
        "w_gateup": noise(key_of[7], (D, 2, FF), D ** -0.5, 0.125, ((2, 4),)),
        "w_down": noise(key_of[8], (FF, D), FF ** -0.5, 0.078125, ((0, 4),)),
        "cotangent": noise(key_of[9], (SEQS, LEN, D), 1.0, 6.0, ((0, 2), (1, 4))),
    }


@jax.custom_vjp
def low(v):
    return lax.optimization_barrier(v.astype(jnp.bfloat16)).astype(jnp.float32)

@jax.custom_vjp
def low_back(v):
    return v

def low_keep(v):
    return (low(v), None)

def low_pass(kept, grad):
    return (grad,)

def back_keep(v):
    return (v, None)

def back_low(kept, grad):
    return (low(grad),)
low.defvjp(low_keep, low_pass)
low_back.defvjp(back_keep, back_low)
epsilon = 1e-05
neg_large = -1e+30

def rotate(values, cosine, sine):
    half_width = values.shape[-1] // 2
    first_half = values[..., :half_width]
    second_half = values[..., half_width:]
    return jnp.concatenate([first_half * cosine - second_half * sine, second_half * cosine + first_half * sine], -1)

def angles(positions, head_dim):
    freqs = 10000.0 ** (-(jnp.arange(head_dim // 2, dtype=jnp.float32) * 2.0) / head_dim)
    phase = positions.astype(jnp.float32)[:, None] * freqs[None, :]
    return (jnp.cos(phase), jnp.sin(phase))

def layer(x_in, seq_segments, gain_one, w_query, w_keyval, w_out, gain_two, w_gateup, w_down):
    length = x_in.shape[0]
    highest = lax.Precision.HIGHEST
    inverse_one = lax.rsqrt(lax.optimization_barrier(jnp.mean(x_in * x_in, -1, keepdims=True)) + epsilon)
    normed_one = low(x_in * inverse_one * gain_one)
    queries = low_back(jnp.dot(normed_one, w_query, precision=highest)).reshape(length, HK, HQ // HK, HD)
    key_value = low_back(jnp.einsum('ld,dhe->lhe', normed_one, w_keyval, precision=highest))
    key_index = jnp.arange(length, dtype=jnp.int32)
    positions = key_index - seq_segments
    cosine, sine = angles(positions, HD)
    rot_q = low(rotate(queries, cosine[:, None, None, :], sine[:, None, None, :]))
    rot_k = low(rotate(key_value[..., :HD], cosine[:, None, :], sine[:, None, :]))
    values = low(key_value[..., HD:])
    block_len = min(512, length)
    blocks = length // block_len
    scale = 1.0 / math.sqrt(HD)

    @jax.checkpoint
    def one_block(items):
        block_q, block_index, block_seg = items
        raw = low_back(jnp.einsum('qkgd,pkd->kgqp', block_q, rot_k, precision=highest) * scale)
        allowed = (key_index[None, :] <= block_index[:, None]) & (seq_segments[None, :] == block_seg[:, None])
        probs = low(jax.nn.softmax(jnp.where(allowed, raw, neg_large), -1))
        return jnp.einsum('kgqp,pkd->qkgd', probs, values, precision=highest)
    attended = lax.map(one_block, (rot_q.reshape(blocks, block_len, HK, HQ // HK, HD), key_index.reshape(blocks, block_len), seq_segments.reshape(blocks, block_len)))
    attended = low(low_back(attended.reshape(length, HQ * HD)))
    branch = low_back(jnp.dot(attended, w_out, precision=highest))
    resid = x_in + branch
    inverse_two = lax.rsqrt(lax.optimization_barrier(jnp.mean(resid * resid, -1, keepdims=True)) + epsilon)
    normed_two = low(resid * inverse_two * gain_two)
    gate_up = low_back(jnp.einsum('ld,dcf->lcf', normed_two, w_gateup, precision=highest))
    hidden = low(jax.nn.silu(gate_up[:, 0]) * gate_up[:, 1])
    return resid + jnp.dot(hidden, w_down, precision=highest)

def reference(tokens, segments, gain_one, w_query, w_keyval, w_out, gain_two, w_gateup, w_down, cotangent):
    weights = (gain_one.astype(jnp.float32), w_query.astype(jnp.float32), w_keyval.astype(jnp.float32), w_out.astype(jnp.float32), gain_two.astype(jnp.float32), w_gateup.astype(jnp.float32), w_down.astype(jnp.float32))

    def per_sequence(totals, items):
        seq_tokens, seq_segments, seq_grad = items

        def forward(x_in, *params):
            return layer(x_in, seq_segments, *params)
        result, pull = jax.vjp(forward, seq_tokens.astype(jnp.float32), *weights)
        grads = pull(seq_grad.astype(jnp.float32))
        totals = jax.tree.map(jnp.add, totals, tuple(grads[1:]))
        return (totals, (result.astype(jnp.bfloat16), grads[0]))
    zeros = tuple((jnp.zeros_like(entry) for entry in weights))
    totals, (mixed, grad_tokens) = lax.scan(per_sequence, zeros, (tokens, segments, cotangent))
    return (mixed, grad_tokens, totals[0], totals[1], totals[2], totals[3], totals[4], totals[5], totals[6])
```

```python
import math

import jax
import jax.numpy as jnp
from jax import lax
from jax.experimental import pallas as pl
from jax.experimental.pallas import tpu as pltpu
from jax.sharding import PartitionSpec as P

HD = 64


epsilon = 1e-05
neg_large = -1e30


def rotate(values, cosine, sine):
    half_width = values.shape[-1] // 2
    first_half = values[..., :half_width]
    second_half = values[..., half_width:]
    return jnp.concatenate(
        [first_half * cosine - second_half * sine, second_half * cosine + first_half * sine], -1
    )


def angles(positions, head_dim):
    freqs = 10000.0 ** (-(jnp.arange(head_dim // 2, dtype=jnp.float32) * 2.0) / head_dim)
    phase = positions.astype(jnp.float32)[:, None] * freqs[None, :]
    return (jnp.cos(phase), jnp.sin(phase))


def norm_back(inputs, inverse, gain, grad_normed):
    grad_gain = jnp.sum(grad_normed * inputs * inverse, 0)
    scaled = grad_normed * gain
    grad_inputs = inverse * scaled - inputs * (inverse * inverse * inverse) * jnp.mean(
        scaled * inputs, -1, keepdims=True
    )
    return (grad_inputs, grad_gain)


MESH = pl.DeviceIdType.MESH
MIB = 1 << 20


def dot(left, right):
    return jnp.dot(left, right, preferred_element_type=jnp.float32)


def dot_t(left, right):
    return lax.dot_general(left, right, (((1,), (1,)), ((), ())), preferred_element_type=jnp.float32)


def lanes(shape):
    return lax.broadcasted_iota(jnp.int32, shape, len(shape) - 1)


def turn(values, cosine, sine):
    low_half = lax.rem(lanes(values.shape), 64) < 32
    swapped = jnp.where(low_half, pltpu.roll(values, 96, 1), pltpu.roll(values, 32, 1))
    return values * cosine + swapped * sine


def aligned(index, size):
    return pl.ds(pl.multiple_of(index * size, size), size)


def forward_kernel(
    x_hbm, seg_ref, cos_ref, sin_ref, gain_one_ref, gain_two_ref, wq_hbm, wkv_hbm, wout_hbm, raw_hbm,
    wdown_hbm, g_hbm,
    q_out, kv_out, att_out, lse_out, n1_out, n2_out, resid_out, hid_out, gg_out, wgu_out,
    x, n1, wq, wkv, wout, raw, wdown, g, wgu, q, kv, keys, vals_t, run_max, run_sum, acc, att_low,
    own, stage_core, got_core, stage_x, got_x, resid, n2, gh, hid, gg,
    load_sem, store_sem, kv_send, kv_recv, core_send, core_recv, x_send, x_recv, ag_send, ag_recv,
):
    rows, width = x.shape
    quarter = rows // 4
    units = gh.shape[1]
    tensor = lax.axis_index("tensor")
    place = lax.axis_index("context")
    core, chip = lax.rem(tensor, 2), lax.div(tensor, 2)
    core_mate = {"tensor": chip * 2 + 1 - core}
    chip_mate = {"tensor": (1 - chip) * 2 + core}

    barrier = pltpu.get_barrier_semaphore()
    for mate in (core_mate, chip_mate, *({"context": lax.rem(place + k, 4)} for k in (1, 2, 3))):
        pl.semaphore_signal(barrier, inc=1, device_id=mate, device_id_type=MESH)

    loads = [
        pltpu.make_async_copy(src, dst, load_sem.at[i])
        for i, (src, dst) in enumerate(
            [(x_hbm, x), (wkv_hbm, wkv), (wq_hbm, wq), (raw_hbm, raw), (wout_hbm, wout), (g_hbm, g),
             (wdown_hbm, wdown)]
        )
    ]
    for load in loads:
        load.start()
    load_x, load_wkv, load_wq, load_raw, load_wout, load_g, load_wdown = loads
    stores = []

    def store(src, dst):
        copy = pltpu.make_async_copy(src, dst, store_sem.at[len(stores)])
        copy.start()
        stores.append(copy)

    load_x.wait()

    @pl.loop(0, rows // 64)
    def _(i):
        at = aligned(i, 64)
        values = x[at, :].astype(jnp.float32)
        inverse = lax.rsqrt(jnp.mean(values * values, -1, keepdims=True) + epsilon)
        n1[at, :] = (values * inverse * gain_one_ref[...]).astype(jnp.bfloat16)

    store(n1, n1_out)

    load_wkv.wait()
    key_lane = lanes((rows, 128)) < 64
    kv[0] = turn(
        dot(n1[...], wkv[...]),
        jnp.where(key_lane, cos_ref[...], 1.0),
        jnp.where(key_lane, sin_ref[...], 0.0),
    ).astype(jnp.bfloat16)
    pl.semaphore_wait(barrier, 5)

    def kv_copy(k):
        return pltpu.make_async_remote_copy(
            src_ref=kv.at[0], dst_ref=kv.at[k], send_sem=kv_send.at[k], recv_sem=kv_recv.at[k],
            device_id={"context": lax.rem(place + k, 4)}, device_id_type=MESH,
        )

    for k in (1, 2, 3):
        pl.when(place + k < 4)(kv_copy(k).start)

    load_wq.wait()

    @pl.loop(0, q.shape[1] // 256)
    def _(i):
        wide = dot(n1[...], wq[:, aligned(i, 256)])
        for half in range(2):
            turned = turn(wide[:, 128 * half : 128 * half + 128], cos_ref[...], sin_ref[...])
            at = pl.ds(pl.multiple_of(i * 256 + 128 * half, 128), 128)
            q[:, at] = (turned * 0.125).astype(jnp.bfloat16)

    store(q, q_out)

    def attend_block(k, first):
        block = kv[k].astype(jnp.float32)
        keys[0] = jnp.where(key_lane, block, 0.0).astype(jnp.bfloat16)
        keys[1] = jnp.where(key_lane, 0.0, pltpu.roll(block, 64, 1)).astype(jnp.bfloat16)
        vals_t[...] = block.T[64:].astype(jnp.bfloat16)

        @pl.loop(0, q.shape[1] // 128)
        def _(pair):
            pair_q = q[:, aligned(pair, 128)]
            for e in range(2):
                head = pair * 2 + e
                scores = dot_t(keys[e], pair_q)
                key_index = (place - k) * rows + lax.broadcasted_iota(jnp.int32, (rows, rows), 0)
                allowed = key_index >= seg_ref[...]
                if first:
                    query_index = place * rows + lax.broadcasted_iota(jnp.int32, (rows, rows), 1)
                    allowed = allowed & (key_index <= query_index)
                scores = jnp.where(allowed, scores, neg_large)
                top = jnp.max(scores, 0, keepdims=True)
                at = aligned(head, 64)
                if first:
                    weights = jnp.exp(scores - top)
                    run_sum[head] = jnp.sum(weights, 0, keepdims=True)
                    acc[at, :] = dot(vals_t[...], weights.astype(jnp.bfloat16))
                else:
                    old = run_max[head]
                    top = jnp.maximum(top, old)
                    fade = jnp.exp(old - top)
                    weights = jnp.exp(scores - top)
                    run_sum[head] = run_sum[head] * fade + jnp.sum(weights, 0, keepdims=True)
                    acc[at, :] = acc[at, :] * fade + dot(
                        vals_t[...], weights.astype(jnp.bfloat16)
                    )
                run_max[head] = top

    attend_block(0, True)

    load_raw.wait()
    row = lax.broadcasted_iota(jnp.int32, (256, 256), 0)
    column = lax.broadcasted_iota(jnp.int32, (256, 256), 1)
    source = jnp.where(row < 128, 2 * row, 2 * row - 255)
    order = (column == source).astype(jnp.bfloat16)

    @pl.loop(0, width // 128)
    def _(i):
        at = aligned(i, 128)
        split = dot(order, raw[at].reshape(256, units)).astype(jnp.bfloat16)
        for b in range(units // 128):
            wgu[at, 256 * b : 256 * b + 128] = split[:128, 128 * b : 128 * b + 128]
            wgu[at, 256 * b + 128 : 256 * b + 256] = split[128:, 128 * b : 128 * b + 128]

    store(wgu, wgu_out)

    @pl.loop(1, place + 1)
    def _(k):
        kv_copy(k).wait_recv()
        attend_block(k, False)

    for k in (1, 2, 3):
        pl.when(place + k < 4)(kv_copy(k).wait_send)
    store(kv, kv_out)

    @pl.loop(0, q.shape[1] // 128)
    def _(pair):
        for e in range(2):
            head = pair * 2 + e
            at = aligned(head, 64)
            acc[at, :] = acc[at, :] * (1.0 / run_sum[head])
            run_max[head] = run_max[head] + jnp.log(run_sum[head])
        at = aligned(pair, 128)
        att_low[:, at] = acc[at, :].T.astype(jnp.bfloat16)

    store(acc, att_out)
    store(run_max, lse_out)

    load_wout.wait()
    chunks = own.shape[1]
    span = own.shape[3]

    def core_copy(i, c):
        return pltpu.make_async_remote_copy(
            src_ref=stage_core.at[i, c], dst_ref=got_core.at[i, c], send_sem=core_send.at[i, c],
            recv_sem=core_recv.at[i, c], device_id=core_mate, device_id_type=MESH,
        )

    def x_copy(c):
        return pltpu.make_async_remote_copy(
            src_ref=stage_x.at[c], dst_ref=got_x.at[c], send_sem=x_send.at[c],
            recv_sem=x_recv.at[c], device_id=chip_mate, device_id_type=MESH,
        )

    for i in range(2):
        half = 1 - chip if i == 0 else chip
        theirs = aligned(half * 2 + 1 - core, quarter)
        mine = aligned(half * 2 + core, quarter)
        for c in range(chunks):

            @pl.loop(0, span // 256)
            def _(tile):
                left = jnp.concatenate([att_low[theirs, :], att_low[mine, :]], 0)
                at = aligned(tile, 256)
                out_at = pl.ds(pl.multiple_of(c * span + tile * 256, 256), 256)
                both = dot(left, wout[:, out_at])
                stage_core[i, c, :, at] = both[:quarter].astype(jnp.bfloat16)
                own[i, c, :, at] = both[quarter:]

            core_copy(i, c).start()
        if i == 0:
            for c in range(chunks):
                core_copy(0, c).wait_recv()
                stage_x[c] = (own[0, c] + got_core[0, c].astype(jnp.float32)).astype(jnp.bfloat16)
                x_copy(c).start()

    load_g.wait()
    load_wdown.wait()

    @pl.loop(0, units // 128)
    def _(b):
        at = aligned(b, 128)
        gh[:, at] = dot_t(g[...], wdown[at, :])

    mine = aligned(tensor, quarter)
    square = jnp.zeros((quarter, 1), jnp.float32)
    for c in range(chunks):
        core_copy(1, c).wait_recv()
        x_copy(c).wait_recv()
        at = slice(c * span, (c + 1) * span)
        part = own[1, c] + got_core[1, c].astype(jnp.float32) + got_x[c].astype(jnp.float32)
        part = part + x[mine, at].astype(jnp.float32)
        resid[:, at] = part
        square = square + jnp.sum(part * part, -1, keepdims=True)
    inverse = lax.rsqrt(square / width + epsilon)
    n2[mine, :] = (resid[...] * inverse * gain_two_ref[...]).astype(jnp.bfloat16)
    store(resid, resid_out)

    def ag_copy(slot, owner, mate):
        at = aligned(owner, quarter)
        return pltpu.make_async_remote_copy(
            src_ref=n2.at[at, :], dst_ref=n2.at[at, :], send_sem=ag_send.at[slot],
            recv_sem=ag_recv.at[slot], device_id=mate, device_id_type=MESH,
        )

    to_chip = ag_copy(0, tensor, chip_mate)
    to_core = ag_copy(1, tensor, core_mate)
    onward = ag_copy(2, chip_mate["tensor"], core_mate)
    to_chip.start()
    to_core.start()

    def feed_forward(half):
        at = aligned(half, 2 * quarter)

        @pl.loop(0, units // 128)
        def _(b):
            wide = dot(n2[at, :], wgu[:, aligned(b, 256)])
            gate, up = wide[:, :128], wide[:, 128:]
            grad = gh[at, aligned(b, 128)]
            sigmoid = 1.0 / (1.0 + jnp.exp(-gate))
            active = gate * sigmoid
            hid[at, aligned(b, 128)] = (active * up).astype(jnp.bfloat16)
            grad_gate = grad * up * (sigmoid * (1.0 + gate * (1.0 - sigmoid)))
            both = jnp.concatenate([grad_gate, grad * active], 1).astype(jnp.bfloat16)
            gg[at, aligned(b, 256)] = both

    to_core.wait_recv()
    feed_forward(chip)
    to_chip.wait_recv()
    onward.start()
    onward.wait_recv()
    feed_forward(1 - chip)
    store(n2, n2_out)
    store(hid, hid_out)
    store(gg, gg_out)
    for copy in (to_chip, to_core, onward):
        copy.wait_send()
    for c in range(chunks):
        x_copy(c).wait_send()
        for i in range(2):
            core_copy(i, c).wait_send()
    for copy in stores:
        copy.wait()


def forward(x, segments, cosine, sine, gain_one, gain_two, w_query, w_keyval, w_out, w_gateup, w_down, g):
    rows, width = x.shape
    units = w_down.shape[0]
    heads = w_query.shape[1] // HD
    quarter = rows // 4
    chunks = 2
    bf16, f32 = jnp.bfloat16, jnp.float32
    anywhere = pl.BlockSpec(memory_space=pl.ANY)
    inside = pl.BlockSpec(memory_space=pltpu.VMEM)
    outs = [
        ((rows, heads * HD), bf16),
        ((4, rows, 2 * HD), bf16),
        ((heads * HD, rows), f32),
        ((heads, 1, rows), f32),
        ((rows, width), bf16),
        ((rows, width), bf16),
        ((quarter, width), f32),
        ((rows, units), bf16),
        ((rows, 2 * units), bf16),
        ((width, 2 * units), bf16),
    ]
    dma = pltpu.SemaphoreType.DMA
    return pl.pallas_call(
        forward_kernel,
        out_shape=[jax.ShapeDtypeStruct(*out) for out in outs],
        in_specs=[anywhere] + [inside] * 5 + [anywhere] * 6,
        out_specs=[anywhere] * len(outs),
        scratch_shapes=[
            pltpu.VMEM((rows, width), bf16),
            pltpu.VMEM((rows, width), bf16),
            pltpu.VMEM(w_query.shape, bf16),
            pltpu.VMEM(w_keyval.shape, bf16),
            pltpu.VMEM(w_out.shape, bf16),
            pltpu.VMEM(w_gateup.shape, bf16),
            pltpu.VMEM(w_down.shape, bf16),
            pltpu.VMEM((rows, width), bf16),
            pltpu.VMEM((width, 2 * units), bf16),
            pltpu.VMEM((rows, heads * HD), bf16),
            pltpu.VMEM((4, rows, 2 * HD), bf16),
            pltpu.VMEM((2, rows, 2 * HD), bf16),
            pltpu.VMEM((HD, rows), bf16),
            pltpu.VMEM((heads, 1, rows), f32),
            pltpu.VMEM((heads, 1, rows), f32),
            pltpu.VMEM((heads * HD, rows), f32),
            pltpu.VMEM((rows, heads * HD), bf16),
            pltpu.VMEM((2, chunks, quarter, width // chunks), f32),
            pltpu.VMEM((2, chunks, quarter, width // chunks), bf16),
            pltpu.VMEM((2, chunks, quarter, width // chunks), bf16),
            pltpu.VMEM((chunks, quarter, width // chunks), bf16),
            pltpu.VMEM((chunks, quarter, width // chunks), bf16),
            pltpu.VMEM((quarter, width), f32),
            pltpu.VMEM((rows, width), bf16),
            pltpu.VMEM((rows, units), f32),
            pltpu.VMEM((rows, units), bf16),
            pltpu.VMEM((rows, 2 * units), bf16),
            dma((7,)),
            dma((len(outs),)),
            dma((4,)),
            dma((4,)),
            dma((2, chunks)),
            dma((2, chunks)),
            dma((chunks,)),
            dma((chunks,)),
            dma((3,)),
            dma((3,)),
        ],
        compiler_params=pltpu.CompilerParams(
            collective_id=0, has_side_effects=True, vmem_limit_bytes=60 * MIB
        ),
        name="forward",
    )(x, segments, cosine, sine, gain_one, gain_two, w_query, w_keyval, w_out, w_gateup, w_down, g)


def core_swap(array):
    return lax.ppermute(array, "tensor", [(0, 1), (1, 0), (2, 3), (3, 2)])


def chip_swap(array):
    return lax.ppermute(array, "tensor", [(0, 2), (2, 0), (1, 3), (3, 1)])


def pick(array, index, axis):
    return lax.dynamic_index_in_dim(array, index, axis, keepdims=False)


def sum_scatter(part):
    core, chip = lax.axis_index("tensor") % 2, lax.axis_index("tensor") // 2
    rows, width = part.shape
    quarters = part.reshape(2, 2, rows // 4, width)
    got = core_swap(pick(quarters, 1 - core, 1).astype(jnp.bfloat16))
    pair = pick(quarters, core, 1) + got.astype(jnp.float32)
    got = chip_swap(pick(pair, 1 - chip, 0).astype(jnp.bfloat16))
    return pick(pair, chip, 0) + got.astype(jnp.float32)


def gather_rows(quarter):
    core, chip = lax.axis_index("tensor") % 2, lax.axis_index("tensor") // 2
    rows, width = quarter.shape
    other = chip_swap(quarter)
    pair = jnp.where(chip == 0, jnp.stack([quarter, other]), jnp.stack([other, quarter]))
    other = core_swap(pair)
    whole = jnp.where(core == 0, jnp.stack([pair, other], 1), jnp.stack([other, pair], 1))
    return whole.reshape(4 * rows, width)


def line_sum(part):
    place = lax.axis_index("context")
    order = jnp.array([[3, 2, 1, 0], [3, 2, 0, 1], [0, 1, 3, 2], [0, 1, 2, 3]], jnp.int32)[place]
    first, second, third, own = (part(order[i]) for i in range(4))

    def inward(array):
        return lax.ppermute(array.astype(jnp.bfloat16), "context", [(0, 1), (3, 2)])

    def across(array):
        return lax.ppermute(array.astype(jnp.bfloat16), "context", [(1, 2), (2, 1)])

    def outward(array):
        return lax.ppermute(array.astype(jnp.bfloat16), "context", [(1, 0), (2, 3)])

    in_one, in_two, in_three = inward(first), inward(second), inward(third)
    over_two = across(first + in_one.astype(jnp.float32))
    over_three = across(second + in_two.astype(jnp.float32))
    out_three = outward(third + over_two.astype(jnp.float32))
    return (
        own
        + in_three.astype(jnp.float32)
        + over_three.astype(jnp.float32)
        + out_three.astype(jnp.float32)
    )


def weight_grad(left, right, split_left):
    parts_dp = lax.axis_size("dp")
    index = lax.axis_index("dp")
    cut, kept = (left, right) if split_left else (right, left)
    if parts_dp == 2:
        halves = cut.reshape(cut.shape[0], 2, cut.shape[1] // 2)
        swap = [(0, 1), (1, 0)]
        cut_rows = jnp.concatenate(
            [pick(halves, index, 1), lax.ppermute(pick(halves, 1 - index, 1), "dp", swap)]
        )
        kept_rows = jnp.concatenate([kept, lax.ppermute(kept, "dp", swap)])
        step = cut_rows.shape[1] // 4

        def part(chunk):
            columns = lax.dynamic_slice_in_dim(cut_rows, chunk * step, step, 1)
            pair = (columns, kept_rows) if split_left else (kept_rows, columns)
            return jnp.einsum("ta,tb->ab", *pair, preferred_element_type=jnp.float32)

        return line_sum(part)
    whole = jnp.einsum("ta,tb->ab", left, right, preferred_element_type=jnp.float32)
    axis = 0 if split_left else 1
    mine = lax.psum_scatter(
        whole.astype(jnp.bfloat16), "dp", scatter_dimension=axis, tiled=True
    )
    step = mine.shape[axis] // 4
    return line_sum(
        lambda chunk: lax.dynamic_slice_in_dim(mine, chunk * step, step, axis).astype(jnp.float32)
    )


def gain_grad(partial):
    partial = partial + core_swap(partial)
    partial = partial + chip_swap(partial)
    return lax.psum_scatter(partial, ("dp", "context"), scatter_dimension=1, tiled=True)


def tables(positions):
    cosine, sine = angles(positions, HD)
    return jnp.concatenate([cosine] * 4, 1), jnp.concatenate([-sine, sine] * 2, 1)


def shards(
    tokens, segments, gain_one, w_query, w_keyval, w_out, gain_two, w_gateup, w_down, cotangent
):
    num_seqs, tok_count, model_width = tokens.shape
    head_dim = HD
    heads_kv = w_keyval.shape[1]
    heads = w_query.shape[1] // head_dim
    units = w_down.shape[0]
    place = lax.axis_index("context")
    tensor = lax.axis_index("tensor")
    quarter = tok_count // 4

    def own_rows(array):
        return lax.dynamic_slice_in_dim(array, tensor * quarter, quarter, 0)

    tokens_flat = tokens.reshape(tok_count, model_width)
    grad_out = cotangent.reshape(tok_count, model_width)
    query_index = place * tok_count + jnp.arange(tok_count, dtype=jnp.int32)
    cosine, sine = tables(query_index - segments[0])
    w_kv = w_keyval.reshape(model_width, 2 * head_dim)
    (
        rot_q, kv, attended_t, log_total, normed_one, normed_two, resid, hidden, grad_gateup, w_gu
    ) = forward(
        tokens_flat, segments, cosine, sine, gain_one[None], gain_two[None], w_query, w_kv, w_out,
        w_gateup, w_down, grad_out,
    )
    inverse_two = lax.rsqrt(jnp.mean(resid * resid, -1, keepdims=True) + epsilon)
    grad_normed_two = sum_scatter(
        jnp.einsum("rf,df->rd", grad_gateup, w_gu, preferred_element_type=jnp.float32)
    )
    grad_resid_norm, gain_two_part = norm_back(resid, inverse_two, gain_two, grad_normed_two)
    grad_resid = own_rows(grad_out).astype(jnp.float32) + grad_resid_norm
    grad_branch = gather_rows(grad_resid.astype(jnp.bfloat16))
    down_part = jnp.dot(hidden, w_down, preferred_element_type=jnp.float32)
    mixed = gather_rows((resid + sum_scatter(down_part)).astype(jnp.bfloat16))
    sent_wdown = weight_grad(hidden, grad_out, False)
    sent_gateup = weight_grad(normed_two, grad_gateup, True)
    attended = attended_t.T
    sent_wout = weight_grad(attended.astype(jnp.bfloat16), grad_branch, False)
    grad_attended = jnp.einsum(
        "rd,ad->ra", grad_branch, w_out, preferred_element_type=jnp.float32
    ).astype(jnp.bfloat16)
    delta = jnp.sum(
        (grad_attended.astype(jnp.float32) * attended).reshape(tok_count, heads, head_dim), -1
    ).T
    queries = rot_q.reshape(tok_count, heads, head_dim)
    grad_heads = grad_attended.reshape(tok_count, heads, head_dim)
    grad_rot_q = jnp.zeros((tok_count, heads, head_dim), jnp.float32)
    grad_blocks = []
    for back in range(4):
        keys, values = kv[back][:, :head_dim], kv[back][:, head_dim:]
        index = (place - back) * tok_count + jnp.arange(tok_count, dtype=jnp.int32)
        allowed = (index[None, :] <= query_index[:, None]) & (
            index[None, :] >= segments[0][:, None]
        )
        raw = jnp.einsum("qhd,pd->hqp", queries, keys, preferred_element_type=jnp.float32)
        probs = jnp.where(allowed, jnp.exp(jnp.where(allowed, raw, neg_large) - log_total.reshape(heads, tok_count, 1)), 0.0)
        grad_probs = jnp.einsum("qhd,pd->hqp", grad_heads, values, preferred_element_type=jnp.float32)
        grad_raw = (probs * (grad_probs - delta[..., None])).astype(jnp.bfloat16)
        grad_raw = jnp.where(allowed, grad_raw, 0)
        grad_rot_q = grad_rot_q + 0.125 * jnp.einsum("hqp,pd->qhd", grad_raw, keys, preferred_element_type=jnp.float32)
        grad_key = jnp.einsum("hqp,qhd->pd", grad_raw, queries, preferred_element_type=jnp.float32)
        grad_value = jnp.einsum("hqp,qhd->pd", probs.astype(jnp.bfloat16), grad_heads, preferred_element_type=jnp.float32)
        grad_blocks.append(jnp.concatenate([grad_key, grad_value], -1))
    grad_kv = grad_blocks[0]
    for back in range(1, 4):
        grad_kv = grad_kv + lax.ppermute(
            grad_blocks[back].astype(jnp.bfloat16),
            "context",
            [(i + back, i) for i in range(4 - back)],
        ).astype(jnp.float32)
    cos, sin = angles(query_index - segments[0], head_dim)
    grad_queries = (
        rotate(grad_rot_q, cos[:, None, :], -sin[:, None, :]).reshape(tok_count, -1).astype(jnp.bfloat16)
    )
    grad_keyval = jnp.concatenate(
        [rotate(grad_kv[..., :head_dim], cos, -sin), grad_kv[..., head_dim:]], -1
    ).astype(jnp.bfloat16)
    grad_normed_part = jnp.einsum(
        "re,de->rd", grad_queries, w_query, preferred_element_type=jnp.float32
    ) + jnp.einsum("re,de->rd", grad_keyval, w_kv, preferred_element_type=jnp.float32)
    sent_wqkv = weight_grad(
        normed_one, jnp.concatenate([grad_queries, grad_keyval], 1), True
    )
    grad_normed_one = sum_scatter(grad_normed_part)
    x_own = own_rows(tokens_flat).astype(jnp.float32)
    inverse_one = lax.rsqrt(jnp.mean(x_own * x_own, -1, keepdims=True) + epsilon)
    grad_x_norm, gain_one_part = norm_back(x_own, inverse_one, gain_one, grad_normed_one)
    grad_tokens = gather_rows((grad_resid + grad_x_norm).astype(jnp.bfloat16))
    gains = gain_grad(jnp.stack([gain_one_part, gain_two_part]))
    width_q = w_query.shape[1]
    return (
        mixed.reshape(num_seqs, tok_count, model_width),
        grad_tokens.astype(jnp.float32).reshape(num_seqs, tok_count, model_width),
        gains[0],
        sent_wqkv[:, :width_q],
        sent_wqkv[:, width_q:].reshape(-1, heads_kv, 2 * head_dim),
        sent_wout,
        gains[1],
        sent_gateup.reshape(-1, units // 128, 2, 128).transpose(0, 2, 1, 3).reshape(-1, 2, units),
        sent_wdown,
    )


def solution(mesh):
    return jax.shard_map(
        shards,
        mesh=mesh,
        in_specs=(
            P("dp", "context", None),
            P("dp", "context"),
            P(),
            P(None, "tensor"),
            P(None, "tensor", None),
            P("tensor", None),
            P(),
            P(None, None, "tensor"),
            P("tensor", None),
            P("dp", "context", None),
        ),
        out_specs=(
            P("dp", "context", None),
            P("dp", "context", None),
            P(("dp", "context")),
            P(("dp", "context"), "tensor"),
            P(("dp", "context"), "tensor", None),
            P("tensor", ("dp", "context")),
            P(("dp", "context")),
            P(("dp", "context"), None, "tensor"),
            P("tensor", ("dp", "context")),
        ),
        check_vma=False,
    )
```

```python
import functools
import types

import jax
import jax.numpy as jnp
from jax import lax
from jax.experimental import pallas as pl
from jax.experimental.pallas import tpu as pltpu
from jax.sharding import PartitionSpec as P

HD = 64


epsilon = 1e-05
neg_large = -1e30


def angles(positions, head_dim):
    freqs = 10000.0 ** (-(jnp.arange(head_dim // 2, dtype=jnp.float32) * 2.0) / head_dim)
    phase = positions.astype(jnp.float32)[:, None] * freqs[None, :]
    return (jnp.cos(phase), jnp.sin(phase))


MESH = pl.DeviceIdType.MESH
MIB = 1 << 20


def dot(left, right):
    return jnp.dot(left, right, preferred_element_type=jnp.float32)


def dot_t(left, right):
    return lax.dot_general(left, right, (((1,), (1,)), ((), ())), preferred_element_type=jnp.float32)


def lanes(shape):
    return lax.broadcasted_iota(jnp.int32, shape, len(shape) - 1)


def turn(values, cosine, sine):
    low_half = lax.rem(lanes(values.shape), 64) < 32
    swapped = jnp.where(low_half, pltpu.roll(values, 96, 1), pltpu.roll(values, 32, 1))
    return values * cosine + swapped * sine


def aligned(index, size):
    return pl.ds(pl.multiple_of(index * size, size), size)


def forward_kernel(
    swap,
    x_hbm, seg_ref, cos_ref, sin_ref, gain_one_ref, gain_two_ref, wq_hbm, wkv_hbm, wout_hbm, raw_hbm,
    wdown_hbm, g_hbm,
    q_out, kv_out, att_out, lse_out, n1_out, n2_out, resid_out, hid_out, gg_out, wgu_out, low_out,
    g_other, n1_other, low_other,
    x, n1, wq, wkv, wout, raw, wdown, g, wgu, q, kv, keys, vals_t, run_max, run_sum, acc, att_low,
    own, stage_core, got_core, stage_x, got_x, resid, n2, gh, hid, gg,
    load_sem, store_sem, kv_send, kv_recv, core_send, core_recv, x_send, x_recv, ag_send, ag_recv,
    dp_send, dp_recv,
):
    rows, width = x.shape
    quarter = rows // 4
    units = gh.shape[1]
    tensor = lax.axis_index("tensor")
    place = lax.axis_index("context")
    core, chip = lax.rem(tensor, 2), lax.div(tensor, 2)
    core_mate = {"tensor": chip * 2 + 1 - core}
    chip_mate = {"tensor": (1 - chip) * 2 + core}

    mates = [core_mate, chip_mate, *({"context": lax.rem(place + k, 4)} for k in (1, 2, 3))]
    if swap:
        side = lax.axis_index("dp")
        mates.append({"dp": 1 - side})
    barrier = pltpu.get_barrier_semaphore()
    for mate in mates:
        pl.semaphore_signal(barrier, inc=1, device_id=mate, device_id_type=MESH)

    loads = [
        pltpu.make_async_copy(src, dst, load_sem.at[i])
        for i, (src, dst) in enumerate(
            [(x_hbm, x), (wkv_hbm, wkv), (wq_hbm, wq), (raw_hbm, raw), (wout_hbm, wout), (g_hbm, g),
             (wdown_hbm, wdown)]
        )
    ]
    for load in loads:
        load.start()
    load_x, load_wkv, load_wq, load_raw, load_wout, load_g, load_wdown = loads
    stores = []

    def store(src, dst):
        copy = pltpu.make_async_copy(src, dst, store_sem.at[len(stores)])
        copy.start()
        stores.append(copy)

    load_x.wait()

    @pl.loop(0, rows // 64)
    def _(i):
        at = aligned(i, 64)
        values = x[at, :].astype(jnp.float32)
        inverse = lax.rsqrt(jnp.mean(values * values, -1, keepdims=True) + epsilon)
        n1[at, :] = (values * inverse * gain_one_ref[...]).astype(jnp.bfloat16)

    store(n1, n1_out)

    load_wkv.wait()
    key_lane = lanes((rows, 128)) < 64
    kv[0] = turn(
        dot(n1[...], wkv[...]),
        jnp.where(key_lane, cos_ref[...], 1.0),
        jnp.where(key_lane, sin_ref[...], 0.0),
    ).astype(jnp.bfloat16)
    pl.semaphore_wait(barrier, len(mates))
    swaps = []

    def swap_start(src, dst):
        if swap:
            i = len(swaps)
            copy = pltpu.make_async_remote_copy(
                src_ref=src, dst_ref=dst, send_sem=dp_send.at[i], recv_sem=dp_recv.at[i],
                device_id={"dp": 1 - side}, device_id_type=MESH,
            )
            copy.start()
            swaps.append(copy)

    if swap:
        theirs_cols = aligned(1 - side, width // 2)
        swap_start(g_hbm.at[:, theirs_cols], g_other)
        swap_start(n1.at[:, theirs_cols], n1_other)

    def kv_copy(k):
        return pltpu.make_async_remote_copy(
            src_ref=kv.at[0], dst_ref=kv.at[k], send_sem=kv_send.at[k], recv_sem=kv_recv.at[k],
            device_id={"context": lax.rem(place + k, 4)}, device_id_type=MESH,
        )

    for k in (1, 2, 3):
        pl.when(place + k < 4)(kv_copy(k).start)

    load_wq.wait()

    @pl.loop(0, q.shape[1] // 256)
    def _(i):
        wide = dot(n1[...], wq[:, aligned(i, 256)])
        for half in range(2):
            turned = turn(wide[:, 128 * half : 128 * half + 128], cos_ref[...], sin_ref[...])
            at = pl.ds(pl.multiple_of(i * 256 + 128 * half, 128), 128)
            q[:, at] = (turned * 0.125).astype(jnp.bfloat16)

    store(q, q_out)

    def attend_block(k, first):
        block = kv[k].astype(jnp.float32)
        keys[0] = jnp.where(key_lane, block, 0.0).astype(jnp.bfloat16)
        keys[1] = jnp.where(key_lane, 0.0, pltpu.roll(block, 64, 1)).astype(jnp.bfloat16)
        vals_t[...] = block.T[64:].astype(jnp.bfloat16)

        @pl.loop(0, q.shape[1] // 128)
        def _(pair):
            pair_q = q[:, aligned(pair, 128)]
            for e in range(2):
                head = pair * 2 + e
                scores = dot_t(keys[e], pair_q)
                key_index = (place - k) * rows + lax.broadcasted_iota(jnp.int32, (rows, rows), 0)
                allowed = key_index >= seg_ref[...]
                if first:
                    query_index = place * rows + lax.broadcasted_iota(jnp.int32, (rows, rows), 1)
                    allowed = allowed & (key_index <= query_index)
                scores = jnp.where(allowed, scores, neg_large)
                top = jnp.max(scores, 0, keepdims=True)
                at = aligned(head, 64)
                if first:
                    weights = jnp.exp(scores - top)
                    run_sum[head] = jnp.sum(weights, 0, keepdims=True)
                    acc[at, :] = dot(vals_t[...], weights.astype(jnp.bfloat16))
                else:
                    old = run_max[head]
                    top = jnp.maximum(top, old)
                    fade = jnp.exp(old - top)
                    weights = jnp.exp(scores - top)
                    run_sum[head] = run_sum[head] * fade + jnp.sum(weights, 0, keepdims=True)
                    acc[at, :] = acc[at, :] * fade + dot(
                        vals_t[...], weights.astype(jnp.bfloat16)
                    )
                run_max[head] = top

    attend_block(0, True)

    load_raw.wait()
    row = lax.broadcasted_iota(jnp.int32, (256, 256), 0)
    column = lax.broadcasted_iota(jnp.int32, (256, 256), 1)
    source = jnp.where(row < 128, 2 * row, 2 * row - 255)
    order = (column == source).astype(jnp.bfloat16)

    @pl.loop(0, width // 128)
    def _(i):
        at = aligned(i, 128)
        split = dot(order, raw[at].reshape(256, units)).astype(jnp.bfloat16)
        for b in range(units // 128):
            wgu[at, 256 * b : 256 * b + 128] = split[:128, 128 * b : 128 * b + 128]
            wgu[at, 256 * b + 128 : 256 * b + 256] = split[128:, 128 * b : 128 * b + 128]

    store(wgu, wgu_out)

    @pl.loop(1, place + 1)
    def _(k):
        kv_copy(k).wait_recv()
        attend_block(k, False)

    for k in (1, 2, 3):
        pl.when(place + k < 4)(kv_copy(k).wait_send)
    store(kv, kv_out)

    @pl.loop(0, q.shape[1] // 128)
    def _(pair):
        for e in range(2):
            head = pair * 2 + e
            at = aligned(head, 64)
            acc[at, :] = acc[at, :] * (1.0 / run_sum[head])
            run_max[head] = run_max[head] + jnp.log(run_sum[head])
        at = aligned(pair, 128)
        att_low[:, at] = acc[at, :].T.astype(jnp.bfloat16)

    store(acc, att_out)
    store(att_low, low_out)
    swap_start(att_low, low_other)
    store(run_max, lse_out)

    load_wout.wait()
    chunks = own.shape[1]
    span = own.shape[3]

    def core_copy(i, c):
        return pltpu.make_async_remote_copy(
            src_ref=stage_core.at[i, c], dst_ref=got_core.at[i, c], send_sem=core_send.at[i, c],
            recv_sem=core_recv.at[i, c], device_id=core_mate, device_id_type=MESH,
        )

    def x_copy(c):
        return pltpu.make_async_remote_copy(
            src_ref=stage_x.at[c], dst_ref=got_x.at[c], send_sem=x_send.at[c],
            recv_sem=x_recv.at[c], device_id=chip_mate, device_id_type=MESH,
        )

    for i in range(2):
        half = 1 - chip if i == 0 else chip
        theirs = aligned(half * 2 + 1 - core, quarter)
        mine = aligned(half * 2 + core, quarter)
        for c in range(chunks):

            @pl.loop(0, span // 256)
            def _(tile):
                left = jnp.concatenate([att_low[theirs, :], att_low[mine, :]], 0)
                at = aligned(tile, 256)
                out_at = pl.ds(pl.multiple_of(c * span + tile * 256, 256), 256)
                both = dot(left, wout[:, out_at])
                stage_core[i, c, :, at] = both[:quarter].astype(jnp.bfloat16)
                own[i, c, :, at] = both[quarter:]

            core_copy(i, c).start()
        if i == 0:
            for c in range(chunks):
                core_copy(0, c).wait_recv()
                stage_x[c] = (own[0, c] + got_core[0, c].astype(jnp.float32)).astype(jnp.bfloat16)
                x_copy(c).start()

    load_g.wait()
    load_wdown.wait()

    @pl.loop(0, units // 128)
    def _(b):
        at = aligned(b, 128)
        gh[:, at] = dot_t(g[...], wdown[at, :])

    mine = aligned(tensor, quarter)
    square = jnp.zeros((quarter, 1), jnp.float32)
    for c in range(chunks):
        core_copy(1, c).wait_recv()
        x_copy(c).wait_recv()
        at = slice(c * span, (c + 1) * span)
        part = own[1, c] + got_core[1, c].astype(jnp.float32) + got_x[c].astype(jnp.float32)
        part = part + x[mine, at].astype(jnp.float32)
        resid[:, at] = part
        square = square + jnp.sum(part * part, -1, keepdims=True)
    inverse = lax.rsqrt(square / width + epsilon)
    n2[mine, :] = (resid[...] * inverse * gain_two_ref[...]).astype(jnp.bfloat16)
    store(resid, resid_out)

    def ag_copy(slot, owner, mate):
        at = aligned(owner, quarter)
        return pltpu.make_async_remote_copy(
            src_ref=n2.at[at, :], dst_ref=n2.at[at, :], send_sem=ag_send.at[slot],
            recv_sem=ag_recv.at[slot], device_id=mate, device_id_type=MESH,
        )

    to_chip = ag_copy(0, tensor, chip_mate)
    to_core = ag_copy(1, tensor, core_mate)
    onward = ag_copy(2, chip_mate["tensor"], core_mate)
    to_chip.start()
    to_core.start()

    def feed_forward(half):
        at = aligned(half, 2 * quarter)

        @pl.loop(0, units // 128)
        def _(b):
            wide = dot(n2[at, :], wgu[:, aligned(b, 256)])
            gate, up = wide[:, :128], wide[:, 128:]
            grad = gh[at, aligned(b, 128)]
            sigmoid = 1.0 / (1.0 + jnp.exp(-gate))
            active = gate * sigmoid
            hid[at, aligned(b, 128)] = (active * up).astype(jnp.bfloat16)
            grad_gate = grad * up * (sigmoid * (1.0 + gate * (1.0 - sigmoid)))
            both = jnp.concatenate([grad_gate, grad * active], 1).astype(jnp.bfloat16)
            gg[at, aligned(b, 256)] = both

    to_core.wait_recv()
    feed_forward(chip)
    to_chip.wait_recv()
    onward.start()
    onward.wait_recv()
    feed_forward(1 - chip)
    store(n2, n2_out)
    store(hid, hid_out)
    store(gg, gg_out)
    for copy in (to_chip, to_core, onward):
        copy.wait_send()
    for c in range(chunks):
        x_copy(c).wait_send()
        for i in range(2):
            core_copy(i, c).wait_send()
    for copy in (*stores, *swaps):
        copy.wait()


def forward(swap, x, segments, cosine, sine, gain_one, gain_two, w_query, w_keyval, w_out, w_gateup, w_down, g):
    rows, width = x.shape
    units = w_down.shape[0]
    heads = w_query.shape[1] // HD
    quarter = rows // 4
    chunks = 2
    bf16, f32 = jnp.bfloat16, jnp.float32
    anywhere = pl.BlockSpec(memory_space=pl.ANY)
    inside = pl.BlockSpec(memory_space=pltpu.VMEM)
    outs = [
        ((rows, heads * HD), bf16),
        ((4, rows, 2 * HD), bf16),
        ((heads * HD, rows), f32),
        ((heads, 1, rows), f32),
        ((rows, width), bf16),
        ((rows, width), bf16),
        ((quarter, width), f32),
        ((rows, units), bf16),
        ((rows, 2 * units), bf16),
        ((width, 2 * units), bf16),
        ((rows, heads * HD), bf16),
        ((rows, width // 2), bf16),
        ((rows, width // 2), bf16),
        ((rows, heads * HD), bf16),
    ]
    dma = pltpu.SemaphoreType.DMA
    return pl.pallas_call(
        functools.partial(forward_kernel, swap),
        out_shape=[jax.ShapeDtypeStruct(*out) for out in outs],
        in_specs=[anywhere] + [inside] * 5 + [anywhere] * 6,
        out_specs=[anywhere] * len(outs),
        scratch_shapes=[
            pltpu.VMEM((rows, width), bf16),
            pltpu.VMEM((rows, width), bf16),
            pltpu.VMEM(w_query.shape, bf16),
            pltpu.VMEM(w_keyval.shape, bf16),
            pltpu.VMEM(w_out.shape, bf16),
            pltpu.VMEM(w_gateup.shape, bf16),
            pltpu.VMEM(w_down.shape, bf16),
            pltpu.VMEM((rows, width), bf16),
            pltpu.VMEM((width, 2 * units), bf16),
            pltpu.VMEM((rows, heads * HD), bf16),
            pltpu.VMEM((4, rows, 2 * HD), bf16),
            pltpu.VMEM((2, rows, 2 * HD), bf16),
            pltpu.VMEM((HD, rows), bf16),
            pltpu.VMEM((heads, 1, rows), f32),
            pltpu.VMEM((heads, 1, rows), f32),
            pltpu.VMEM((heads * HD, rows), f32),
            pltpu.VMEM((rows, heads * HD), bf16),
            pltpu.VMEM((2, chunks, quarter, width // chunks), f32),
            pltpu.VMEM((2, chunks, quarter, width // chunks), bf16),
            pltpu.VMEM((2, chunks, quarter, width // chunks), bf16),
            pltpu.VMEM((chunks, quarter, width // chunks), bf16),
            pltpu.VMEM((chunks, quarter, width // chunks), bf16),
            pltpu.VMEM((quarter, width), f32),
            pltpu.VMEM((rows, width), bf16),
            pltpu.VMEM((rows, units), f32),
            pltpu.VMEM((rows, units), bf16),
            pltpu.VMEM((rows, 2 * units), bf16),
            dma((7,)),
            dma((len(outs),)),
            dma((4,)),
            dma((4,)),
            dma((2, chunks)),
            dma((2, chunks)),
            dma((chunks,)),
            dma((chunks,)),
            dma((3,)),
            dma((3,)),
            dma((3,)),
            dma((3,)),
        ],
        compiler_params=pltpu.CompilerParams(
            collective_id=0, has_side_effects=True, vmem_limit_bytes=60 * MIB
        ),
        name="forward",
    )(x, segments, cosine, sine, gain_one, gain_two, w_query, w_keyval, w_out, w_gateup, w_down, g)


def backward_kernel(names, swap, *refs):
    r = types.SimpleNamespace(**dict(zip(names, refs, strict=True)))
    rows, width = r.gb.shape
    quarter = rows // 4
    units = r.hid.shape[1]
    heads_width = r.q.shape[1]
    f32, bf16 = jnp.float32, jnp.bfloat16
    tensor = lax.axis_index("tensor")
    place = lax.axis_index("context")
    core, chip = lax.rem(tensor, 2), lax.div(tensor, 2)
    core_mate = {"tensor": chip * 2 + 1 - core}
    chip_mate = {"tensor": (1 - chip) * 2 + core}
    mates = [core_mate, chip_mate, *({"context": lax.rem(place + k, 4)} for k in (1, 2, 3))]
    if swap:
        side = lax.axis_index("dp")
        dp_mate = {"dp": 1 - side}
        mates.append(dp_mate)

    barrier = pltpu.get_barrier_semaphore()
    for mate in mates:
        pl.semaphore_signal(barrier, inc=1, device_id=mate, device_id_type=MESH)

    def remote(src, dst, send, recv, mate):
        return pltpu.make_async_remote_copy(
            src_ref=src, dst_ref=dst, send_sem=send, recv_sem=recv, device_id=mate,
            device_id_type=MESH,
        )

    def tile_gu(n):
        slot = lax.rem(n, 3)
        return pltpu.make_async_copy(
            r.wgu_hbm.at[aligned(n, 256)], r.w_rows.at[slot], r.w_rows_sem.at[slot]
        )

    def tile_down(n):
        slot = lax.rem(n, 3)
        return pltpu.make_async_copy(
            r.wdown_hbm.at[:, aligned(n, 256)], r.w_cols.at[slot], r.w_cols_sem.at[slot]
        )

    def tile_qkv(n):
        slot = lax.rem(n, 3)
        at = aligned(n, 256)
        copies = (
            pltpu.make_async_copy(
                r.wq_hbm.at[at], r.w_rows.at[slot, :, 0:heads_width], r.w_rows_sem.at[slot]
            ),
            pltpu.make_async_copy(
                r.wkv_hbm.at[at],
                r.w_rows.at[slot, :, heads_width : heads_width + 128],
                r.w_cols_sem.at[slot],
            ),
        )
        return types.SimpleNamespace(
            start=lambda: [copy.start() for copy in copies],
            wait=lambda: [copy.wait() for copy in copies],
        )

    mine = aligned(tensor, quarter)
    loads = {}
    for name, src, dst in (
        ("gg", r.gg_hbm, r.gg),
        ("hid", r.hid_hbm, r.hid),
        ("resid", r.resid_hbm, r.resid),
        ("g_own", r.g_hbm.at[mine, :], r.g_own),
        ("x_own", r.x_hbm.at[mine, :], r.x_own),
        ("wout", r.wout_hbm, r.wout),
        ("q", r.q_hbm, r.q),
        ("kv", r.kv_hbm, r.kv),
        ("att", r.att_hbm, r.att),
    ):
        loads[name] = pltpu.make_async_copy(src, dst, r.load_sem.at[len(loads)])
    loads["gg"].start()
    for n in range(3):
        tile_gu(n).start()
    loads["hid"].start()
    for n in range(3):
        tile_down(n).start()
    for name in ("resid", "g_own", "x_own", "wout", "q", "kv", "att"):
        loads[name].start()

    pl.semaphore_wait(barrier, len(mates))

    if swap:
        half = width // 2
        theirs_cols = aligned(1 - side, half)
        mine_cols = aligned(side, half)
        lead = r.stage.shape[3]

        def swap_copy(i, src, dst):
            return remote(src, dst, r.dp_send.at[i], r.dp_recv.at[i], dp_mate)

        swap_hid = swap_copy(0, r.hid_hbm, r.hid_o)
        swap_n2 = swap_copy(1, r.n2_hbm.at[:, theirs_cols], r.n2_o)
        swap_gg = [
            swap_copy(2 + i, r.gg_hbm.at[:, i * lead : (i + 1) * lead], r.gg_o.at[i])
            for i in range(2)
        ]
        swap_gb = swap_copy(4, r.gb.at[:, theirs_cols], r.gb_o)
        swap_gqkv = swap_copy(5, r.gqkv, r.gqkv_o)
        for copy in (swap_hid, swap_n2, *swap_gg):
            copy.start()

    chunks = r.own_fin.shape[1]
    span = r.own_fin.shape[3]

    def core_copy(b, c):
        return remote(
            r.stage_core.at[b, c], r.got_core.at[b, c], r.core_send.at[b, c],
            r.core_recv.at[b, c], core_mate,
        )

    def x_copy(b, c):
        return remote(
            r.stage_x.at[b, c], r.got_x.at[b, c], r.x_send.at[b, c], r.x_recv.at[b, c], chip_mate
        )

    def start_sum(b, tile, product, send):
        routes = (
            ((1 - chip) * 2 + 1 - core, lambda c, at, v: put(r.stage_core, (b, c, 0), at, v)),
            (chip * 2 + 1 - core, lambda c, at, v: put(r.stage_core, (b, c, 1), at, v)),
            ((1 - chip) * 2 + core, lambda c, at, v: put(r.own_fwd, (c,), at, v)),
            (chip * 2 + core, lambda c, at, v: put(r.own_fin, (b, c), at, v)),
        )

        def put(ref, index, at, value):
            ref[(*index, slice(None), at)] = value.astype(ref.dtype)

        def forward_chunk(c):
            core_copy(b, c).wait_recv()
            r.stage_x[b, c] = (r.own_fwd[c] + r.got_core[b, c, 0].astype(f32)).astype(bf16)
            if send:
                x_copy(b, c).start()

        @pl.loop(0, chunks)
        def _(c):
            for t in range(span // 256):
                n = c * (span // 256) + t
                tile(n).wait()
                r.tmp[...] = product(lax.rem(n, 3))
                for owner, route in routes:
                    route(c, slice(t * 256, t * 256 + 256), r.tmp[aligned(owner, quarter), :])

                @pl.when(n + 3 < width // 256)
                def _():
                    tile(n + 3).start()

            core_copy(b, c).start()
            pl.when(c > 0)(lambda: forward_chunk(c - 1))

        forward_chunk(chunks - 1)

    def finish_sum(b):
        for c in range(chunks):
            x_copy(b, c).wait_recv()
            r.own_fin[b, c] = (
                r.own_fin[b, c] + r.got_core[b, c, 1].astype(f32) + r.got_x[b, c].astype(f32)
            )
        for c in range(chunks):
            core_copy(b, c).wait_send()
            x_copy(b, c).wait_send()

    def back_through_norm(b, values, gain_ref, gain_row, emit):
        square = jnp.zeros((quarter, 1), f32)
        inner = jnp.zeros((quarter, 1), f32)
        for c in range(chunks):
            at = slice(c * span, (c + 1) * span)
            v = values[:, at].astype(f32)
            square = square + jnp.sum(v * v, -1, keepdims=True)
            inner = inner + jnp.sum(r.own_fin[b, c] * gain_ref[:, at] * v, -1, keepdims=True)
        inverse = lax.rsqrt(square / width + epsilon)
        slope = inner / width * (inverse * inverse * inverse)
        for c in range(chunks):
            at = slice(c * span, (c + 1) * span)
            v = values[:, at].astype(f32)
            dn = r.own_fin[b, c]
            r.gain_sum[0, gain_row : gain_row + 1, at] = jnp.sum(dn * v * inverse, 0, keepdims=True)
            emit(at, inverse * dn * gain_ref[:, at] - v * slope)

    def gather(i, src, dst):
        def copy(slot, src, owner, mate):
            return remote(
                src, dst.at[aligned(owner, quarter), :], r.ag_send.at[i, slot],
                r.ag_recv.at[i, slot], mate,
            )

        other = chip_mate["tensor"]
        return (
            copy(0, src, tensor, chip_mate),
            copy(1, src, tensor, core_mate),
            copy(2, dst.at[aligned(other, quarter), :], other, core_mate),
        )

    if swap:
        is_end = (place == 0) | (place == 3)
        is_mid = jnp.logical_not(is_end)
        beside = place + 1 - 2 * lax.rem(place, 2)
        low_side = place < 2
        io_mate, across_mate = {"context": beside}, {"context": 3 - place}
        plan = (
            (r.g_hbm.at[:, mine_cols], r.go_hbm, r.hid, r.hid_o, units, r.dwdown_out),
            (r.n2_hbm.at[:, mine_cols], r.n2_o, r.gg.at[:, 0:lead], r.gg_o.at[0], lead,
             r.dgu_out.at[:, 0:lead]),
            (None, None, r.gg.at[:, lead : 2 * lead], r.gg_o.at[1], lead,
             r.dgu_out.at[:, lead : 2 * lead]),
            (r.gb.at[:, mine_cols], r.gb_o, r.att_low, r.att_o, heads_width, r.dwout_out),
            (r.n1_hbm.at[:, mine_cols], r.n1o_hbm, r.gqkv, r.gqkv_o, r.gqkv.shape[1],
             r.dwqkv_out),
        )

        def cut_loads(u):
            own, other = plan[u][:2]
            return (
                pltpu.make_async_copy(own, r.cut.at[0:rows], r.cut_sem.at[0]),
                pltpu.make_async_copy(other, r.cut.at[rows : 2 * rows], r.cut_sem.at[1]),
            )

        def piece(ref, s, j, u):
            return ref.at[s, j, :, 0 : plan[u][4]]

        def line_copy(u, j, slot, mate):
            s = u % 2
            return remote(
                piece(r.stage, s, j, u), piece(r.got, s, slot, u), r.line_send.at[s, j],
                r.line_recv.at[s, slot], mate,
            )

        def result(u):
            return pltpu.make_async_copy(
                r.sums.at[u % 2, :, 0 : plan[u][4]], plan[u][5], r.sums_sem.at[u % 2]
            )

        def prepare(u, load_next):
            s = u % 2
            own, other, width_u = plan[u][2], plan[u][3], plan[u][4]
            if u >= 2:
                for j in range(3):
                    line_copy(u - 2, j, 0, io_mate).wait_send()
                result(u - 2).wait()
                pl.when(is_end)(lambda: pl.semaphore_wait(r.io_credit, 1))
            if plan[u][0] is not None:
                for copy in cut_loads(u):
                    copy.wait()

            @pl.loop(0, 4)
            def _(j):
                chunk = jnp.where(
                    j == 0,
                    jnp.where(low_side, 3, 0),
                    jnp.where(
                        j == 1, jnp.where(low_side, 2, 1), jnp.where(j == 2, beside, place)
                    ),
                )
                r.turned[...] = r.cut[:, aligned(chunk, 256)].astype(f32).T.astype(bf16)

                def block(at):
                    term = dot(r.turned[:, 0:rows], own[:, at]) + dot(
                        r.turned[:, rows : 2 * rows], other[:, at]
                    )

                    @pl.when(j < 3)
                    def _():
                        r.stage[s, j, :, at] = term.astype(bf16)

                    @pl.when(j == 3)
                    def _():
                        r.sums[s, :, at] = term

                @pl.loop(0, width_u // 256)
                def _(tile):
                    block(aligned(tile, 256))

                if width_u % 256:
                    block(slice(width_u - width_u % 256, width_u))

                @pl.when((j < 3) & is_end)
                def _():
                    line_copy(u, j, j, io_mate).start()

            if load_next is not None:
                for copy in cut_loads(load_next):
                    copy.start()

        def add_in(u, j, slot):
            width_u, s = plan[u][4], u % 2
            line_copy(u, 0, slot, io_mate).wait_recv()

            @pl.loop(0, 4)
            def _(i):
                at = aligned(i, 64)
                total = r.stage[s, j, at, 0:width_u].astype(f32)
                total = total + r.got[s, slot, at, 0:width_u].astype(f32)
                r.stage[s, j, at, 0:width_u] = total.astype(bf16)

        def pass_on(u, step):
            @pl.when(is_mid)
            def _():
                if step < 2:
                    add_in(u, step, step)
                    if u >= 2 and step == 0:
                        pl.semaphore_wait(r.across_credit, 1)
                    line_copy(u, step, 3 + step, across_mate).start()
                else:
                    add_in(u, 2, 3)
                    if u >= 2:
                        pl.semaphore_wait(r.io_credit, 1)
                    line_copy(u, 2, 0, io_mate).start()

        def complete(u):
            width_u, s = plan[u][4], u % 2

            def take(slots):
                for slot in slots:
                    line_copy(u, 0, slot, io_mate).wait_recv()

                @pl.loop(0, 4)
                def _(i):
                    at = aligned(i, 64)
                    total = r.sums[s, at, 0:width_u]
                    for slot in slots:
                        total = total + r.got[s, slot, at, 0:width_u].astype(f32)
                    r.sums[s, at, 0:width_u] = total

            @pl.when(is_end)
            def _():
                take((0,))

            @pl.when(is_mid)
            def _():
                take((2, 4))

            result(u).start()
            if u + 2 < len(plan):
                pl.semaphore_signal(r.io_credit, inc=1, device_id=io_mate, device_id_type=MESH)

                @pl.when(is_mid)
                def _():
                    pl.semaphore_signal(
                        r.across_credit, inc=1, device_id=across_mate, device_id_type=MESH
                    )

        late = (
            pltpu.make_async_copy(r.attlow_hbm, r.att_low, r.late_sem.at[0]),
            pltpu.make_async_copy(r.atto_hbm, r.att_o, r.late_sem.at[1]),
        )
        for copy in (*cut_loads(0), *late):
            copy.start()

    r.gain_sum[...] = jnp.zeros_like(r.gain_sum)

    loads["gg"].wait()
    start_sum(0, tile_gu, lambda slot: dot_t(r.gg[...], r.w_rows[slot]), True)
    loads["hid"].wait()
    start_sum(1, tile_down, lambda slot: dot(r.hid[...], r.w_cols[slot]), False)
    for n in range(3):
        tile_qkv(n).start()
    finish_sum(0)
    loads["resid"].wait()
    loads["g_own"].wait()

    def keep_resid(at, grad):
        total = r.g_own[:, at].astype(f32) + grad
        r.grad_resid[:, at] = total
        r.gb[mine, at] = total.astype(bf16)

    back_through_norm(0, r.resid, r.gain_two, 1, keep_resid)
    gb_chip, gb_core, gb_onward = gather(0, r.gb.at[mine, :], r.gb)
    gb_chip.start()
    gb_core.start()
    for c in range(chunks):
        x_copy(1, c).start()
    gb_chip.wait_recv()
    gb_onward.start()
    if swap:
        swap_hid.wait_recv()
        prepare(0, None)
        swap_n2.wait_recv()
        for copy in cut_loads(1):
            copy.start()
    gb_core.wait_recv()
    gb_onward.wait_recv()
    if swap:
        swap_gb.start()
    else:
        pltpu.make_async_copy(r.gb, r.gb_out, r.cut_sem.at[0]).start()

    loads["wout"].wait()
    for i in range(heads_width // 256):
        at = slice(i * 256, i * 256 + 256)
        r.ga[:, at] = dot_t(r.gb[...], r.wout[at, :]).astype(bf16)
    loads["att"].wait()

    @pl.loop(0, heads_width // 128)
    def _(pair):
        at = aligned(pair, 128)
        product = r.ga[:, at].astype(f32).T * r.att[at, :]
        for e in range(2):
            r.delta[pair * 2 + e] = jnp.sum(product[64 * e : 64 * e + 64], 0, keepdims=True)

    loads["q"].wait()
    loads["kv"].wait()
    r.dq[...] = jnp.zeros_like(r.dq)
    key_lane = lanes((rows, 128)) < 64

    def back_block(k, first):
        block = r.kv[k].astype(f32)
        rolled = pltpu.roll(block, 64, 1)
        r.keys[0] = jnp.where(key_lane, block, 0.0).astype(bf16)
        r.keys[1] = jnp.where(key_lane, 0.0, rolled).astype(bf16)
        r.vals[0] = jnp.where(key_lane, rolled, 0.0).astype(bf16)
        r.vals[1] = jnp.where(key_lane, 0.0, block).astype(bf16)
        r.keys_t[...] = block.T[:64].astype(bf16)
        r.dk[...] = jnp.zeros_like(r.dk)
        r.dv[...] = jnp.zeros_like(r.dv)

        @pl.loop(0, heads_width // 128)
        def _(pair):
            pair_q = r.q[:, aligned(pair, 128)]
            pair_ga = r.ga[:, aligned(pair, 128)]
            for e in range(2):
                head = pair * 2 + e
                scores = dot_t(r.keys[e], pair_q)
                key_index = (place - k) * rows + lax.broadcasted_iota(jnp.int32, (rows, rows), 0)
                allowed = key_index >= r.seg[...]
                if first:
                    query_index = place * rows + lax.broadcasted_iota(jnp.int32, (rows, rows), 1)
                    allowed = allowed & (key_index <= query_index)
                probs = jnp.where(allowed, jnp.exp(scores - r.lse[head]), 0.0)
                grad_probs = dot_t(r.vals[e], pair_ga)
                grad_scores = (probs * (grad_probs - r.delta[head])).astype(bf16)
                r.dv[e] += dot(probs.astype(bf16), pair_ga)
                r.dk[e] += dot(grad_scores, pair_q)
                r.dq[aligned(head, 64), :] += dot(r.keys_t[...], grad_scores)

        return jnp.where(
            key_lane,
            r.dk[0] + pltpu.roll(r.dk[1], 64, 1),
            r.dv[1] + pltpu.roll(r.dv[0], 64, 1),
        )

    def dkv_copy(k, mate):
        return remote(
            r.stage_kv.at[k], r.got_kv.at[k], r.kv_send.at[k], r.kv_recv.at[k], {"context": mate}
        )

    @pl.loop(0, place)
    def _(i):
        k = place - i
        r.stage_kv[k] = back_block(k, False).astype(bf16)
        dkv_copy(k, i).start()

    r.dkv[...] = back_block(0, True)
    if swap:
        pass_on(0, 0)

    @pl.loop(0, heads_width // 128)
    def _(pair):
        at = aligned(pair, 128)
        turned = turn(r.dq[at, :].T * 0.125, r.cos[...], -r.sin[...])
        r.gqkv[:, at] = turned.astype(bf16)

    for k in (1, 2, 3):

        @pl.when(place + k < 4)
        def _():
            dkv_copy(k, 0).wait_recv()
            r.dkv[...] += r.got_kv[k].astype(f32)

    r.gqkv[:, heads_width : heads_width + 128] = turn(
        r.dkv[...], jnp.where(key_lane, r.cos[...], 1.0), jnp.where(key_lane, -r.sin[...], 0.0)
    ).astype(bf16)
    if swap:
        swap_gqkv.start()
    else:
        pltpu.make_async_copy(r.gqkv, r.gqkv_out, r.cut_sem.at[1]).start()

    start_sum(
        0, tile_qkv,
        lambda slot: dot_t(r.gqkv[...], r.w_rows[slot, :, 0 : r.gqkv.shape[1]]), True,
    )

    finish_sum(1)
    for c in range(chunks):
        at = slice(c * span, (c + 1) * span)
        r.mixed_own[:, at] = (r.resid[:, at] + r.own_fin[1, c]).astype(bf16)
    mixed_chip, mixed_core, mixed_onward = gather(1, r.mixed_own, r.mixed_out)
    mixed_store = pltpu.make_async_copy(r.mixed_own, r.mixed_out.at[mine, :], r.out_sem.at[0])
    for copy in (mixed_chip, mixed_core, mixed_store):
        copy.start()
    if swap:
        pass_on(0, 1)
        pass_on(0, 2)

    finish_sum(0)
    loads["x_own"].wait()

    def keep_tokens(at, grad):
        r.tokens_own[:, at] = (r.grad_resid[:, at] + grad).astype(bf16)

    back_through_norm(0, r.x_own, r.gain_one, 0, keep_tokens)
    tokens_chip, tokens_core, tokens_onward = gather(2, r.tokens_own, r.tokens_out)
    tokens_store = pltpu.make_async_copy(r.tokens_own, r.tokens_out.at[mine, :], r.out_sem.at[1])
    for copy in (tokens_chip, tokens_core, tokens_store):
        copy.start()

    for i, mate in enumerate((core_mate, chip_mate)):
        copy = remote(
            r.gain_sum.at[i], r.gain_got.at[i], r.gain_send.at[i], r.gain_recv.at[i], mate
        )
        copy.start()
        copy.wait()
        r.gain_sum[i + 1] = r.gain_sum[i] + r.gain_got[i]
    if swap:
        copy = remote(
            r.gain_sum.at[2, :, theirs_cols], r.gain_half.at[0], r.gain_send.at[2],
            r.gain_recv.at[2], dp_mate,
        )
        copy.start()
        copy.wait()
        r.gain_half[1] = r.gain_sum[2, :, mine_cols] + r.gain_half[0]
        part = half // 4
        pieces = [
            remote(
                r.gain_half.at[1, :, aligned(lax.rem(place + k, 4), part)], r.gain_piece.at[k],
                r.gain_send.at[2 + k], r.gain_recv.at[2 + k], {"context": lax.rem(place + k, 4)},
            )
            for k in (1, 2, 3)
        ]
        for copy in pieces:
            copy.start()
        for copy in pieces:
            copy.wait()
        r.gains_out[...] = (
            r.gain_half[1, :, aligned(place, part)]
            + r.gain_piece[1]
            + r.gain_piece[2]
            + r.gain_piece[3]
        )
    else:
        r.gains_out[...] = r.gain_sum[2]

    if swap:
        complete(0)
        swap_gg[0].wait_recv()
        prepare(1, None)
    mixed_chip.wait_recv()
    mixed_onward.start()
    tokens_chip.wait_recv()
    tokens_onward.start()
    if swap:
        pass_on(1, 0)
        swap_gg[1].wait_recv()
        swap_gb.wait_recv()
        prepare(2, 3)
        pass_on(1, 1)
        pass_on(1, 2)
        complete(1)
        for copy in late:
            copy.wait()
        prepare(3, 4)
        pass_on(2, 0)
        pass_on(2, 1)
        pass_on(2, 2)
        complete(2)
        swap_gqkv.wait_recv()
        prepare(4, None)
        for u in (3, 4):
            for step in range(3):
                pass_on(u, step)
            complete(u)

    for copy in (mixed_core, mixed_onward, tokens_core, tokens_onward):
        copy.wait_recv()
    for copy in (
        gb_chip, gb_core, gb_onward, mixed_chip, mixed_core, mixed_onward, tokens_chip,
        tokens_core, tokens_onward,
    ):
        copy.wait_send()
    mixed_store.wait()
    tokens_store.wait()
    for k in (1, 2, 3):
        pl.when(place >= k)(dkv_copy(k, 0).wait_send)
    if swap:
        for copy in (swap_hid, swap_n2, *swap_gg, swap_gb, swap_gqkv):
            copy.wait_send()
        for u in (3, 4):
            for j in range(3):
                line_copy(u, j, 0, io_mate).wait_send()
            result(u).wait()
    else:
        pltpu.make_async_copy(r.gb, r.gb_out, r.cut_sem.at[0]).wait()
        pltpu.make_async_copy(r.gqkv, r.gqkv_out, r.cut_sem.at[1]).wait()


def backward(swap, inputs, rows, width, units, heads):
    bf16, f32 = jnp.bfloat16, jnp.float32
    quarter = rows // 4
    chunks = 4
    span = width // chunks
    wide = heads * HD
    qkv = wide + 2 * HD
    outs = {
        "mixed_out": ((rows, width), bf16),
        "tokens_out": ((rows, width), bf16),
        "gains_out": ((8, width // 8 if swap else width), f32),
    }
    if swap:
        outs |= {
            "dwdown_out": ((width // 8, units), f32),
            "dgu_out": ((width // 8, 2 * units), f32),
            "dwout_out": ((width // 8, wide), f32),
            "dwqkv_out": ((width // 8, qkv), f32),
            "n2_o": ((rows, width // 2), bf16),
            "gb_o": ((rows, width // 2), bf16),
        }
    else:
        outs |= {"gb_out": ((rows, width), bf16), "gqkv_out": ((rows, qkv), bf16)}
    scratch = {
        "gg": ((rows, 2 * units), bf16),
        "hid": ((rows, units), bf16),
        "resid": ((quarter, width), f32),
        "g_own": ((quarter, width), bf16),
        "x_own": ((quarter, width), bf16),
        "wout": ((wide, width), bf16),
        "q": ((rows, wide), bf16),
        "kv": ((4, rows, 2 * HD), bf16),
        "att": ((wide, rows), f32),
        "w_rows": ((3, 256, 2 * units), bf16),
        "w_cols": ((3, units, 256), bf16),
        "tmp": ((rows, 256), f32),
        "stage_core": ((2, chunks, 2, quarter, span), bf16),
        "got_core": ((2, chunks, 2, quarter, span), bf16),
        "own_fwd": ((chunks, quarter, span), f32),
        "own_fin": ((2, chunks, quarter, span), f32),
        "stage_x": ((2, chunks, quarter, span), bf16),
        "got_x": ((2, chunks, quarter, span), bf16),
        "grad_resid": ((quarter, width), f32),
        "gb": ((rows, width), bf16),
        "ga": ((rows, wide), bf16),
        "mixed_own": ((quarter, width), bf16),
        "tokens_own": ((quarter, width), bf16),
        "delta": ((heads, 1, rows), f32),
        "dq": ((wide, rows), f32),
        "keys": ((2, rows, 2 * HD), bf16),
        "vals": ((2, rows, 2 * HD), bf16),
        "keys_t": ((HD, rows), bf16),
        "dk": ((2, rows, 2 * HD), f32),
        "dv": ((2, rows, 2 * HD), f32),
        "dkv": ((rows, 2 * HD), f32),
        "stage_kv": ((4, rows, 2 * HD), bf16),
        "got_kv": ((4, rows, 2 * HD), bf16),
        "gqkv": ((rows, qkv), bf16),
        "gain_sum": ((3, 8, width), f32),
        "gain_got": ((2, 8, width), f32),
    }
    if swap:
        scratch |= {
            "hid_o": ((rows, units), bf16),
            "gg_o": ((2, rows, units), bf16),
            "gqkv_o": ((rows, qkv), bf16),
            "att_low": ((rows, wide), bf16),
            "att_o": ((rows, wide), bf16),
            "cut": ((2 * rows, width // 2), bf16),
            "turned": ((256, 2 * rows), bf16),
            "stage": ((2, 3, width // 8, units), bf16),
            "got": ((2, 5, width // 8, units), bf16),
            "sums": ((2, width // 8, units), f32),
            "gain_half": ((2, 8, width // 2), f32),
            "gain_piece": ((4, 8, width // 8), f32),
        }
    sems = {
        "load_sem": (9,),
        "w_rows_sem": (3,),
        "w_cols_sem": (3,),
        "core_send": (2, chunks),
        "core_recv": (2, chunks),
        "x_send": (2, chunks),
        "x_recv": (2, chunks),
        "ag_send": (3, 3),
        "ag_recv": (3, 3),
        "kv_send": (4,),
        "kv_recv": (4,),
        "gain_send": (6,),
        "gain_recv": (6,),
        "out_sem": (2,),
        "cut_sem": (2,),
    }
    if swap:
        sems |= {
            "dp_send": (6,),
            "dp_recv": (6,),
            "line_send": (2, 3),
            "line_recv": (2, 5),
            "sums_sem": (2,),
            "late_sem": (2,),
        }
    credits = ["io_credit", "across_credit"] if swap else []
    names = [*inputs, *outs, *scratch, *sems, *credits]
    anywhere = pl.BlockSpec(memory_space=pl.ANY)
    inside = pl.BlockSpec(memory_space=pltpu.VMEM)
    results = pl.pallas_call(
        functools.partial(backward_kernel, names, swap),
        out_shape=[jax.ShapeDtypeStruct(*out) for out in outs.values()],
        in_specs=[anywhere if name.endswith("_hbm") else inside for name in inputs],
        out_specs=[inside if name == "gains_out" else anywhere for name in outs],
        scratch_shapes=[
            *(pltpu.VMEM(*shape) for shape in scratch.values()),
            *(pltpu.SemaphoreType.DMA(shape) for shape in sems.values()),
            *(pltpu.SemaphoreType.REGULAR for _ in credits),
        ],
        compiler_params=pltpu.CompilerParams(
            collective_id=1, has_side_effects=True, vmem_limit_bytes=63 * MIB
        ),
        name="backward",
    )(*inputs.values())
    return dict(zip(outs, results, strict=True))


def pick(array, index, axis):
    return lax.dynamic_index_in_dim(array, index, axis, keepdims=False)


def line_sum(part):
    place = lax.axis_index("context")
    order = jnp.array([[3, 2, 1, 0], [3, 2, 0, 1], [0, 1, 3, 2], [0, 1, 2, 3]], jnp.int32)[place]
    first, second, third, own = (part(order[i]) for i in range(4))

    def inward(array):
        return lax.ppermute(array.astype(jnp.bfloat16), "context", [(0, 1), (3, 2)])

    def across(array):
        return lax.ppermute(array.astype(jnp.bfloat16), "context", [(1, 2), (2, 1)])

    def outward(array):
        return lax.ppermute(array.astype(jnp.bfloat16), "context", [(1, 0), (2, 3)])

    in_one, in_two, in_three = inward(first), inward(second), inward(third)
    over_two = across(first + in_one.astype(jnp.float32))
    over_three = across(second + in_two.astype(jnp.float32))
    out_three = outward(third + over_two.astype(jnp.float32))
    return (
        own
        + in_three.astype(jnp.float32)
        + over_three.astype(jnp.float32)
        + out_three.astype(jnp.float32)
    )


def weight_grad(left, right, axis):
    whole = lax.dot_general(
        left, right, (((0,), (0,)), ((), ())), preferred_element_type=jnp.float32
    )
    mine = lax.psum_scatter(
        whole.astype(jnp.bfloat16), "dp", scatter_dimension=axis, tiled=True
    )
    step = mine.shape[axis] // 4
    return line_sum(
        lambda chunk: lax.dynamic_slice_in_dim(mine, chunk * step, step, axis).astype(jnp.float32)
    )


def tables(positions):
    cosine, sine = angles(positions, HD)
    return jnp.concatenate([cosine] * 4, 1), jnp.concatenate([-sine, sine] * 2, 1)


def shards(
    tokens, segments, gain_one, w_query, w_keyval, w_out, gain_two, w_gateup, w_down, cotangent
):
    num_seqs, tok_count, model_width = tokens.shape
    heads_kv = w_keyval.shape[1]
    width_q = w_query.shape[1]
    units = w_down.shape[0]
    swap = lax.axis_size("dp") == 2
    x = tokens.reshape(tok_count, model_width)
    g = cotangent.reshape(tok_count, model_width)
    query_index = lax.axis_index("context") * tok_count + jnp.arange(tok_count, dtype=jnp.int32)
    cosine, sine = tables(query_index - segments[0])
    w_kv = w_keyval.reshape(model_width, 2 * HD)
    one, two = gain_one[None], gain_two[None]
    (
        queries, kv, attended, log_total, normed_one, normed_two, resid, hidden, grad_gateup, w_gu,
        attended_low, g_other, normed_one_other, attended_other,
    ) = forward(
        swap, x, segments, cosine, sine, one, two, w_query, w_kv, w_out, w_gateup, w_down, g
    )
    inputs = {
        "seg": segments, "cos": cosine, "sin": sine, "gain_one": one, "gain_two": two,
        "lse": log_total, "q_hbm": queries, "kv_hbm": kv, "att_hbm": attended,
        "resid_hbm": resid, "hid_hbm": hidden, "gg_hbm": grad_gateup, "wgu_hbm": w_gu,
        "wdown_hbm": w_down, "wout_hbm": w_out, "wq_hbm": w_query, "wkv_hbm": w_kv, "x_hbm": x,
        "g_hbm": g,
    }
    if swap:
        inputs |= {
            "n1_hbm": normed_one, "n2_hbm": normed_two, "attlow_hbm": attended_low,
            "go_hbm": g_other, "n1o_hbm": normed_one_other, "atto_hbm": attended_other,
        }
    out = backward(swap, inputs, tok_count, model_width, units, width_q // HD)
    if swap:
        gains = out["gains_out"]
        sent_wdown, sent_wout = out["dwdown_out"].T, out["dwout_out"].T
        sent_gateup, sent_wqkv = out["dgu_out"], out["dwqkv_out"]
    else:
        gains = lax.psum_scatter(
            out["gains_out"], ("dp", "context"), scatter_dimension=1, tiled=True
        )
        sent_wdown = weight_grad(hidden, g, 1)
        sent_gateup = weight_grad(normed_two, grad_gateup, 0)
        sent_wout = weight_grad(attended_low, out["gb_out"], 1)
        sent_wqkv = weight_grad(normed_one, out["gqkv_out"], 0)
    return (
        out["mixed_out"].reshape(tokens.shape),
        out["tokens_out"].astype(jnp.float32).reshape(tokens.shape),
        gains[0],
        sent_wqkv[:, :width_q],
        sent_wqkv[:, width_q:].reshape(-1, heads_kv, 2 * HD),
        sent_wout,
        gains[1],
        sent_gateup.reshape(-1, units // 128, 2, 128).transpose(0, 2, 1, 3).reshape(-1, 2, units),
        sent_wdown,
    )


def solution(mesh):
    return jax.shard_map(
        shards,
        mesh=mesh,
        in_specs=(
            P("dp", "context", None),
            P("dp", "context"),
            P(),
            P(None, "tensor"),
            P(None, "tensor", None),
            P("tensor", None),
            P(),
            P(None, None, "tensor"),
            P("tensor", None),
            P("dp", "context", None),
        ),
        out_specs=(
            P("dp", "context", None),
            P("dp", "context", None),
            P(("dp", "context")),
            P(("dp", "context"), "tensor"),
            P(("dp", "context"), "tensor", None),
            P("tensor", ("dp", "context")),
            P(("dp", "context")),
            P(("dp", "context"), None, "tensor"),
            P("tensor", ("dp", "context")),
        ),
        check_vma=False,
    )
```

```python
import functools
import types

import jax
import jax.numpy as jnp
from jax import lax
from jax.experimental import pallas as pl
from jax.experimental.pallas import tpu as pltpu
from jax.sharding import PartitionSpec as P

HD = 64


epsilon = 1e-05
neg_large = -1e30


def angles(positions, head_dim):
    freqs = 10000.0 ** (-(jnp.arange(head_dim // 2, dtype=jnp.float32) * 2.0) / head_dim)
    phase = positions.astype(jnp.float32)[:, None] * freqs[None, :]
    return (jnp.cos(phase), jnp.sin(phase))


MESH = pl.DeviceIdType.MESH
MIB = 1 << 20


def dot(left, right):
    return jnp.dot(left, right, preferred_element_type=jnp.float32)


def dot_t(left, right):
    return lax.dot_general(left, right, (((1,), (1,)), ((), ())), preferred_element_type=jnp.float32)


def lanes(shape):
    return lax.broadcasted_iota(jnp.int32, shape, len(shape) - 1)


def turn(values, cosine, sine):
    low_half = lax.rem(lanes(values.shape), 64) < 32
    swapped = jnp.where(low_half, pltpu.roll(values, 96, 1), pltpu.roll(values, 32, 1))
    return values * cosine + swapped * sine


def aligned(index, size):
    return pl.ds(pl.multiple_of(index * size, size), size)


def forward_kernel(
    swap,
    x_hbm, seg_ref, cos_ref, sin_ref, gain_one_ref, gain_two_ref, wq_hbm, wkv_hbm, wout_hbm, raw_hbm,
    wdown_hbm, g_hbm,
    q_out, kv_out, att_out, lse_out, n1_out, n2_out, resid_out, hid_out, gg_out, wgu_out, low_out,
    g_other, low_other,
    x, n1, wq, wkv, wout, raw, wdown, g, wgu, q, kv, keys, vals_t, run_max, run_sum, acc, att_low,
    own, stage_core, got_core, stage_x, got_x, resid, n2, gh, hid, gg,
    load_sem, store_sem, kv_send, kv_recv, core_send, core_recv, x_send, x_recv, ag_send, ag_recv,
    dp_send, dp_recv,
):
    rows, width = x.shape
    quarter = rows // 4
    units = gh.shape[1]
    tensor = lax.axis_index("tensor")
    place = lax.axis_index("context")
    core, chip = lax.rem(tensor, 2), lax.div(tensor, 2)
    core_mate = {"tensor": chip * 2 + 1 - core}
    chip_mate = {"tensor": (1 - chip) * 2 + core}

    mates = [core_mate, chip_mate, *({"context": lax.rem(place + k, 4)} for k in (1, 2, 3))]
    if swap:
        side = lax.axis_index("dp")
        mates.append({"dp": 1 - side})
    barrier = pltpu.get_barrier_semaphore()
    for mate in mates:
        pl.semaphore_signal(barrier, inc=1, device_id=mate, device_id_type=MESH)

    loads = [
        pltpu.make_async_copy(src, dst, load_sem.at[i])
        for i, (src, dst) in enumerate(
            [(x_hbm, x), (wkv_hbm, wkv), (wq_hbm, wq), (raw_hbm, raw), (wout_hbm, wout), (g_hbm, g),
             (wdown_hbm, wdown)]
        )
    ]
    for load in loads:
        load.start()
    load_x, load_wkv, load_wq, load_raw, load_wout, load_g, load_wdown = loads
    stores = []

    def store(src, dst):
        copy = pltpu.make_async_copy(src, dst, store_sem.at[len(stores)])
        copy.start()
        stores.append(copy)

    load_x.wait()

    @pl.loop(0, rows // 64)
    def _(i):
        at = aligned(i, 64)
        values = x[at, :].astype(jnp.float32)
        inverse = lax.rsqrt(jnp.mean(values * values, -1, keepdims=True) + epsilon)
        n1[at, :] = (values * inverse * gain_one_ref[...]).astype(jnp.bfloat16)

    store(n1, n1_out)

    load_wkv.wait()
    key_lane = lanes((rows, 128)) < 64
    kv[0] = turn(
        dot(n1[...], wkv[...]),
        jnp.where(key_lane, cos_ref[...], 1.0),
        jnp.where(key_lane, sin_ref[...], 0.0),
    ).astype(jnp.bfloat16)
    pl.semaphore_wait(barrier, len(mates))
    swaps = []

    def swap_start(src, dst):
        if swap:
            i = len(swaps)
            copy = pltpu.make_async_remote_copy(
                src_ref=src, dst_ref=dst, send_sem=dp_send.at[i], recv_sem=dp_recv.at[i],
                device_id={"dp": 1 - side}, device_id_type=MESH,
            )
            copy.start()
            swaps.append(copy)

    if swap:
        theirs_cols = aligned(1 - side, width // 2)
        swap_start(g_hbm.at[:, theirs_cols], g_other)

    def kv_copy(k):
        return pltpu.make_async_remote_copy(
            src_ref=kv.at[0], dst_ref=kv.at[k], send_sem=kv_send.at[k], recv_sem=kv_recv.at[k],
            device_id={"context": lax.rem(place + k, 4)}, device_id_type=MESH,
        )

    for k in (1, 2, 3):
        pl.when(place + k < 4)(kv_copy(k).start)

    load_wq.wait()

    @pl.loop(0, q.shape[1] // 256)
    def _(i):
        wide = dot(n1[...], wq[:, aligned(i, 256)])
        for half in range(2):
            turned = turn(wide[:, 128 * half : 128 * half + 128], cos_ref[...], sin_ref[...])
            at = pl.ds(pl.multiple_of(i * 256 + 128 * half, 128), 128)
            q[:, at] = (turned * 0.125).astype(jnp.bfloat16)

    store(q, q_out)

    def attend_block(k, first):
        block = kv[k].astype(jnp.float32)
        keys[0] = jnp.where(key_lane, block, 0.0).astype(jnp.bfloat16)
        keys[1] = jnp.where(key_lane, 0.0, pltpu.roll(block, 64, 1)).astype(jnp.bfloat16)
        vals_t[...] = block.T[64:].astype(jnp.bfloat16)

        @pl.loop(0, q.shape[1] // 128)
        def _(pair):
            pair_q = q[:, aligned(pair, 128)]
            for e in range(2):
                head = pair * 2 + e
                scores = dot_t(keys[e], pair_q)
                key_index = (place - k) * rows + lax.broadcasted_iota(jnp.int32, (rows, rows), 0)
                allowed = key_index >= seg_ref[...]
                if first:
                    query_index = place * rows + lax.broadcasted_iota(jnp.int32, (rows, rows), 1)
                    allowed = allowed & (key_index <= query_index)
                scores = jnp.where(allowed, scores, neg_large)
                top = jnp.max(scores, 0, keepdims=True)
                at = aligned(head, 64)
                if first:
                    weights = jnp.exp(scores - top)
                    run_sum[head] = jnp.sum(weights, 0, keepdims=True)
                    acc[at, :] = dot(vals_t[...], weights.astype(jnp.bfloat16))
                else:
                    old = run_max[head]
                    top = jnp.maximum(top, old)
                    fade = jnp.exp(old - top)
                    weights = jnp.exp(scores - top)
                    run_sum[head] = run_sum[head] * fade + jnp.sum(weights, 0, keepdims=True)
                    acc[at, :] = acc[at, :] * fade + dot(
                        vals_t[...], weights.astype(jnp.bfloat16)
                    )
                run_max[head] = top

    attend_block(0, True)

    load_raw.wait()
    row = lax.broadcasted_iota(jnp.int32, (256, 256), 0)
    column = lax.broadcasted_iota(jnp.int32, (256, 256), 1)
    source = jnp.where(row < 128, 2 * row, 2 * row - 255)
    order = (column == source).astype(jnp.bfloat16)

    @pl.loop(0, width // 128)
    def _(i):
        at = aligned(i, 128)
        split = dot(order, raw[at].reshape(256, units)).astype(jnp.bfloat16)
        for b in range(units // 128):
            wgu[at, 256 * b : 256 * b + 128] = split[:128, 128 * b : 128 * b + 128]
            wgu[at, 256 * b + 128 : 256 * b + 256] = split[128:, 128 * b : 128 * b + 128]

    store(wgu, wgu_out)

    @pl.loop(1, place + 1)
    def _(k):
        kv_copy(k).wait_recv()
        attend_block(k, False)

    for k in (1, 2, 3):
        pl.when(place + k < 4)(kv_copy(k).wait_send)
    store(kv, kv_out)

    @pl.loop(0, q.shape[1] // 128)
    def _(pair):
        for e in range(2):
            head = pair * 2 + e
            at = aligned(head, 64)
            acc[at, :] = acc[at, :] * (1.0 / run_sum[head])
            run_max[head] = run_max[head] + jnp.log(run_sum[head])
        at = aligned(pair, 128)
        att_low[:, at] = acc[at, :].T.astype(jnp.bfloat16)

    store(acc, att_out)
    store(att_low, low_out)
    swap_start(att_low, low_other)
    store(run_max, lse_out)

    load_wout.wait()
    chunks = own.shape[1]
    span = own.shape[3]

    def core_copy(i, c):
        return pltpu.make_async_remote_copy(
            src_ref=stage_core.at[i, c], dst_ref=got_core.at[i, c], send_sem=core_send.at[i, c],
            recv_sem=core_recv.at[i, c], device_id=core_mate, device_id_type=MESH,
        )

    def x_copy(c):
        return pltpu.make_async_remote_copy(
            src_ref=stage_x.at[c], dst_ref=got_x.at[c], send_sem=x_send.at[c],
            recv_sem=x_recv.at[c], device_id=chip_mate, device_id_type=MESH,
        )

    for i in range(2):
        half = 1 - chip if i == 0 else chip
        theirs = aligned(half * 2 + 1 - core, quarter)
        mine = aligned(half * 2 + core, quarter)
        for c in range(chunks):

            @pl.loop(0, span // 256)
            def _(tile):
                left = jnp.concatenate([att_low[theirs, :], att_low[mine, :]], 0)
                at = aligned(tile, 256)
                out_at = pl.ds(pl.multiple_of(c * span + tile * 256, 256), 256)
                both = dot(left, wout[:, out_at])
                stage_core[i, c, :, at] = both[:quarter].astype(jnp.bfloat16)
                own[i, c, :, at] = both[quarter:]

            core_copy(i, c).start()
        if i == 0:
            for c in range(chunks):
                core_copy(0, c).wait_recv()
                stage_x[c] = (own[0, c] + got_core[0, c].astype(jnp.float32)).astype(jnp.bfloat16)
                x_copy(c).start()

    load_g.wait()
    load_wdown.wait()

    @pl.loop(0, units // 128)
    def _(b):
        at = aligned(b, 128)
        gh[:, at] = dot_t(g[...], wdown[at, :])

    mine = aligned(tensor, quarter)
    square = jnp.zeros((quarter, 1), jnp.float32)
    for c in range(chunks):
        core_copy(1, c).wait_recv()
        x_copy(c).wait_recv()
        at = slice(c * span, (c + 1) * span)
        part = own[1, c] + got_core[1, c].astype(jnp.float32) + got_x[c].astype(jnp.float32)
        part = part + x[mine, at].astype(jnp.float32)
        resid[:, at] = part
        square = square + jnp.sum(part * part, -1, keepdims=True)
    inverse = lax.rsqrt(square / width + epsilon)
    n2[mine, :] = (resid[...] * inverse * gain_two_ref[...]).astype(jnp.bfloat16)
    store(resid, resid_out)

    def ag_copy(slot, owner, mate):
        at = aligned(owner, quarter)
        return pltpu.make_async_remote_copy(
            src_ref=n2.at[at, :], dst_ref=n2.at[at, :], send_sem=ag_send.at[slot],
            recv_sem=ag_recv.at[slot], device_id=mate, device_id_type=MESH,
        )

    to_chip = ag_copy(0, tensor, chip_mate)
    to_core = ag_copy(1, tensor, core_mate)
    onward = ag_copy(2, chip_mate["tensor"], core_mate)
    to_chip.start()
    to_core.start()

    def feed_forward(half):
        at = aligned(half, 2 * quarter)

        @pl.loop(0, units // 128)
        def _(b):
            wide = dot(n2[at, :], wgu[:, aligned(b, 256)])
            gate, up = wide[:, :128], wide[:, 128:]
            grad = gh[at, aligned(b, 128)]
            sigmoid = 1.0 / (1.0 + jnp.exp(-gate))
            active = gate * sigmoid
            hid[at, aligned(b, 128)] = (active * up).astype(jnp.bfloat16)
            grad_gate = grad * up * (sigmoid * (1.0 + gate * (1.0 - sigmoid)))
            both = jnp.concatenate([grad_gate, grad * active], 1).astype(jnp.bfloat16)
            gg[at, aligned(b, 256)] = both

    to_core.wait_recv()
    feed_forward(chip)
    to_chip.wait_recv()
    onward.start()
    onward.wait_recv()
    feed_forward(1 - chip)
    store(n2, n2_out)
    store(hid, hid_out)
    store(gg, gg_out)
    for copy in (to_chip, to_core, onward):
        copy.wait_send()
    for c in range(chunks):
        x_copy(c).wait_send()
        for i in range(2):
            core_copy(i, c).wait_send()
    for copy in (*stores, *swaps):
        copy.wait()


def forward(swap, x, segments, cosine, sine, gain_one, gain_two, w_query, w_keyval, w_out, w_gateup, w_down, g):
    rows, width = x.shape
    units = w_down.shape[0]
    heads = w_query.shape[1] // HD
    quarter = rows // 4
    chunks = 2
    bf16, f32 = jnp.bfloat16, jnp.float32
    anywhere = pl.BlockSpec(memory_space=pl.ANY)
    inside = pl.BlockSpec(memory_space=pltpu.VMEM)
    outs = [
        ((rows, heads * HD), bf16),
        ((4, rows, 2 * HD), bf16),
        ((heads * HD, rows), f32),
        ((heads, 1, rows), f32),
        ((rows, width), bf16),
        ((rows, width), bf16),
        ((quarter, width), f32),
        ((rows, units), bf16),
        ((rows, 2 * units), bf16),
        ((width, 2 * units), bf16),
        ((rows, heads * HD), bf16),
        ((rows, width // 2), bf16),
        ((rows, heads * HD), bf16),
    ]
    dma = pltpu.SemaphoreType.DMA
    return pl.pallas_call(
        functools.partial(forward_kernel, swap),
        out_shape=[jax.ShapeDtypeStruct(*out) for out in outs],
        in_specs=[anywhere] + [inside] * 5 + [anywhere] * 6,
        out_specs=[anywhere] * len(outs),
        scratch_shapes=[
            pltpu.VMEM((rows, width), bf16),
            pltpu.VMEM((rows, width), bf16),
            pltpu.VMEM(w_query.shape, bf16),
            pltpu.VMEM(w_keyval.shape, bf16),
            pltpu.VMEM(w_out.shape, bf16),
            pltpu.VMEM(w_gateup.shape, bf16),
            pltpu.VMEM(w_down.shape, bf16),
            pltpu.VMEM((rows, width), bf16),
            pltpu.VMEM((width, 2 * units), bf16),
            pltpu.VMEM((rows, heads * HD), bf16),
            pltpu.VMEM((4, rows, 2 * HD), bf16),
            pltpu.VMEM((2, rows, 2 * HD), bf16),
            pltpu.VMEM((HD, rows), bf16),
            pltpu.VMEM((heads, 1, rows), f32),
            pltpu.VMEM((heads, 1, rows), f32),
            pltpu.VMEM((heads * HD, rows), f32),
            pltpu.VMEM((rows, heads * HD), bf16),
            pltpu.VMEM((2, chunks, quarter, width // chunks), f32),
            pltpu.VMEM((2, chunks, quarter, width // chunks), bf16),
            pltpu.VMEM((2, chunks, quarter, width // chunks), bf16),
            pltpu.VMEM((chunks, quarter, width // chunks), bf16),
            pltpu.VMEM((chunks, quarter, width // chunks), bf16),
            pltpu.VMEM((quarter, width), f32),
            pltpu.VMEM((rows, width), bf16),
            pltpu.VMEM((rows, units), f32),
            pltpu.VMEM((rows, units), bf16),
            pltpu.VMEM((rows, 2 * units), bf16),
            dma((7,)),
            dma((len(outs),)),
            dma((4,)),
            dma((4,)),
            dma((2, chunks)),
            dma((2, chunks)),
            dma((chunks,)),
            dma((chunks,)),
            dma((3,)),
            dma((3,)),
            dma((2,)),
            dma((2,)),
        ],
        compiler_params=pltpu.CompilerParams(
            collective_id=0, has_side_effects=True, vmem_limit_bytes=60 * MIB
        ),
        name="forward",
    )(x, segments, cosine, sine, gain_one, gain_two, w_query, w_keyval, w_out, w_gateup, w_down, g)


def backward_kernel(names, swap, *refs):
    r = types.SimpleNamespace(**dict(zip(names, refs, strict=True)))
    rows, width = r.gb.shape
    quarter = rows // 4
    units = r.hid.shape[1]
    heads_width = r.q.shape[1]
    f32, bf16 = jnp.float32, jnp.bfloat16
    tensor = lax.axis_index("tensor")
    place = lax.axis_index("context")
    core, chip = lax.rem(tensor, 2), lax.div(tensor, 2)
    core_mate = {"tensor": chip * 2 + 1 - core}
    chip_mate = {"tensor": (1 - chip) * 2 + core}
    mates = [core_mate, chip_mate, *({"context": lax.rem(place + k, 4)} for k in (1, 2, 3))]
    if swap:
        side = lax.axis_index("dp")
        dp_mate = {"dp": 1 - side}
        mates.append(dp_mate)

    barrier = pltpu.get_barrier_semaphore()
    for mate in mates:
        pl.semaphore_signal(barrier, inc=1, device_id=mate, device_id_type=MESH)

    def remote(src, dst, send, recv, mate):
        return pltpu.make_async_remote_copy(
            src_ref=src, dst_ref=dst, send_sem=send, recv_sem=recv, device_id=mate,
            device_id_type=MESH,
        )

    def tile_gu(n):
        slot = lax.rem(n, 3)
        return pltpu.make_async_copy(
            r.wgu_hbm.at[aligned(n, 256)], r.w_rows.at[slot], r.w_rows_sem.at[slot]
        )

    def tile_down(n):
        slot = lax.rem(n, 3)
        return pltpu.make_async_copy(
            r.wdown_hbm.at[:, aligned(n, 256)], r.w_cols.at[slot], r.w_cols_sem.at[slot]
        )

    def tile_qkv(n):
        slot = lax.rem(n, 3)
        at = aligned(n, 256)
        copies = (
            pltpu.make_async_copy(
                r.wq_hbm.at[at], r.w_rows.at[slot, :, 0:heads_width], r.w_rows_sem.at[slot]
            ),
            pltpu.make_async_copy(
                r.wkv_hbm.at[at],
                r.w_rows.at[slot, :, heads_width : heads_width + 128],
                r.w_kv_sem.at[slot],
            ),
        )
        return types.SimpleNamespace(
            start=lambda: [copy.start() for copy in copies],
            wait=lambda: [copy.wait() for copy in copies],
        )

    mine = aligned(tensor, quarter)
    loads = {}
    for name, src, dst in (
        ("gg", r.gg_hbm, r.gg),
        ("hid", r.hid_hbm, r.hid),
        ("resid", r.resid_hbm, r.resid),
        ("g_own", r.g_hbm.at[mine, :], r.g_own),
        ("x_own", r.x_hbm.at[mine, :], r.x_own),
        ("wout", r.wout_hbm, r.wout),
        ("q", r.q_hbm, r.q),
        ("kv", r.kv_hbm, r.kv),
        ("att", r.att_hbm, r.att),
    ):
        loads[name] = pltpu.make_async_copy(src, dst, r.load_sem.at[len(loads)])
    loads["gg"].start()
    for n in range(3):
        tile_gu(n).start()
    loads["hid"].start()
    for n in range(3):
        tile_down(n).start()
    for name in ("resid", "g_own", "x_own", "wout", "q", "kv", "att"):
        loads[name].start()

    pl.semaphore_wait(barrier, len(mates))

    if swap:
        half = width // 2
        theirs_cols = aligned(1 - side, half)
        mine_cols = aligned(side, half)
        lead = r.stage.shape[3]

        def cuts(total):
            return [(at, min(lead, total - at)) for at in range(0, total, lead)]

        swaps = []

        def swap_copy(src, dst):
            i = len(swaps)
            swaps.append(remote(src, dst, r.dp_send.at[i], r.dp_recv.at[i], dp_mate))
            return swaps[i]

        hid_cuts, gg_cuts = cuts(units), cuts(2 * units)
        swap_hid = [
            swap_copy(r.hid_hbm.at[:, at : at + size], r.hid_o.at[i, :, 0:size])
            for i, (at, size) in enumerate(hid_cuts)
        ]
        swap_n2 = swap_copy(r.n2_hbm.at[mine, theirs_cols], r.n2_o.at[mine, :])
        swap_gg = [
            swap_copy(r.gg_hbm.at[:, at : at + size], r.gg_o.at[i, :, 0:size])
            for i, (at, size) in enumerate(gg_cuts)
        ]
        swap_gb = swap_copy(r.gb.at[mine, theirs_cols], r.gb_o.at[mine, :])
        swap_gqkv = swap_copy(r.gqkv, r.gqkv_o)
        swap_n1 = swap_copy(r.n1_hbm.at[:, theirs_cols], r.n1_o)
        for copy in (*swap_hid, swap_n2, *swap_gg):
            copy.start()

    chunks = r.own_fin.shape[1]
    span = r.own_fin.shape[3]

    def core_copy(b, c):
        return remote(
            r.stage_core.at[b, c], r.got_core.at[b, c], r.core_send.at[b, c],
            r.core_recv.at[b, c], core_mate,
        )

    def x_copy(b, c):
        return remote(
            r.stage_x.at[b, c], r.got_x.at[b, c], r.x_send.at[b, c], r.x_recv.at[b, c], chip_mate
        )

    def start_sum(b, tile, product, send):
        routes = (
            ((1 - chip) * 2 + 1 - core, lambda c, at, v: put(r.stage_core, (b, c, 0), at, v)),
            (chip * 2 + 1 - core, lambda c, at, v: put(r.stage_core, (b, c, 1), at, v)),
            ((1 - chip) * 2 + core, lambda c, at, v: put(r.own_fwd, (c,), at, v)),
            (chip * 2 + core, lambda c, at, v: put(r.own_fin, (b, c), at, v)),
        )

        def put(ref, index, at, value):
            ref[(*index, slice(None), at)] = value.astype(ref.dtype)

        def forward_chunk(c):
            core_copy(b, c).wait_recv()
            r.stage_x[b, c] = (r.own_fwd[c] + r.got_core[b, c, 0].astype(f32)).astype(bf16)
            if send:
                x_copy(b, c).start()

        @pl.loop(0, chunks)
        def _(c):
            for t in range(span // 256):
                n = c * (span // 256) + t
                tile(n).wait()
                r.tmp[...] = product(lax.rem(n, 3))
                for owner, route in routes:
                    route(c, slice(t * 256, t * 256 + 256), r.tmp[aligned(owner, quarter), :])

                @pl.when(n + 3 < width // 256)
                def _():
                    tile(n + 3).start()

            core_copy(b, c).start()
            pl.when(c > 0)(lambda: forward_chunk(c - 1))

        forward_chunk(chunks - 1)

    def finish_sum(b):
        for c in range(chunks):
            x_copy(b, c).wait_recv()
            r.own_fin[b, c] = (
                r.own_fin[b, c] + r.got_core[b, c, 1].astype(f32) + r.got_x[b, c].astype(f32)
            )
        for c in range(chunks):
            core_copy(b, c).wait_send()
            x_copy(b, c).wait_send()

    def back_through_norm(b, values, gain_ref, gain_row, emit):
        square = jnp.zeros((quarter, 1), f32)
        inner = jnp.zeros((quarter, 1), f32)
        for c in range(chunks):
            at = slice(c * span, (c + 1) * span)
            v = values[:, at].astype(f32)
            square = square + jnp.sum(v * v, -1, keepdims=True)
            inner = inner + jnp.sum(r.own_fin[b, c] * gain_ref[:, at] * v, -1, keepdims=True)
        inverse = lax.rsqrt(square / width + epsilon)
        slope = inner / width * (inverse * inverse * inverse)
        for c in range(chunks):
            at = slice(c * span, (c + 1) * span)
            v = values[:, at].astype(f32)
            dn = r.own_fin[b, c]
            r.gain_sum[0, gain_row : gain_row + 1, at] = jnp.sum(dn * v * inverse, 0, keepdims=True)
            emit(at, inverse * dn * gain_ref[:, at] - v * slope)

    def gather(i, src, dst):
        def copy(slot, src, owner, mate):
            return remote(
                src, dst.at[aligned(owner, quarter), :], r.ag_send.at[i, slot],
                r.ag_recv.at[i, slot], mate,
            )

        other = chip_mate["tensor"]
        return (
            copy(0, src, tensor, chip_mate),
            copy(1, src, tensor, core_mate),
            copy(2, dst.at[aligned(other, quarter), :], other, core_mate),
        )

    if swap:
        is_end = (place == 0) | (place == 3)
        is_mid = jnp.logical_not(is_end)
        beside = place + 1 - 2 * lax.rem(place, 2)
        low_side = place < 2
        io_mate, across_mate = {"context": beside}, {"context": 3 - place}
        plan = []
        for i, (at, size) in enumerate(hid_cuts):
            cut = (r.g_hbm.at[:, mine_cols], r.go_hbm) if i == 0 else None
            plan.append(
                (cut, r.hid.at[:, at : at + size], r.hid_o.at[i], size,
                 r.dwdown_out.at[:, at : at + size])
            )
        for i, (at, size) in enumerate(gg_cuts):
            cut = (r.n2_hbm.at[:, mine_cols], r.n2_o) if i == 0 else None
            plan.append(
                (cut, r.gg.at[:, at : at + size], r.gg_o.at[i], size,
                 r.dgu_out.at[:, at : at + size])
            )
        cut = (r.gb.at[:, mine_cols], r.gb_o)
        plan.append((cut, r.att_low, r.att_o, heads_width, r.dwout_out))
        cut = (r.n1_hbm.at[:, mine_cols], r.n1_o)
        plan.append((cut, r.gqkv, r.gqkv_o, r.gqkv.shape[1], r.dwqkv_out))
        sets = r.stage.shape[0]
        last = len(plan) - 1
        first_gg = len(hid_cuts)

        def cut_loads(u):
            own, other = plan[u][0]
            return (
                pltpu.make_async_copy(own, r.cut.at[0:rows], r.cut_sem.at[0]),
                pltpu.make_async_copy(other, r.cut.at[rows : 2 * rows], r.cut_sem.at[1]),
            )

        def piece(ref, s, j, u):
            return ref.at[s, j, :, 0 : plan[u][3]]

        def line_copy(u, j, slot, mate):
            s = u % sets
            return remote(
                piece(r.stage, s, j, u), piece(r.got, s, slot, u), r.line_send.at[s, j],
                r.line_recv.at[s, slot], mate,
            )

        def result(u):
            return pltpu.make_async_copy(
                r.sums.at[u % sets, :, 0 : plan[u][3]], plan[u][4], r.sums_sem.at[u % sets]
            )

        def prepare(u, load_next=None):
            s = u % sets
            own, other, width_u = plan[u][1], plan[u][2], plan[u][3]
            if u >= sets:
                for j in range(3):
                    line_copy(u - sets, j, 0, io_mate).wait_send()
                result(u - sets).wait()
                pl.when(is_end)(lambda: pl.semaphore_wait(r.io_credit, 1))
            if plan[u][0] is not None:
                for copy in cut_loads(u):
                    copy.wait()

            @pl.loop(0, 4)
            def _(j):
                chunk = jnp.where(
                    j == 0,
                    jnp.where(low_side, 3, 0),
                    jnp.where(
                        j == 1, jnp.where(low_side, 2, 1), jnp.where(j == 2, beside, place)
                    ),
                )
                r.turned[...] = r.cut[:, aligned(chunk, 256)].astype(f32).T.astype(bf16)

                def block(at):
                    term = dot(r.turned[:, 0:rows], own[:, at]) + dot(
                        r.turned[:, rows : 2 * rows], other[:, at]
                    )

                    @pl.when(j < 3)
                    def _():
                        r.stage[s, j, :, at] = term.astype(bf16)

                    @pl.when(j == 3)
                    def _():
                        r.sums[s, :, at] = term

                @pl.loop(0, width_u // 256)
                def _(tile):
                    block(aligned(tile, 256))

                if width_u % 256:
                    block(slice(width_u - width_u % 256, width_u))

                @pl.when((j < 3) & is_end)
                def _():
                    line_copy(u, j, j, io_mate).start()

            if load_next is not None:
                for copy in cut_loads(load_next):
                    copy.start()

        def add_in(u, j, slot):
            width_u, s = plan[u][3], u % sets
            line_copy(u, 0, slot, io_mate).wait_recv()

            @pl.loop(0, 4)
            def _(i):
                at = aligned(i, 64)
                total = r.stage[s, j, at, 0:width_u].astype(f32)
                total = total + r.got[s, slot, at, 0:width_u].astype(f32)
                r.stage[s, j, at, 0:width_u] = total.astype(bf16)

        def pass_on(u, step):
            @pl.when(is_mid)
            def _():
                if step < 2:
                    add_in(u, step, step)
                    if u >= sets and step == 0:
                        pl.semaphore_wait(r.across_credit, 1)
                    line_copy(u, step, 3 + step, across_mate).start()
                else:
                    add_in(u, 2, 3)
                    if u >= sets:
                        pl.semaphore_wait(r.io_credit, 1)
                    line_copy(u, 2, 0, io_mate).start()

        def complete(u):
            width_u, s = plan[u][3], u % sets

            def take(slots):
                for slot in slots:
                    line_copy(u, 0, slot, io_mate).wait_recv()

                @pl.loop(0, 4)
                def _(i):
                    at = aligned(i, 64)
                    total = r.sums[s, at, 0:width_u]
                    for slot in slots:
                        total = total + r.got[s, slot, at, 0:width_u].astype(f32)
                    r.sums[s, at, 0:width_u] = total

            @pl.when(is_end)
            def _():
                take((0,))

            @pl.when(is_mid)
            def _():
                take((2, 4))

            result(u).start()
            if u + sets <= last:
                pl.semaphore_signal(r.io_credit, inc=1, device_id=io_mate, device_id_type=MESH)

                @pl.when(is_mid)
                def _():
                    pl.semaphore_signal(
                        r.across_credit, inc=1, device_id=across_mate, device_id_type=MESH
                    )

        late = (
            pltpu.make_async_copy(r.attlow_hbm, r.att_low, r.late_sem.at[0]),
            pltpu.make_async_copy(r.atto_hbm, r.att_o, r.late_sem.at[1]),
        )
        for copy in (*cut_loads(0), *late):
            copy.start()

    r.gain_sum[...] = jnp.zeros_like(r.gain_sum)

    loads["gg"].wait()
    start_sum(0, tile_gu, lambda slot: dot_t(r.gg[...], r.w_rows[slot]), True)
    loads["hid"].wait()
    if swap:
        swap_hid[0].wait_recv()
        prepare(0)
    for n in range(3):
        tile_qkv(n).start()
    finish_sum(0)
    loads["resid"].wait()
    loads["g_own"].wait()

    def keep_resid(at, grad):
        total = r.g_own[:, at].astype(f32) + grad
        r.grad_resid[:, at] = total
        r.gb[mine, at] = total.astype(bf16)

    back_through_norm(0, r.resid, r.gain_two, 1, keep_resid)
    gb_chip, gb_core, gb_onward = gather(0, r.gb.at[mine, :], r.gb)
    gb_chip.start()
    gb_core.start()
    if swap:
        swap_gb.start()
    start_sum(1, tile_down, lambda slot: dot(r.hid[...], r.w_cols[slot]), False)
    for c in range(chunks):
        x_copy(1, c).start()
    if swap:
        pass_on(0, 0)
        swap_hid[1].wait_recv()
        prepare(1)
        pass_on(0, 1)
    gb_chip.wait_recv()
    gb_onward.start()
    if swap:
        swap_n2.wait_recv()
        n2_chip, n2_core, n2_onward = gather(3, r.n2_o.at[mine, :], r.n2_o)
        n2_chip.start()
        n2_core.start()
    gb_core.wait_recv()
    gb_onward.wait_recv()
    if not swap:
        pltpu.make_async_copy(r.gb, r.gb_out, r.cut_sem.at[0]).start()

    loads["wout"].wait()
    for i in range(heads_width // 256):
        at = slice(i * 256, i * 256 + 256)
        r.ga[:, at] = dot_t(r.gb[...], r.wout[at, :]).astype(bf16)
    loads["att"].wait()

    @pl.loop(0, heads_width // 128)
    def _(pair):
        at = aligned(pair, 128)
        product = r.ga[:, at].astype(f32).T * r.att[at, :]
        for e in range(2):
            r.delta[pair * 2 + e] = jnp.sum(product[64 * e : 64 * e + 64], 0, keepdims=True)

    if swap:
        pass_on(0, 2)

    loads["q"].wait()
    loads["kv"].wait()
    r.dq[...] = jnp.zeros_like(r.dq)
    key_lane = lanes((rows, 128)) < 64

    def back_block(k, first):
        block = r.kv[k].astype(f32)
        rolled = pltpu.roll(block, 64, 1)
        r.keys[0] = jnp.where(key_lane, block, 0.0).astype(bf16)
        r.keys[1] = jnp.where(key_lane, 0.0, rolled).astype(bf16)
        r.vals[0] = jnp.where(key_lane, rolled, 0.0).astype(bf16)
        r.vals[1] = jnp.where(key_lane, 0.0, block).astype(bf16)
        r.keys_t[...] = block.T[:64].astype(bf16)
        r.dk[...] = jnp.zeros_like(r.dk)
        r.dv[...] = jnp.zeros_like(r.dv)

        @pl.loop(0, heads_width // 128)
        def _(pair):
            pair_q = r.q[:, aligned(pair, 128)]
            pair_ga = r.ga[:, aligned(pair, 128)]
            for e in range(2):
                head = pair * 2 + e
                scores = dot_t(r.keys[e], pair_q)
                key_index = (place - k) * rows + lax.broadcasted_iota(jnp.int32, (rows, rows), 0)
                allowed = key_index >= r.seg[...]
                if first:
                    query_index = place * rows + lax.broadcasted_iota(jnp.int32, (rows, rows), 1)
                    allowed = allowed & (key_index <= query_index)
                probs = jnp.where(allowed, jnp.exp(scores - r.lse[head]), 0.0)
                grad_probs = dot_t(r.vals[e], pair_ga)
                grad_scores = (probs * (grad_probs - r.delta[head])).astype(bf16)
                r.dv[e] += dot(probs.astype(bf16), pair_ga)
                r.dk[e] += dot(grad_scores, pair_q)
                r.dq[aligned(head, 64), :] += dot(r.keys_t[...], grad_scores)

        return jnp.where(
            key_lane,
            r.dk[0] + pltpu.roll(r.dk[1], 64, 1),
            r.dv[1] + pltpu.roll(r.dv[0], 64, 1),
        )

    def dkv_copy(k, mate):
        return remote(
            r.stage_kv.at[k], r.got_kv.at[k], r.kv_send.at[k], r.kv_recv.at[k], {"context": mate}
        )

    @pl.loop(0, place)
    def _(i):
        k = place - i
        r.stage_kv[k] = back_block(k, False).astype(bf16)
        dkv_copy(k, i).start()

    r.dkv[...] = back_block(0, True)
    if swap:
        pass_on(1, 0)
        pass_on(1, 1)
        n2_chip.wait_recv()
        n2_onward.start()
        n2_core.wait_recv()
        n2_onward.wait_recv()
        for copy in cut_loads(first_gg):
            copy.start()
        swap_gg[0].wait_recv()
        prepare(2)
        complete(0)

    @pl.loop(0, heads_width // 128)
    def _(pair):
        at = aligned(pair, 128)
        turned = turn(r.dq[at, :].T * 0.125, r.cos[...], -r.sin[...])
        r.gqkv[:, at] = turned.astype(bf16)

    for k in (1, 2, 3):

        @pl.when(place + k < 4)
        def _():
            dkv_copy(k, 0).wait_recv()
            r.dkv[...] += r.got_kv[k].astype(f32)

    r.gqkv[:, heads_width : heads_width + 128] = turn(
        r.dkv[...], jnp.where(key_lane, r.cos[...], 1.0), jnp.where(key_lane, -r.sin[...], 0.0)
    ).astype(bf16)
    if swap:
        swap_gqkv.start()
        swap_n1.start()
        pass_on(1, 2)
    else:
        pltpu.make_async_copy(r.gqkv, r.gqkv_out, r.cut_sem.at[1]).start()

    start_sum(
        0, tile_qkv,
        lambda slot: dot_t(r.gqkv[...], r.w_rows[slot, :, 0 : r.gqkv.shape[1]]), True,
    )
    if swap:
        swap_gg[1].wait_recv()
        prepare(3)
        complete(1)
        pass_on(2, 0)

    finish_sum(0)
    loads["x_own"].wait()

    def keep_tokens(at, grad):
        r.tokens_own[:, at] = (r.grad_resid[:, at] + grad).astype(bf16)

    back_through_norm(0, r.x_own, r.gain_one, 0, keep_tokens)
    tokens_chip, tokens_core, tokens_onward = gather(2, r.tokens_own, r.tokens_out)
    tokens_store = pltpu.make_async_copy(r.tokens_own, r.tokens_out.at[mine, :], r.out_sem.at[1])
    for copy in (tokens_chip, tokens_core, tokens_store):
        copy.start()
    if swap:
        pass_on(2, 1)
        pass_on(2, 2)
        swap_gg[2].wait_recv()
        prepare(4)

    finish_sum(1)
    for c in range(chunks):
        at = slice(c * span, (c + 1) * span)
        r.mixed_own[:, at] = (r.resid[:, at] + r.own_fin[1, c]).astype(bf16)
    mixed_chip, mixed_core, mixed_onward = gather(1, r.mixed_own, r.mixed_out)
    mixed_store = pltpu.make_async_copy(r.mixed_own, r.mixed_out.at[mine, :], r.out_sem.at[0])
    for copy in (mixed_chip, mixed_core, mixed_store):
        copy.start()
    if swap:
        complete(2)
        pass_on(3, 0)
        swap_gg[3].wait_recv()
        for copy in late:
            copy.wait()
        prepare(5)
        swap_gb.wait_recv()
        gbo_chip, gbo_core, gbo_onward = gather(4, r.gb_o.at[mine, :], r.gb_o)
        gbo_chip.start()
        gbo_core.start()
        pass_on(3, 1)
        pass_on(3, 2)

    for i, mate in enumerate((core_mate, chip_mate)):
        copy = remote(
            r.gain_sum.at[i], r.gain_got.at[i], r.gain_send.at[i], r.gain_recv.at[i], mate
        )
        copy.start()
        copy.wait()
        r.gain_sum[i + 1] = r.gain_sum[i] + r.gain_got[i]
    if swap:
        copy = remote(
            r.gain_sum.at[2, :, theirs_cols], r.gain_half.at[0], r.gain_send.at[2],
            r.gain_recv.at[2], dp_mate,
        )
        copy.start()
        copy.wait()
        r.gain_half[1] = r.gain_sum[2, :, mine_cols] + r.gain_half[0]
        part = half // 4
        pieces = [
            remote(
                r.gain_half.at[1, :, aligned(lax.rem(place + k, 4), part)], r.gain_piece.at[k],
                r.gain_send.at[2 + k], r.gain_recv.at[2 + k], {"context": lax.rem(place + k, 4)},
            )
            for k in (1, 2, 3)
        ]
        for copy in pieces:
            copy.start()
        complete(3)
    else:
        r.gains_out[...] = r.gain_sum[2]
    tokens_chip.wait_recv()
    tokens_onward.start()
    mixed_chip.wait_recv()
    mixed_onward.start()
    if swap:
        gbo_chip.wait_recv()
        gbo_onward.start()
        gbo_core.wait_recv()
        gbo_onward.wait_recv()
        for copy in cut_loads(last - 1):
            copy.start()
        prepare(6)
        swap_n1.wait_recv()
        for copy in cut_loads(last):
            copy.start()
        for step in range(3):
            pass_on(4, step)
        complete(4)
        swap_gqkv.wait_recv()
        prepare(7)
        for u in (5, 6, 7):
            for step in range(3):
                pass_on(u, step)
            complete(u)
        for copy in pieces:
            copy.wait()
        r.gains_out[...] = (
            r.gain_half[1, :, aligned(place, part)]
            + r.gain_piece[1]
            + r.gain_piece[2]
            + r.gain_piece[3]
        )

    for copy in (mixed_core, mixed_onward, tokens_core, tokens_onward):
        copy.wait_recv()
    for copy in (
        gb_chip, gb_core, gb_onward, mixed_chip, mixed_core, mixed_onward, tokens_chip,
        tokens_core, tokens_onward,
    ):
        copy.wait_send()
    mixed_store.wait()
    tokens_store.wait()
    for k in (1, 2, 3):
        pl.when(place >= k)(dkv_copy(k, 0).wait_send)
    if swap:
        for copy in (
            *swaps, n2_chip, n2_core, n2_onward, gbo_chip, gbo_core, gbo_onward
        ):
            copy.wait_send()
        for u in range(last + 1 - sets, last + 1):
            for j in range(3):
                line_copy(u, j, 0, io_mate).wait_send()
            result(u).wait()
    else:
        pltpu.make_async_copy(r.gb, r.gb_out, r.cut_sem.at[0]).wait()
        pltpu.make_async_copy(r.gqkv, r.gqkv_out, r.cut_sem.at[1]).wait()


def backward(swap, inputs, rows, width, units, heads):
    bf16, f32 = jnp.bfloat16, jnp.float32
    quarter = rows // 4
    chunks = 4
    span = width // chunks
    wide = heads * HD
    qkv = wide + 2 * HD
    lead, sets = 768, 3
    outs = {
        "mixed_out": ((rows, width), bf16),
        "tokens_out": ((rows, width), bf16),
        "gains_out": ((8, width // 8 if swap else width), f32),
    }
    if swap:
        outs |= {
            "dwdown_out": ((width // 8, units), f32),
            "dgu_out": ((width // 8, 2 * units), f32),
            "dwout_out": ((width // 8, wide), f32),
            "dwqkv_out": ((width // 8, qkv), f32),
            "n2_o": ((rows, width // 2), bf16),
            "gb_o": ((rows, width // 2), bf16),
            "n1_o": ((rows, width // 2), bf16),
        }
    else:
        outs |= {"gb_out": ((rows, width), bf16), "gqkv_out": ((rows, qkv), bf16)}
    scratch = {
        "gg": ((rows, 2 * units), bf16),
        "hid": ((rows, units), bf16),
        "resid": ((quarter, width), f32),
        "g_own": ((quarter, width), bf16),
        "x_own": ((quarter, width), bf16),
        "wout": ((wide, width), bf16),
        "q": ((rows, wide), bf16),
        "kv": ((4, rows, 2 * HD), bf16),
        "att": ((wide, rows), f32),
        "w_rows": ((3, 256, 2 * units), bf16),
        "w_cols": ((3, units, 256), bf16),
        "tmp": ((rows, 256), f32),
        "stage_core": ((2, chunks, 2, quarter, span), bf16),
        "got_core": ((2, chunks, 2, quarter, span), bf16),
        "own_fwd": ((chunks, quarter, span), f32),
        "own_fin": ((2, chunks, quarter, span), f32),
        "stage_x": ((2, chunks, quarter, span), bf16),
        "got_x": ((2, chunks, quarter, span), bf16),
        "grad_resid": ((quarter, width), f32),
        "gb": ((rows, width), bf16),
        "ga": ((rows, wide), bf16),
        "mixed_own": ((quarter, width), bf16),
        "tokens_own": ((quarter, width), bf16),
        "delta": ((heads, 1, rows), f32),
        "dq": ((wide, rows), f32),
        "keys": ((2, rows, 2 * HD), bf16),
        "vals": ((2, rows, 2 * HD), bf16),
        "keys_t": ((HD, rows), bf16),
        "dk": ((2, rows, 2 * HD), f32),
        "dv": ((2, rows, 2 * HD), f32),
        "dkv": ((rows, 2 * HD), f32),
        "stage_kv": ((4, rows, 2 * HD), bf16),
        "got_kv": ((4, rows, 2 * HD), bf16),
        "gqkv": ((rows, qkv), bf16),
        "gain_sum": ((3, 8, width), f32),
        "gain_got": ((2, 8, width), f32),
    }
    if swap:
        scratch |= {
            "hid_o": ((-(-units // lead), rows, lead), bf16),
            "gg_o": ((-(-2 * units // lead), rows, lead), bf16),
            "gqkv_o": ((rows, qkv), bf16),
            "att_low": ((rows, wide), bf16),
            "att_o": ((rows, wide), bf16),
            "cut": ((2 * rows, width // 2), bf16),
            "turned": ((256, 2 * rows), bf16),
            "stage": ((sets, 3, width // 8, lead), bf16),
            "got": ((sets, 5, width // 8, lead), bf16),
            "sums": ((sets, width // 8, lead), f32),
            "gain_half": ((2, 8, width // 2), f32),
            "gain_piece": ((4, 8, width // 8), f32),
        }
    sems = {
        "load_sem": (9,),
        "w_rows_sem": (3,),
        "w_cols_sem": (3,),
        "w_kv_sem": (3,),
        "core_send": (2, chunks),
        "core_recv": (2, chunks),
        "x_send": (2, chunks),
        "x_recv": (2, chunks),
        "ag_send": (5, 3),
        "ag_recv": (5, 3),
        "kv_send": (4,),
        "kv_recv": (4,),
        "gain_send": (6,),
        "gain_recv": (6,),
        "out_sem": (2,),
        "cut_sem": (2,),
    }
    if swap:
        sems |= {
            "dp_send": (10,),
            "dp_recv": (10,),
            "line_send": (sets, 3),
            "line_recv": (sets, 5),
            "sums_sem": (sets,),
            "late_sem": (2,),
        }
    credits = ["io_credit", "across_credit"] if swap else []
    names = [*inputs, *outs, *scratch, *sems, *credits]
    anywhere = pl.BlockSpec(memory_space=pl.ANY)
    inside = pl.BlockSpec(memory_space=pltpu.VMEM)
    results = pl.pallas_call(
        functools.partial(backward_kernel, names, swap),
        out_shape=[jax.ShapeDtypeStruct(*out) for out in outs.values()],
        in_specs=[anywhere if name.endswith("_hbm") else inside for name in inputs],
        out_specs=[inside if name == "gains_out" else anywhere for name in outs],
        scratch_shapes=[
            *(pltpu.VMEM(*shape) for shape in scratch.values()),
            *(pltpu.SemaphoreType.DMA(shape) for shape in sems.values()),
            *(pltpu.SemaphoreType.REGULAR for _ in credits),
        ],
        compiler_params=pltpu.CompilerParams(
            collective_id=1, has_side_effects=True, vmem_limit_bytes=63 * MIB
        ),
        name="backward",
    )(*inputs.values())
    return dict(zip(outs, results, strict=True))


def finish_kernel(
    down_hbm, gateup_hbm, out_hbm, qkv_hbm, tokens_hbm, mixed_hbm,
    down_o, gateup_o, out_o, q_o, kv_o, tokens_o, mixed_o,
    down, gateup, out, qkv, tokens, mixed, down_t, gateup_t, out_t, kv_t, tokens_t,
    load_sem, store_sem,
):
    wide = q_o.shape[1]
    parts = 4
    loads, stores = [], []

    def load(src, dst):
        copy = pltpu.make_async_copy(src, dst, load_sem.at[len(loads)])
        copy.start()
        loads.append(copy)
        return copy

    def store(src, dst):
        copy = pltpu.make_async_copy(src, dst, store_sem.at[len(stores)])
        copy.start()
        stores.append(copy)

    def piece(ref, i):
        size = ref.shape[0] // parts
        return ref.at[i * size : (i + 1) * size]

    token_loads = [load(piece(tokens_hbm, i), piece(tokens, i)) for i in range(parts)]
    gateup_loads = [load(piece(gateup_hbm, i), piece(gateup, i)) for i in range(parts)]
    load_mixed = load(mixed_hbm, mixed)
    load_down = load(down_hbm, down)
    load_qkv = load(qkv_hbm, qkv)
    load_out = load(out_hbm, out)
    for i in range(parts):
        token_loads[i].wait()
        piece(tokens_t, i)[...] = piece(tokens, i)[...].astype(jnp.float32)
        store(piece(tokens_t, i), piece(tokens_o, i))
    for i in range(parts):
        gateup_loads[i].wait()
        values, target = piece(gateup, i), piece(gateup_t, i)
        for b in range(gateup.shape[1] // 256):
            at = slice(b * 128, b * 128 + 128)
            target[:, 0, at] = values[:, b * 256 : b * 256 + 128]
            target[:, 1, at] = values[:, b * 256 + 128 : b * 256 + 256]
        store(target, piece(gateup_o, i))
    load_mixed.wait()
    store(mixed, mixed_o)
    load_down.wait()
    for i in range(down.shape[1] // 128):
        at = slice(i * 128, i * 128 + 128)
        down_t[at, :] = down[:, at].T
    store(down_t, down_o)
    load_qkv.wait()
    store(qkv.at[:, 0:wide], q_o)
    kv_t[:, 0, :] = qkv[:, wide:]
    store(kv_t, kv_o)
    load_out.wait()
    for i in range(wide // 128):
        at = slice(i * 128, i * 128 + 128)
        out_t[at, :] = out[:, at].T
    store(out_t, out_o)
    for copy in stores:
        copy.wait()


def finish(down, gateup, out, qkv, tokens, mixed):
    depth, units = down.shape
    wide = out.shape[1]
    rows, width = tokens.shape
    bf16, f32 = jnp.bfloat16, jnp.float32
    outs = [
        ((units, depth), f32),
        ((depth, 2, units), f32),
        ((wide, depth), f32),
        ((depth, wide), f32),
        ((depth, 1, 2 * HD), f32),
        ((rows, width), f32),
        ((rows, width), bf16),
    ]
    scratch = [
        *((array.shape, array.dtype) for array in (down, gateup, out, qkv, tokens, mixed)),
        *outs[:3],
        *outs[4:6],
    ]
    anywhere = pl.BlockSpec(memory_space=pl.ANY)
    return pl.pallas_call(
        finish_kernel,
        out_shape=[jax.ShapeDtypeStruct(*entry) for entry in outs],
        in_specs=[anywhere] * 6,
        out_specs=[anywhere] * len(outs),
        scratch_shapes=[
            *(pltpu.VMEM(*entry) for entry in scratch),
            pltpu.SemaphoreType.DMA((12,)),
            pltpu.SemaphoreType.DMA((13,)),
        ],
        compiler_params=pltpu.CompilerParams(vmem_limit_bytes=62 * MIB),
        name="finish",
    )(down, gateup, out, qkv, tokens, mixed)


def pick(array, index, axis):
    return lax.dynamic_index_in_dim(array, index, axis, keepdims=False)


def line_sum(part):
    place = lax.axis_index("context")
    order = jnp.array([[3, 2, 1, 0], [3, 2, 0, 1], [0, 1, 3, 2], [0, 1, 2, 3]], jnp.int32)[place]
    first, second, third, own = (part(order[i]) for i in range(4))

    def inward(array):
        return lax.ppermute(array.astype(jnp.bfloat16), "context", [(0, 1), (3, 2)])

    def across(array):
        return lax.ppermute(array.astype(jnp.bfloat16), "context", [(1, 2), (2, 1)])

    def outward(array):
        return lax.ppermute(array.astype(jnp.bfloat16), "context", [(1, 0), (2, 3)])

    in_one, in_two, in_three = inward(first), inward(second), inward(third)
    over_two = across(first + in_one.astype(jnp.float32))
    over_three = across(second + in_two.astype(jnp.float32))
    out_three = outward(third + over_two.astype(jnp.float32))
    return (
        own
        + in_three.astype(jnp.float32)
        + over_three.astype(jnp.float32)
        + out_three.astype(jnp.float32)
    )


def weight_grad(left, right, axis):
    whole = lax.dot_general(
        left, right, (((0,), (0,)), ((), ())), preferred_element_type=jnp.float32
    )
    mine = lax.psum_scatter(
        whole.astype(jnp.bfloat16), "dp", scatter_dimension=axis, tiled=True
    )
    step = mine.shape[axis] // 4
    return line_sum(
        lambda chunk: lax.dynamic_slice_in_dim(mine, chunk * step, step, axis).astype(jnp.float32)
    )


def tables(positions):
    cosine, sine = angles(positions, HD)
    return jnp.concatenate([cosine] * 4, 1), jnp.concatenate([-sine, sine] * 2, 1)


def shards(
    tokens, segments, gain_one, w_query, w_keyval, w_out, gain_two, w_gateup, w_down, cotangent
):
    num_seqs, tok_count, model_width = tokens.shape
    heads_kv = w_keyval.shape[1]
    width_q = w_query.shape[1]
    units = w_down.shape[0]
    swap = lax.axis_size("dp") == 2
    x = tokens.reshape(tok_count, model_width)
    g = cotangent.reshape(tok_count, model_width)
    query_index = lax.axis_index("context") * tok_count + jnp.arange(tok_count, dtype=jnp.int32)
    cosine, sine = tables(query_index - segments[0])
    w_kv = w_keyval.reshape(model_width, 2 * HD)
    one, two = gain_one[None], gain_two[None]
    (
        queries, kv, attended, log_total, normed_one, normed_two, resid, hidden, grad_gateup, w_gu,
        attended_low, g_other, attended_other,
    ) = forward(
        swap, x, segments, cosine, sine, one, two, w_query, w_kv, w_out, w_gateup, w_down, g
    )
    inputs = {
        "seg": segments, "cos": cosine, "sin": sine, "gain_one": one, "gain_two": two,
        "lse": log_total, "q_hbm": queries, "kv_hbm": kv, "att_hbm": attended,
        "resid_hbm": resid, "hid_hbm": hidden, "gg_hbm": grad_gateup, "wgu_hbm": w_gu,
        "wdown_hbm": w_down, "wout_hbm": w_out, "wq_hbm": w_query, "wkv_hbm": w_kv, "x_hbm": x,
        "g_hbm": g,
    }
    if swap:
        inputs |= {
            "n1_hbm": normed_one, "n2_hbm": normed_two, "attlow_hbm": attended_low,
            "go_hbm": g_other, "atto_hbm": attended_other,
        }
    out = backward(swap, inputs, tok_count, model_width, units, width_q // HD)
    if swap:
        gains = out["gains_out"]
        sent_wdown, sent_gateup, sent_wout, sent_wq, sent_wkv, grad_tokens, mixed = finish(
            *(out[name] for name in ("dwdown_out", "dgu_out", "dwout_out", "dwqkv_out")),
            out["tokens_out"],
            out["mixed_out"],
        )
    else:
        gains = lax.psum_scatter(
            out["gains_out"], ("dp", "context"), scatter_dimension=1, tiled=True
        )
        sent_wdown = weight_grad(hidden, g, 1)
        sent_gateup = weight_grad(normed_two, grad_gateup, 0)
        sent_wout = weight_grad(attended_low, out["gb_out"], 1)
        sent_wqkv = weight_grad(normed_one, out["gqkv_out"], 0)
        sent_wq, sent_wkv = sent_wqkv[:, :width_q], sent_wqkv[:, width_q:]
        sent_gateup = sent_gateup.reshape(-1, units // 128, 2, 128).transpose(0, 2, 1, 3)
        grad_tokens, mixed = out["tokens_out"].astype(jnp.float32), out["mixed_out"]
    return (
        mixed.reshape(tokens.shape),
        grad_tokens.reshape(tokens.shape),
        gains[0],
        sent_wq,
        sent_wkv.reshape(-1, heads_kv, 2 * HD),
        sent_wout,
        gains[1],
        sent_gateup.reshape(-1, 2, units),
        sent_wdown,
    )


def solution(mesh):
    return jax.shard_map(
        shards,
        mesh=mesh,
        in_specs=(
            P("dp", "context", None),
            P("dp", "context"),
            P(),
            P(None, "tensor"),
            P(None, "tensor", None),
            P("tensor", None),
            P(),
            P(None, None, "tensor"),
            P("tensor", None),
            P("dp", "context", None),
        ),
        out_specs=(
            P("dp", "context", None),
            P("dp", "context", None),
            P(("dp", "context")),
            P(("dp", "context"), "tensor"),
            P(("dp", "context"), "tensor", None),
            P("tensor", ("dp", "context")),
            P(("dp", "context")),
            P(("dp", "context"), None, "tensor"),
            P("tensor", ("dp", "context")),
        ),
        check_vma=False,
    )
```

```python
import functools
import types

import jax
import jax.numpy as jnp
import numpy as np
from jax import lax
from jax.experimental import pallas as pl
from jax.experimental.pallas import tpu as pltpu
from jax.sharding import PartitionSpec as P

HD = 64


epsilon = 1e-05
neg_large = -1e30


MESH = pl.DeviceIdType.MESH
MIB = 1 << 20
log2_e = 1.4426950408889634


def dot(left, right):
    return jnp.dot(left, right, preferred_element_type=jnp.float32)


def dot_t(left, right):
    return lax.dot_general(left, right, (((1,), (1,)), ((), ())), preferred_element_type=jnp.float32)


def lanes(shape):
    return lax.broadcasted_iota(jnp.int32, shape, len(shape) - 1)


def turn_of(n, size):
    return n % size if isinstance(n, int) else lax.rem(n, size)


def aligned(index, size):
    if isinstance(index, int):
        return pl.ds(index * size, size)
    return pl.ds(pl.multiple_of(index * size, size), size)


def turn(values, cosine, sine):
    low_half = lax.rem(lanes(values.shape), 64) < 32
    swapped = jnp.where(low_half, pltpu.roll(values, 96, 1), pltpu.roll(values, 32, 1))
    return values * cosine + swapped * sine


def cos_sin(phase):
    count = jnp.floor(phase * 0.6366197723675814 + 0.5)
    rest = phase - count * 1.5703125
    rest = rest - count * 0.0004837512969970703
    rest = rest - count * 7.549789954e-08
    square = rest * rest
    sine = rest + rest * square * (
        -0.16666666666 + square * (0.0083333333333 + square * -0.0001984126984)
    )
    cosine = 1.0 + square * (
        -0.5 + square * (0.041666666666 + square * (-0.0013888888889 + square * 2.48015873e-05))
    )
    place = count - 4.0 * jnp.floor(count * 0.25)
    odd = (place == 1.0) | (place == 3.0)
    first, second = jnp.where(odd, sine, cosine), jnp.where(odd, cosine, sine)
    return (
        jnp.where((place == 1.0) | (place == 2.0), -first, first),
        jnp.where(place >= 2.0, -second, second),
    )


def layer_kernel(names, swap, *refs):
    r = types.SimpleNamespace(**dict(zip(names, refs, strict=True)))
    rows, width = r.x_n2.shape
    quarter = rows // 4
    units = r.hid.shape[1]
    heads_width = r.q.shape[1]
    f32, bf16 = jnp.float32, jnp.bfloat16
    tensor = lax.axis_index("tensor")
    place = lax.axis_index("context")
    core, chip = lax.rem(tensor, 2), lax.div(tensor, 2)
    core_mate = {"tensor": chip * 2 + 1 - core}
    chip_mate = {"tensor": (1 - chip) * 2 + core}
    mates = [core_mate, chip_mate, *({"context": lax.rem(place + k, 4)} for k in (1, 2, 3))]
    if swap:
        side = lax.axis_index("dp")
        dp_mate = {"dp": 1 - side}
        mates.append(dp_mate)
    mine = aligned(tensor, quarter)
    key_lane = lanes((rows, 128)) < 64

    barrier = pltpu.get_barrier_semaphore()
    for mate in mates:
        pl.semaphore_signal(barrier, inc=1, device_id=mate, device_id_type=MESH)

    def remote(src, dst, send, recv, mate):
        return pltpu.make_async_remote_copy(
            src_ref=src, dst_ref=dst, send_sem=send, recv_sem=recv, device_id=mate,
            device_id_type=MESH,
        )

    loads, stores = [], []

    def load(src, dst):
        copy = pltpu.make_async_copy(src, dst, r.load_sem.at[len(loads)])
        loads.append(copy)
        copy.start()
        return copy

    def store_copy(i):
        return pltpu.make_async_copy(*stores[i], r.store_sem.at[i])

    def store(src, dst):
        stores.append((src, dst))
        store_copy(len(stores) - 1).start()

    swaps = []

    def swap_copy(src, dst):
        i = len(swaps)
        swaps.append(remote(src, dst, r.dp_send.at[i], r.dp_recv.at[i], dp_mate))
        return swaps[i]

    if swap:
        half = width // 2
        theirs_cols, mine_cols = aligned(1 - side, half), aligned(side, half)
        lead = r.got.shape[3]

        def cuts(total):
            return [(at, min(lead, total - at)) for at in range(0, total, lead)]

        hid_cuts, gg_cuts = cuts(units), cuts(2 * units)
        row_halves = [aligned(chip, rows // 2), aligned(1 - chip, rows // 2)]
        swap_g = swap_copy(r.g_hbm.at[:, theirs_cols], r.g_o)
        swap_low = swap_copy(r.att_low, r.low_o)
        swap_hid = [
            [
                swap_copy(r.hid.at[at_rows, at : at + size], r.hid_o.at[i, at_rows, 0:size])
                for i, (at, size) in enumerate(hid_cuts)
            ]
            for at_rows in row_halves
        ]
        swap_n2 = swap_copy(r.x_n2.at[mine, theirs_cols], r.n2_o.at[mine, :])
        swap_gg = [
            swap_copy(r.gg.at[:, at : at + size], r.gg_o.at[i, :, 0:size])
            for i, (at, size) in enumerate(gg_cuts)
        ]
        swap_gb = swap_copy(r.n1_gb.at[mine, theirs_cols], r.gb_o.at[mine, :])
        swap_n1 = swap_copy(r.n1_out.at[:, theirs_cols], r.n1_o)

    chunks = r.own_fin.shape[1]
    span = r.own_fin.shape[3]

    def core_copy(b, c):
        return remote(
            r.stage_core.at[b, c], r.got_core.at[b, c], r.core_send.at[b, c],
            r.core_recv.at[b, c], core_mate,
        )

    def x_copy(b, c):
        return remote(
            r.stage_x.at[b, c], r.got_x.at[b, c], r.x_send.at[b, c], r.x_recv.at[b, c], chip_mate
        )

    def start_sum(b, tile, product, send=True):
        def put(ref, index, at, value):
            ref[(*index, slice(None), at)] = value.astype(ref.dtype)

        routes = (
            ((1 - chip) * 2 + 1 - core, lambda c, at, v: put(r.stage_core, (b, c, 0), at, v)),
            (chip * 2 + 1 - core, lambda c, at, v: put(r.stage_core, (b, c, 1), at, v)),
            ((1 - chip) * 2 + core, lambda c, at, v: put(r.own_fwd, (c,), at, v)),
            (chip * 2 + core, lambda c, at, v: put(r.own_fin, (b, c), at, v)),
        )

        def forward_chunk(c):
            core_copy(b, c).wait_recv()
            r.stage_x[b, c] = (r.own_fwd[c] + r.got_core[b, c, 0].astype(f32)).astype(bf16)
            if send:
                x_copy(b, c).start()

        @pl.loop(0, chunks)
        def _(c):
            for t in range(span // 256):
                n = c * (span // 256) + t
                if tile is not None:
                    tile(n).wait()
                r.tmp[...] = product(n)
                for owner, route in routes:
                    route(c, slice(t * 256, t * 256 + 256), r.tmp[aligned(owner, quarter), :])
                if tile is not None:

                    @pl.when(n + 3 < width // 256)
                    def _():
                        tile(n + 3).start()

            core_copy(b, c).start()
            pl.when(c > 0)(lambda: forward_chunk(c - 1))

        forward_chunk(chunks - 1)

    def finish_sum(b):
        for c in range(chunks):
            x_copy(b, c).wait_recv()
            r.own_fin[b, c] = (
                r.own_fin[b, c] + r.got_core[b, c, 1].astype(f32) + r.got_x[b, c].astype(f32)
            )
        for c in range(chunks):
            core_copy(b, c).wait_send()
            x_copy(b, c).wait_send()

    def gather(i, src, dst):
        def copy(slot, src, owner, mate):
            return remote(
                src, dst.at[aligned(owner, quarter), :], r.ag_send.at[i, slot],
                r.ag_recv.at[i, slot], mate,
            )

        other = chip_mate["tensor"]
        return (
            copy(0, src, tensor, chip_mate),
            copy(1, src, tensor, core_mate),
            copy(2, dst.at[aligned(other, quarter), :], other, core_mate),
        )

    def mask(bias, k, first):
        key_index = (place - k) * rows + lax.broadcasted_iota(jnp.int32, (rows, rows), 0)
        allowed = key_index >= r.seg[...]
        if first:
            query_index = place * rows + lax.broadcasted_iota(jnp.int32, (rows, rows), 1)
            allowed = allowed & (key_index <= query_index)
        bias[...] = jnp.where(allowed, 0.0, neg_large)

    def pad_keys(keys, block):
        keys[0] = jnp.where(key_lane, block, 0.0).astype(bf16)
        keys[1] = jnp.where(key_lane, 0.0, pltpu.roll(block, 64, 1)).astype(bf16)

    def kv_copy(k):
        return remote(
            r.kv.at[0], r.kv.at[k], r.kv_send.at[k], r.kv_recv.at[k],
            {"context": lax.rem(place + k, 4)},
        )

    def attention(wgu, raw, wq, wkv, keys, vals_t, bias):
        load_x = load(r.x_hbm, r.x_n2)
        load_wkv = load(r.wkv_hbm, wkv)
        load_wq = load(r.wq_hbm, wq)
        ring = raw.shape[0]

        def raw_copy(i):
            slot = turn_of(i, ring)
            return pltpu.make_async_copy(
                r.wgateup_hbm.at[aligned(i, 128)], raw.at[slot], r.raw_sem.at[slot]
            )

        for i in range(ring):
            raw_copy(i).start()

        position = place * rows + lanes((1, rows)) - r.seg[...]
        cosine, sine = cos_sin(r.freqs[...] * position.astype(f32))
        r.cos[...] = jnp.concatenate([cosine] * 4, 0).T
        r.sin[...] = jnp.concatenate([-sine, sine] * 2, 0).T

        load_x.wait()

        @pl.loop(0, rows // 64)
        def _(i):
            at = aligned(i, 64)
            values = r.x_n2[at, :].astype(f32)
            inverse = lax.rsqrt(jnp.mean(values * values, -1, keepdims=True) + epsilon)
            r.n1_gb[at, :] = (values * inverse * r.gain_one[...]).astype(bf16)

        store(r.n1_gb, r.n1_out)

        load_wkv.wait()
        r.kv[0] = turn(
            dot(r.n1_gb[...], wkv[...]),
            jnp.where(key_lane, r.cos[...], 1.0),
            jnp.where(key_lane, r.sin[...], 0.0),
        ).astype(bf16)
        pl.semaphore_wait(barrier, len(mates))
        for k in (1, 2, 3):
            pl.when(place + k < 4)(kv_copy(k).start)
        if swap:
            swap_g.start()

        load_wq.wait()

        @pl.loop(0, heads_width // 256)
        def _(i):
            wide = dot(r.n1_gb[...], wq[:, aligned(i, 256)])
            for part in range(2):
                turned = turn(wide[:, 128 * part : 128 * part + 128], r.cos[...], r.sin[...])
                at = pl.ds(pl.multiple_of(i * 256 + 128 * part, 128), 128)
                r.q[:, at] = (turned * (0.125 * log2_e)).astype(bf16)

        def attend_block(k, first):
            mask(bias, k, first)
            block = r.kv[k].astype(f32)
            pad_keys(keys, block)
            vals_t[...] = block.T[64:].astype(bf16)

            @pl.loop(0, heads_width // 128)
            def _(pair):
                pair_q = r.q[:, aligned(pair, 128)]
                for e in range(2):
                    head = pair * 2 + e
                    scores = dot_t(keys[e], pair_q) + bias[...]
                    top = jnp.max(scores, 0, keepdims=True)
                    at = aligned(head, 64)
                    if first:
                        weights = jnp.exp2(scores - top)
                        r.run_sum[head] = jnp.sum(weights, 0, keepdims=True)
                        r.att[at, :] = dot(vals_t[...], weights.astype(bf16))
                    else:
                        old = r.lse[head]
                        top = jnp.maximum(top, old)
                        fade = jnp.exp2(old - top)
                        weights = jnp.exp2(scores - top)
                        r.run_sum[head] = r.run_sum[head] * fade + jnp.sum(weights, 0, keepdims=True)
                        r.att[at, :] = r.att[at, :] * fade + dot(vals_t[...], weights.astype(bf16))
                    r.lse[head] = top

        attend_block(0, True)

        row = lax.broadcasted_iota(jnp.int32, (256, 256), 0)
        column = lax.broadcasted_iota(jnp.int32, (256, 256), 1)
        source = jnp.where(row < 128, 2 * row, 2 * row - 255)
        order = (column == source).astype(bf16)

        @pl.loop(0, width // 128)
        def _(i):
            raw_copy(i).wait()
            at = aligned(i, 128)
            split = dot(order, raw[turn_of(i, ring)].reshape(256, units)).astype(bf16)
            for b in range(units // 128):
                wgu[at, 256 * b : 256 * b + 128] = split[:128, 128 * b : 128 * b + 128]
                wgu[at, 256 * b + 128 : 256 * b + 256] = split[128:, 128 * b : 128 * b + 128]

            @pl.when(i + ring < width // 128)
            def _():
                raw_copy(i + ring).start()

        @pl.loop(1, place + 1)
        def _(k):
            kv_copy(k).wait_recv()
            attend_block(k, False)

        for k in (1, 2, 3):
            pl.when(place + k < 4)(kv_copy(k).wait_send)

        @pl.loop(0, heads_width // 128)
        def _(pair):
            for e in range(2):
                head = pair * 2 + e
                at = aligned(head, 64)
                r.att[at, :] = r.att[at, :] * (1.0 / r.run_sum[head])
                r.lse[head] = r.lse[head] + jnp.log2(r.run_sum[head])
            at = aligned(pair, 128)
            r.att_low[:, at] = r.att[at, :].T.astype(bf16)

    def feed_forward(wgu, g, gh, wdown):
        load_g = load(r.g_hbm, g)
        load_wdown = load(r.wdown_hbm, wdown)
        load_wout.wait()
        start_sum(0, None, lambda n: dot(r.att_low[...], r.wout[:, aligned(n, 256)]))
        if swap:
            swap_low.start()

        load_g.wait()
        load_wdown.wait()

        @pl.loop(0, units // 128)
        def _(b):
            at = aligned(b, 128)
            gh[:, at] = dot_t(g[...], wdown[at, :])

        finish_sum(0)
        load_x_own.wait()
        square = jnp.zeros((quarter, 1), f32)
        for c in range(chunks):
            at = slice(c * span, (c + 1) * span)
            part = r.own_fin[0, c] + r.x_own[:, at].astype(f32)
            r.resid[:, at] = part
            square = square + jnp.sum(part * part, -1, keepdims=True)
        inverse = lax.rsqrt(square / width + epsilon)
        r.x_n2[mine, :] = (r.resid[...] * inverse * r.gain_two[...]).astype(bf16)
        to_chip, to_core, onward = gather(5, r.x_n2.at[mine, :], r.x_n2)
        to_chip.start()
        to_core.start()

        def units_of(at, first, last):
            @pl.loop(first, last)
            def _(b):
                wide = dot(r.x_n2[at, :], wgu[:, aligned(b, 256)])
                gate, up = wide[:, :128], wide[:, 128:]
                grad = gh[at, aligned(b, 128)]
                sigmoid = 1.0 / (1.0 + jnp.exp(-gate))
                active = gate * sigmoid
                r.hid[at, aligned(b, 128)] = (active * up).astype(bf16)
                grad_gate = grad * up * (sigmoid * (1.0 + gate * (1.0 - sigmoid)))
                both = jnp.concatenate([grad_gate, grad * active], 1).astype(bf16)
                r.gg[at, aligned(b, 256)] = both

        first_at, second_at = aligned(chip, 2 * quarter), aligned(1 - chip, 2 * quarter)
        blocks = units // 128
        to_core.wait_recv()
        units_of(first_at, 0, blocks)
        if swap:
            for copy in swap_hid[0]:
                copy.start()
        to_chip.wait_recv()
        onward.start()
        onward.wait_recv()
        if swap:
            done = 0
            for copy, (at, size) in zip(swap_hid[1], hid_cuts, strict=True):
                units_of(second_at, done, (at + size) // 128)
                done = (at + size) // 128
                copy.start()
            for copy in (swap_n2, *swap_gg):
                copy.start()
        else:
            units_of(second_at, 0, blocks)
            store(r.x_n2, r.n2_out)
            store(r.hid, r.hid_out)
            store(r.gg, r.gg_out)
            store(r.att_low, r.low_out)
        for copy in (to_chip, to_core, onward):
            copy.wait_send()

        store_copy(0).wait()
        start_sum(0, None, lambda n: dot_t(r.gg[...], wgu[aligned(n, 256), :]))

    def first_half(wgu):
        bf = lambda *shape: pltpu.VMEM(shape, bf16)
        pl.run_scoped(
            functools.partial(attention, wgu),
            raw=bf(4, 128, 2, units),
            wq=bf(width, heads_width),
            wkv=bf(width, 128),
            keys=bf(2, rows, 128),
            vals_t=bf(64, rows),
            bias=pltpu.VMEM((rows, rows), f32),
        )
        pl.run_scoped(
            functools.partial(feed_forward, wgu),
            g=bf(rows, width),
            gh=pltpu.VMEM((rows, units), f32),
            wdown=bf(units, width),
        )

    load_wout = load(r.wout_hbm, r.wout)
    load_x_own = load(r.x_hbm.at[mine, :], r.x_own)
    load_g_own = load(r.g_hbm.at[mine, :], r.g_own)
    pl.run_scoped(first_half, pltpu.VMEM((width, 2 * units), bf16))

    def second_half(**scoped):
        vars(r).update(scoped)

        def tile_down(n):
            slot = turn_of(n, 3)
            return pltpu.make_async_copy(
                r.wdown_hbm.at[:, aligned(n, 256)], r.w_cols.at[slot], r.w_cols_sem.at[slot]
            )

        def tile_qkv(n):
            slot = turn_of(n, 3)
            at = aligned(n, 256)
            copies = (
                pltpu.make_async_copy(
                    r.wq_hbm.at[at], r.w_rows.at[slot, :, 0:heads_width], r.w_rows_sem.at[slot]
                ),
                pltpu.make_async_copy(
                    r.wkv_hbm.at[at],
                    r.w_rows.at[slot, :, heads_width : heads_width + 128],
                    r.w_kv_sem.at[slot],
                ),
            )
            return types.SimpleNamespace(
                start=lambda: [copy.start() for copy in copies],
                wait=lambda: [copy.wait() for copy in copies],
            )

        def back_through_norm(b, values, gain_ref, gain_row, emit):
            square = jnp.zeros((quarter, 1), f32)
            inner = jnp.zeros((quarter, 1), f32)
            for c in range(chunks):
                at = slice(c * span, (c + 1) * span)
                v = values[:, at].astype(f32)
                square = square + jnp.sum(v * v, -1, keepdims=True)
                inner = inner + jnp.sum(r.own_fin[b, c] * gain_ref[:, at] * v, -1, keepdims=True)
            inverse = lax.rsqrt(square / width + epsilon)
            slope = inner / width * (inverse * inverse * inverse)
            for c in range(chunks):
                at = slice(c * span, (c + 1) * span)
                v = values[:, at].astype(f32)
                dn = r.own_fin[b, c]
                r.gain_sum[0, gain_row : gain_row + 1, at] = jnp.sum(
                    dn * v * inverse, 0, keepdims=True
                )
                emit(at, inverse * dn * gain_ref[:, at] - v * slope)

        if swap:
            is_end = (place == 0) | (place == 3)
            is_mid = jnp.logical_not(is_end)
            beside = place + 1 - 2 * lax.rem(place, 2)
            low_side = place < 2
            io_mate, across_mate = {"context": beside}, {"context": 3 - place}
            swap_gqkv = swap_copy(r.gqkv, r.gqkv_o)
            plan = []
            for i, (at, size) in enumerate(hid_cuts):
                cut = (r.g_hbm.at[:, mine_cols], r.g_o) if i == 0 else None
                plan.append(
                    (cut, r.hid.at[:, at : at + size], r.hid_o.at[i], size,
                     r.dwdown_out.at[:, at : at + size])
                )
            for i, (at, size) in enumerate(gg_cuts):
                cut = (r.x_n2.at[:, mine_cols], r.n2_o) if i == 0 else None
                plan.append(
                    (cut, r.gg.at[:, at : at + size], r.gg_o.at[i], size,
                     r.dgu_out.at[:, at : at + size])
                )
            cut = (r.n1_gb.at[:, mine_cols], r.gb_o)
            plan.append((cut, r.att_low, r.att_o, heads_width, r.dwout_out))
            cut = (r.n1_out.at[:, mine_cols], r.n1_o)
            plan.append((cut, r.gqkv, r.gqkv_o, r.gqkv.shape[1], r.dwqkv_out))
            sets = r.stage.shape[0]
            last = len(plan) - 1
            first_gg = len(hid_cuts)

            def cut_loads(u):
                own, other = plan[u][0]
                return (
                    pltpu.make_async_copy(own, r.cut.at[0:rows], r.cut_sem.at[0]),
                    pltpu.make_async_copy(other, r.cut.at[rows : 2 * rows], r.cut_sem.at[1]),
                )

            def piece(ref, s, j, u):
                return ref.at[s, j, :, 0 : plan[u][3]]

            def line_copy(u, j, slot, mate):
                s = u % sets
                return remote(
                    piece(r.stage, s, j, u), piece(r.got, s, slot, u), r.line_send.at[s, j],
                    r.line_recv.at[s, slot], mate,
                )

            def result(u):
                return pltpu.make_async_copy(
                    r.sums.at[u % sets, :, 0 : plan[u][3]], plan[u][4], r.sums_sem.at[u % sets]
                )

            def prepare(u):
                s = u % sets
                own, other, width_u = plan[u][1], plan[u][2], plan[u][3]
                if u >= sets:
                    for j in range(3):
                        line_copy(u - sets, j, 0, io_mate).wait_send()
                    result(u - sets).wait()
                    pl.when(is_end)(lambda: pl.semaphore_wait(r.io_credit, 1))
                if plan[u][0] is not None:
                    for copy in cut_loads(u):
                        copy.wait()

                @pl.loop(0, 4)
                def _(j):
                    chunk = jnp.where(
                        j == 0,
                        jnp.where(low_side, 3, 0),
                        jnp.where(
                            j == 1, jnp.where(low_side, 2, 1), jnp.where(j == 2, beside, place)
                        ),
                    )
                    r.turned[...] = r.cut[:, aligned(chunk, 256)].astype(f32).T.astype(bf16)

                    def block(at):
                        term = dot(r.turned[:, 0:rows], own[:, at]) + dot(
                            r.turned[:, rows : 2 * rows], other[:, at]
                        )

                        @pl.when(j < 3)
                        def _():
                            r.stage[s, j, :, at] = term.astype(bf16)

                        @pl.when(j == 3)
                        def _():
                            r.sums[s, :, at] = term

                    @pl.loop(0, width_u // 256)
                    def _(tile):
                        block(aligned(tile, 256))

                    if width_u % 256:
                        block(slice(width_u - width_u % 256, width_u))

                    @pl.when((j < 3) & is_end)
                    def _():
                        line_copy(u, j, j, io_mate).start()

            def add_in(u, j, slot):
                width_u, s = plan[u][3], u % sets
                line_copy(u, 0, slot, io_mate).wait_recv()

                @pl.loop(0, 4)
                def _(i):
                    at = aligned(i, 64)
                    total = r.stage[s, j, at, 0:width_u].astype(f32)
                    total = total + r.got[s, slot, at, 0:width_u].astype(f32)
                    r.stage[s, j, at, 0:width_u] = total.astype(bf16)

            def pass_on(u, step):
                @pl.when(is_mid)
                def _():
                    if step < 2:
                        add_in(u, step, step)
                        if u >= sets and step == 0:
                            pl.semaphore_wait(r.across_credit, 1)
                        line_copy(u, step, 3 + step, across_mate).start()
                    else:
                        add_in(u, 2, 3)
                        if u >= sets:
                            pl.semaphore_wait(r.io_credit, 1)
                        line_copy(u, 2, 0, io_mate).start()

            def complete(u):
                width_u, s = plan[u][3], u % sets

                def take(slots):
                    for slot in slots:
                        line_copy(u, 0, slot, io_mate).wait_recv()

                    @pl.loop(0, 4)
                    def _(i):
                        at = aligned(i, 64)
                        total = r.sums[s, at, 0:width_u]
                        for slot in slots:
                            total = total + r.got[s, slot, at, 0:width_u].astype(f32)
                        r.sums[s, at, 0:width_u] = total

                @pl.when(is_end)
                def _():
                    take((0,))

                @pl.when(is_mid)
                def _():
                    take((2, 4))

                result(u).start()
                if u + sets <= last:
                    pl.semaphore_signal(r.io_credit, inc=1, device_id=io_mate, device_id_type=MESH)

                    @pl.when(is_mid)
                    def _():
                        pl.semaphore_signal(
                            r.across_credit, inc=1, device_id=across_mate, device_id_type=MESH
                        )

            swap_g.wait_recv()
            for copy in cut_loads(0):
                copy.start()
        for n in range(3):
            tile_down(n).start()
            tile_qkv(n).start()
        r.gain_sum[...] = jnp.zeros_like(r.gain_sum)

        if swap:
            swap_hid[0][0].wait_recv()
            swap_hid[1][0].wait_recv()
            prepare(0)
        finish_sum(0)
        load_g_own.wait()
        for i in range(1, len(stores)):
            store_copy(i).wait()

        def keep_resid(at, grad):
            total = r.g_own[:, at].astype(f32) + grad
            r.grad_resid[:, at] = total
            r.n1_gb[mine, at] = total.astype(bf16)

        back_through_norm(0, r.resid, r.gain_two, 1, keep_resid)
        gb_chip, gb_core, gb_onward = gather(0, r.n1_gb.at[mine, :], r.n1_gb)
        gb_chip.start()
        gb_core.start()
        if swap:
            swap_gb.start()
        start_sum(1, tile_down, lambda n: dot(r.hid[...], r.w_cols[turn_of(n, 3)]), False)
        for c in range(chunks):
            x_copy(1, c).start()
        if swap:
            pass_on(0, 0)
            swap_hid[0][1].wait_recv()
            swap_hid[1][1].wait_recv()
            prepare(1)
            pass_on(0, 1)
        gb_chip.wait_recv()
        gb_onward.start()
        if swap:
            swap_n2.wait_recv()
            n2_chip, n2_core, n2_onward = gather(3, r.n2_o.at[mine, :], r.n2_o)
            n2_chip.start()
            n2_core.start()
        gb_core.wait_recv()
        gb_onward.wait_recv()
        if swap:
            swap_low.wait_recv()
            late = pltpu.make_async_copy(r.low_o, r.att_o, r.late_sem)
            late.start()
        else:
            late = pltpu.make_async_copy(r.n1_gb, r.gb_out, r.late_sem)
            late.start()

        for i in range(heads_width // 256):
            at = slice(i * 256, i * 256 + 256)
            r.ga[:, at] = dot_t(r.n1_gb[...], r.wout[at, :]).astype(bf16)

        @pl.loop(0, heads_width // 128)
        def _(pair):
            at = aligned(pair, 128)
            product = r.ga[:, at].astype(f32).T * r.att[at, :]
            for e in range(2):
                r.delta[pair * 2 + e] = jnp.sum(product[64 * e : 64 * e + 64], 0, keepdims=True)

        if swap:
            pass_on(0, 2)

        r.dq[...] = jnp.zeros_like(r.dq)

        def back_block(k, first):
            mask(r.bias, k, first)
            block = r.kv[k].astype(f32)
            rolled = pltpu.roll(block, 64, 1)
            pad_keys(r.keys, block)
            r.vals[0] = jnp.where(key_lane, rolled, 0.0).astype(bf16)
            r.vals[1] = jnp.where(key_lane, 0.0, block).astype(bf16)
            r.keys_t[...] = block.T[:64].astype(bf16)
            r.dk[...] = jnp.zeros_like(r.dk)
            r.dv[...] = jnp.zeros_like(r.dv)

            @pl.loop(0, heads_width // 128)
            def _(pair):
                pair_q = r.q[:, aligned(pair, 128)]
                pair_ga = r.ga[:, aligned(pair, 128)]
                for e in range(2):
                    head = pair * 2 + e
                    probs = jnp.exp2(dot_t(r.keys[e], pair_q) + r.bias[...] - r.lse[head])
                    grad_probs = dot_t(r.vals[e], pair_ga)
                    grad_scores = (probs * (grad_probs - r.delta[head])).astype(bf16)
                    r.dv[e] += dot(probs.astype(bf16), pair_ga)
                    r.dk[e] += dot(grad_scores, pair_q)
                    r.dq[aligned(head, 64), :] += dot(r.keys_t[...], grad_scores)

            return jnp.where(
                key_lane,
                (r.dk[0] + pltpu.roll(r.dk[1], 64, 1)) * (1.0 / log2_e),
                r.dv[1] + pltpu.roll(r.dv[0], 64, 1),
            )

        def dkv_copy(k, mate):
            return remote(
                r.stage_kv.at[k], r.got_kv.at[k], r.dkv_send.at[k], r.dkv_recv.at[k],
                {"context": mate},
            )

        @pl.loop(0, place)
        def _(i):
            k = place - i
            r.stage_kv[k] = back_block(k, False).astype(bf16)
            dkv_copy(k, i).start()

        r.dkv[...] = back_block(0, True)
        if swap:
            pass_on(1, 0)
            pass_on(1, 1)
            n2_chip.wait_recv()
            n2_onward.start()
            n2_core.wait_recv()
            n2_onward.wait_recv()
            for copy in cut_loads(first_gg):
                copy.start()
            swap_gg[0].wait_recv()
            prepare(2)
            complete(0)

        @pl.loop(0, heads_width // 128)
        def _(pair):
            at = aligned(pair, 128)
            turned = turn(r.dq[at, :].T * 0.125, r.cos[...], -r.sin[...])
            r.gqkv[:, at] = turned.astype(bf16)

        for k in (1, 2, 3):

            @pl.when(place + k < 4)
            def _():
                dkv_copy(k, 0).wait_recv()
                r.dkv[...] += r.got_kv[k].astype(f32)

        r.gqkv[:, heads_width : heads_width + 128] = turn(
            r.dkv[...], jnp.where(key_lane, r.cos[...], 1.0), jnp.where(key_lane, -r.sin[...], 0.0)
        ).astype(bf16)
        if swap:
            swap_gqkv.start()
            swap_n1.start()
            pass_on(1, 2)
        else:
            gqkv_store = pltpu.make_async_copy(r.gqkv, r.gqkv_out, r.cut_sem.at[1])
            gqkv_store.start()

        start_sum(0, tile_qkv, lambda n: dot_t(r.gqkv[...], r.w_rows[turn_of(n, 3)]))
        if swap:
            swap_gg[1].wait_recv()
            prepare(3)
            complete(1)
            pass_on(2, 0)

        finish_sum(0)

        def keep_tokens(at, grad):
            r.tokens_own[:, at] = (r.grad_resid[:, at] + grad).astype(bf16)

        back_through_norm(0, r.x_own, r.gain_one, 0, keep_tokens)
        tokens_chip, tokens_core, tokens_onward = gather(2, r.tokens_own, r.tokens_out)
        tokens_store = pltpu.make_async_copy(
            r.tokens_own, r.tokens_out.at[mine, :], r.out_sem.at[1]
        )
        for copy in (tokens_chip, tokens_core, tokens_store):
            copy.start()
        if swap:
            pass_on(2, 1)
            pass_on(2, 2)
            swap_gg[2].wait_recv()
            prepare(4)

        finish_sum(1)
        for c in range(chunks):
            at = slice(c * span, (c + 1) * span)
            r.mixed_own[:, at] = (r.resid[:, at] + r.own_fin[1, c]).astype(bf16)
        mixed_chip, mixed_core, mixed_onward = gather(1, r.mixed_own, r.mixed_out)
        mixed_store = pltpu.make_async_copy(r.mixed_own, r.mixed_out.at[mine, :], r.out_sem.at[0])
        for copy in (mixed_chip, mixed_core, mixed_store):
            copy.start()
        if swap:
            complete(2)
            pass_on(3, 0)
            swap_gg[3].wait_recv()
            prepare(5)
            swap_gb.wait_recv()
            gbo_chip, gbo_core, gbo_onward = gather(4, r.gb_o.at[mine, :], r.gb_o)
            gbo_chip.start()
            gbo_core.start()
            pass_on(3, 1)
            pass_on(3, 2)

        for i, mate in enumerate((core_mate, chip_mate)):
            copy = remote(
                r.gain_sum.at[i], r.gain_got.at[i], r.gain_send.at[i], r.gain_recv.at[i], mate
            )
            copy.start()
            copy.wait()
            r.gain_sum[i + 1] = r.gain_sum[i] + r.gain_got[i]
        if swap:
            copy = remote(
                r.gain_sum.at[2, :, theirs_cols], r.gain_half.at[0], r.gain_send.at[2],
                r.gain_recv.at[2], dp_mate,
            )
            copy.start()
            copy.wait()
            r.gain_half[1] = r.gain_sum[2, :, mine_cols] + r.gain_half[0]
            part = half // 4
            pieces = [
                remote(
                    r.gain_half.at[1, :, aligned(lax.rem(place + k, 4), part)],
                    r.gain_piece.at[k], r.gain_send.at[2 + k], r.gain_recv.at[2 + k],
                    {"context": lax.rem(place + k, 4)},
                )
                for k in (1, 2, 3)
            ]
            for copy in pieces:
                copy.start()
            complete(3)
        else:
            r.gains_out[...] = r.gain_sum[2]
        tokens_chip.wait_recv()
        tokens_onward.start()
        mixed_chip.wait_recv()
        mixed_onward.start()
        if swap:
            gbo_chip.wait_recv()
            gbo_onward.start()
            gbo_core.wait_recv()
            gbo_onward.wait_recv()
            for copy in cut_loads(last - 1):
                copy.start()
            late.wait()
            prepare(6)
            swap_n1.wait_recv()
            for copy in cut_loads(last):
                copy.start()
            for step in range(3):
                pass_on(4, step)
            complete(4)
            swap_gqkv.wait_recv()
            prepare(7)
            for u in (5, 6, 7):
                for step in range(3):
                    pass_on(u, step)
                complete(u)
            for copy in pieces:
                copy.wait()
            r.gains_out[...] = (
                r.gain_half[1, :, aligned(place, part)]
                + r.gain_piece[1]
                + r.gain_piece[2]
                + r.gain_piece[3]
            )

        for copy in (mixed_core, mixed_onward, tokens_core, tokens_onward):
            copy.wait_recv()
        for copy in (
            gb_chip, gb_core, gb_onward, mixed_chip, mixed_core, mixed_onward, tokens_chip,
            tokens_core, tokens_onward,
        ):
            copy.wait_send()
        mixed_store.wait()
        tokens_store.wait()
        for k in (1, 2, 3):
            pl.when(place >= k)(dkv_copy(k, 0).wait_send)
        if swap:
            for copy in (
                *swaps, n2_chip, n2_core, n2_onward, gbo_chip, gbo_core, gbo_onward
            ):
                copy.wait_send()
            for u in range(last + 1 - sets, last + 1):
                for j in range(3):
                    line_copy(u, j, 0, io_mate).wait_send()
                result(u).wait()
        else:
            late.wait()
            gqkv_store.wait()

    bf = lambda *shape: pltpu.VMEM(shape, bf16)
    fl = lambda *shape: pltpu.VMEM(shape, f32)
    qkv = heads_width + 128
    scoped = {
        "w_rows": bf(3, 256, qkv),
        "w_cols": bf(3, units, 256),
        "bias": fl(rows, rows),
        "ga": bf(rows, heads_width),
        "delta": fl(heads_width // HD, 1, rows),
        "dq": fl(heads_width, rows),
        "keys": bf(2, rows, 128),
        "vals": bf(2, rows, 128),
        "keys_t": bf(HD, rows),
        "dk": fl(2, rows, 128),
        "dv": fl(2, rows, 128),
        "dkv": fl(rows, 128),
        "stage_kv": bf(4, rows, 128),
        "gqkv": bf(rows, qkv),
        "grad_resid": fl(quarter, width),
        "mixed_own": bf(quarter, width),
        "tokens_own": bf(quarter, width),
    }
    if swap:
        scoped |= {
            "att_o": bf(rows, heads_width),
            "cut": bf(2 * rows, width // 2),
            "turned": bf(256, 2 * rows),
            "stage": bf(r.got.shape[0], 3, width // 8, lead),
            "sums": fl(r.got.shape[0], width // 8, lead),
        }
    pl.run_scoped(second_half, **scoped)


def layer(swap, inputs, rows, width, units, heads):
    bf16, f32 = jnp.bfloat16, jnp.float32
    quarter = rows // 4
    chunks = 4
    span = width // chunks
    wide = heads * HD
    qkv = wide + 2 * HD
    lead, sets = 768, 3
    outs = {
        "mixed_out": ((rows, width), bf16),
        "tokens_out": ((rows, width), bf16),
        "gains_out": ((8, width // 8 if swap else width), f32),
        "n1_out": ((rows, width), bf16),
    }
    if swap:
        outs |= {
            "dwdown_out": ((width // 8, units), f32),
            "dgu_out": ((width // 8, 2 * units), f32),
            "dwout_out": ((width // 8, wide), f32),
            "dwqkv_out": ((width // 8, qkv), f32),
            "g_o": ((rows, width // 2), bf16),
            "low_o": ((rows, wide), bf16),
            "n2_o": ((rows, width // 2), bf16),
            "gb_o": ((rows, width // 2), bf16),
            "n1_o": ((rows, width // 2), bf16),
        }
    else:
        outs |= {
            "gb_out": ((rows, width), bf16),
            "gqkv_out": ((rows, qkv), bf16),
            "n2_out": ((rows, width), bf16),
            "hid_out": ((rows, units), bf16),
            "gg_out": ((rows, 2 * units), bf16),
            "low_out": ((rows, wide), bf16),
        }
    scratch = {
        "x_n2": ((rows, width), bf16),
        "n1_gb": ((rows, width), bf16),
        "wout": ((wide, width), bf16),
        "q": ((rows, wide), bf16),
        "kv": ((4, rows, 2 * HD), bf16),
        "att": ((wide, rows), f32),
        "att_low": ((rows, wide), bf16),
        "lse": ((heads, 1, rows), f32),
        "run_sum": ((heads, 1, rows), f32),
        "cos": ((rows, 2 * HD), f32),
        "sin": ((rows, 2 * HD), f32),
        "resid": ((quarter, width), f32),
        "g_own": ((quarter, width), bf16),
        "x_own": ((quarter, width), bf16),
        "hid": ((rows, units), bf16),
        "gg": ((rows, 2 * units), bf16),
        "tmp": ((rows, 256), f32),
        "stage_core": ((2, chunks, 2, quarter, span), bf16),
        "got_core": ((2, chunks, 2, quarter, span), bf16),
        "own_fwd": ((chunks, quarter, span), f32),
        "own_fin": ((2, chunks, quarter, span), f32),
        "stage_x": ((2, chunks, quarter, span), bf16),
        "got_x": ((2, chunks, quarter, span), bf16),
        "got_kv": ((4, rows, 2 * HD), bf16),
        "gain_sum": ((3, 8, width), f32),
        "gain_got": ((2, 8, width), f32),
    }
    if swap:
        scratch |= {
            "hid_o": ((-(-units // lead), rows, lead), bf16),
            "gg_o": ((-(-2 * units // lead), rows, lead), bf16),
            "gqkv_o": ((rows, qkv), bf16),
            "got": ((sets, 5, width // 8, lead), bf16),
            "gain_half": ((2, 8, width // 2), f32),
            "gain_piece": ((4, 8, width // 8), f32),
        }
    sems = {
        "load_sem": (8,),
        "store_sem": (5,),
        "raw_sem": (4,),
        "w_rows_sem": (3,),
        "w_cols_sem": (3,),
        "w_kv_sem": (3,),
        "core_send": (2, chunks),
        "core_recv": (2, chunks),
        "x_send": (2, chunks),
        "x_recv": (2, chunks),
        "ag_send": (6, 3),
        "ag_recv": (6, 3),
        "kv_send": (4,),
        "kv_recv": (4,),
        "dkv_send": (4,),
        "dkv_recv": (4,),
        "gain_send": (6,),
        "gain_recv": (6,),
        "out_sem": (2,),
        "cut_sem": (2,),
        "late_sem": (),
    }
    if swap:
        sems |= {
            "dp_send": (16,),
            "dp_recv": (16,),
            "line_send": (sets, 3),
            "line_recv": (sets, 5),
            "sums_sem": (sets,),
        }
    credits = ["io_credit", "across_credit"] if swap else []
    names = [*inputs, *outs, *scratch, *sems, *credits]
    anywhere = pl.BlockSpec(memory_space=pl.ANY)
    inside = pl.BlockSpec(memory_space=pltpu.VMEM)
    results = pl.pallas_call(
        functools.partial(layer_kernel, names, swap),
        out_shape=[jax.ShapeDtypeStruct(*out) for out in outs.values()],
        in_specs=[anywhere if name.endswith("_hbm") else inside for name in inputs],
        out_specs=[inside if name == "gains_out" else anywhere for name in outs],
        scratch_shapes=[
            *(pltpu.VMEM(*shape) for shape in scratch.values()),
            *(pltpu.SemaphoreType.DMA(shape) for shape in sems.values()),
            *(pltpu.SemaphoreType.REGULAR for _ in credits),
        ],
        compiler_params=pltpu.CompilerParams(
            collective_id=0, has_side_effects=True, vmem_limit_bytes=63 * MIB
        ),
        name="layer",
    )(*inputs.values())
    return dict(zip(outs, results, strict=True))


def finish_kernel(
    down_hbm, gateup_hbm, out_hbm, qkv_hbm, tokens_hbm, mixed_hbm, gains,
    down_o, gateup_o, out_o, q_o, kv_o, tokens_o, mixed_o, gain_one_o, gain_two_o,
    down, gateup, out, qkv, tokens, mixed, down_t, gateup_t, out_t, kv_t, tokens_t,
    load_sem, store_sem,
):
    wide = q_o.shape[1]
    parts = 4
    loads, stores = [], []

    def load(src, dst):
        copy = pltpu.make_async_copy(src, dst, load_sem.at[len(loads)])
        copy.start()
        loads.append(copy)
        return copy

    def store(src, dst):
        copy = pltpu.make_async_copy(src, dst, store_sem.at[len(stores)])
        copy.start()
        stores.append(copy)

    def piece(ref, i):
        size = ref.shape[0] // parts
        return ref.at[i * size : (i + 1) * size]

    gain_one_o[...] = gains[0:1, :]
    gain_two_o[...] = gains[1:2, :]
    token_loads = [load(piece(tokens_hbm, i), piece(tokens, i)) for i in range(parts)]
    gateup_loads = [load(piece(gateup_hbm, i), piece(gateup, i)) for i in range(parts)]
    load_mixed = load(mixed_hbm, mixed)
    load_down = load(down_hbm, down)
    load_qkv = load(qkv_hbm, qkv)
    load_out = load(out_hbm, out)
    for i in range(parts):
        token_loads[i].wait()
        piece(tokens_t, i)[...] = piece(tokens, i)[...].astype(jnp.float32)
        store(piece(tokens_t, i), piece(tokens_o, i))
    for i in range(parts):
        gateup_loads[i].wait()
        values, target = piece(gateup, i), piece(gateup_t, i)
        for b in range(gateup.shape[1] // 256):
            at = slice(b * 128, b * 128 + 128)
            target[:, 0, at] = values[:, b * 256 : b * 256 + 128]
            target[:, 1, at] = values[:, b * 256 + 128 : b * 256 + 256]
        store(target, piece(gateup_o, i))
    load_mixed.wait()
    store(mixed, mixed_o)
    load_down.wait()
    for i in range(down.shape[1] // 128):
        at = slice(i * 128, i * 128 + 128)
        down_t[at, :] = down[:, at].T
    store(down_t, down_o)
    load_qkv.wait()
    store(qkv.at[:, 0:wide], q_o)
    kv_t[:, 0, :] = qkv[:, wide:]
    store(kv_t, kv_o)
    load_out.wait()
    for i in range(wide // 128):
        at = slice(i * 128, i * 128 + 128)
        out_t[at, :] = out[:, at].T
    store(out_t, out_o)
    for copy in stores:
        copy.wait()


def finish(down, gateup, out, qkv, tokens, mixed, gains):
    depth, units = down.shape
    wide = out.shape[1]
    rows, width = tokens.shape
    bf16, f32 = jnp.bfloat16, jnp.float32
    outs = [
        ((units, depth), f32),
        ((depth, 2, units), f32),
        ((wide, depth), f32),
        ((depth, wide), f32),
        ((depth, 1, 2 * HD), f32),
        ((rows, width), f32),
        ((rows, width), bf16),
        ((1, depth), f32),
        ((1, depth), f32),
    ]
    scratch = [
        *((array.shape, array.dtype) for array in (down, gateup, out, qkv, tokens, mixed)),
        *outs[:3],
        *outs[4:6],
    ]
    anywhere = pl.BlockSpec(memory_space=pl.ANY)
    inside = pl.BlockSpec(memory_space=pltpu.VMEM)
    return pl.pallas_call(
        finish_kernel,
        out_shape=[jax.ShapeDtypeStruct(*entry) for entry in outs],
        in_specs=[*[anywhere] * 6, inside],
        out_specs=[*[anywhere] * 7, inside, inside],
        scratch_shapes=[
            *(pltpu.VMEM(*entry) for entry in scratch),
            pltpu.SemaphoreType.DMA((12,)),
            pltpu.SemaphoreType.DMA((13,)),
        ],
        compiler_params=pltpu.CompilerParams(vmem_limit_bytes=62 * MIB),
        name="finish",
    )(down, gateup, out, qkv, tokens, mixed, gains)


def pick(array, index, axis):
    return lax.dynamic_index_in_dim(array, index, axis, keepdims=False)


def line_sum(part):
    place = lax.axis_index("context")
    order = jnp.array([[3, 2, 1, 0], [3, 2, 0, 1], [0, 1, 3, 2], [0, 1, 2, 3]], jnp.int32)[place]
    first, second, third, own = (part(order[i]) for i in range(4))

    def inward(array):
        return lax.ppermute(array.astype(jnp.bfloat16), "context", [(0, 1), (3, 2)])

    def across(array):
        return lax.ppermute(array.astype(jnp.bfloat16), "context", [(1, 2), (2, 1)])

    def outward(array):
        return lax.ppermute(array.astype(jnp.bfloat16), "context", [(1, 0), (2, 3)])

    in_one, in_two, in_three = inward(first), inward(second), inward(third)
    over_two = across(first + in_one.astype(jnp.float32))
    over_three = across(second + in_two.astype(jnp.float32))
    out_three = outward(third + over_two.astype(jnp.float32))
    return (
        own
        + in_three.astype(jnp.float32)
        + over_three.astype(jnp.float32)
        + out_three.astype(jnp.float32)
    )


def weight_grad(left, right, axis):
    whole = lax.dot_general(
        left, right, (((0,), (0,)), ((), ())), preferred_element_type=jnp.float32
    )
    mine = lax.psum_scatter(
        whole.astype(jnp.bfloat16), "dp", scatter_dimension=axis, tiled=True
    )
    step = mine.shape[axis] // 4
    return line_sum(
        lambda chunk: lax.dynamic_slice_in_dim(mine, chunk * step, step, axis).astype(jnp.float32)
    )


def shards(
    tokens, segments, gain_one, w_query, w_keyval, w_out, gain_two, w_gateup, w_down, cotangent
):
    num_seqs, tok_count, model_width = tokens.shape
    heads_kv = w_keyval.shape[1]
    width_q = w_query.shape[1]
    units = w_down.shape[0]
    swap = lax.axis_size("dp") == 2
    freqs = 10000.0 ** (-(np.arange(HD // 2, dtype=np.float32) * 2.0) / HD)
    g = cotangent.reshape(tok_count, model_width)
    inputs = {
        "seg": segments,
        "freqs": jnp.asarray(freqs.astype(np.float32)[:, None]),
        "gain_one": gain_one[None],
        "gain_two": gain_two[None],
        "x_hbm": tokens.reshape(tok_count, model_width),
        "g_hbm": g,
        "wq_hbm": w_query,
        "wkv_hbm": w_keyval.reshape(model_width, 2 * HD),
        "wout_hbm": w_out,
        "wgateup_hbm": w_gateup,
        "wdown_hbm": w_down,
    }
    out = layer(swap, inputs, tok_count, model_width, units, width_q // HD)
    if swap:
        sent_wdown, sent_gateup, sent_wout, sent_wq, sent_wkv, grad_tokens, mixed, *gains = finish(
            *(out[name] for name in ("dwdown_out", "dgu_out", "dwout_out", "dwqkv_out")),
            *(out[name] for name in ("tokens_out", "mixed_out", "gains_out")),
        )
    else:
        gains = lax.psum_scatter(
            out["gains_out"], ("dp", "context"), scatter_dimension=1, tiled=True
        )
        sent_wdown = weight_grad(out["hid_out"], g, 1)
        sent_gateup = weight_grad(out["n2_out"], out["gg_out"], 0)
        sent_wout = weight_grad(out["low_out"], out["gb_out"], 1)
        sent_wqkv = weight_grad(out["n1_out"], out["gqkv_out"], 0)
        sent_wq, sent_wkv = sent_wqkv[:, :width_q], sent_wqkv[:, width_q:]
        sent_gateup = sent_gateup.reshape(-1, units // 128, 2, 128).transpose(0, 2, 1, 3)
        grad_tokens, mixed = out["tokens_out"].astype(jnp.float32), out["mixed_out"]
    return (
        mixed.reshape(tokens.shape),
        grad_tokens.reshape(tokens.shape),
        gains[0].reshape(-1),
        sent_wq,
        sent_wkv.reshape(-1, heads_kv, 2 * HD),
        sent_wout,
        gains[1].reshape(-1),
        sent_gateup.reshape(-1, 2, units),
        sent_wdown,
    )


def solution(mesh):
    return jax.shard_map(
        shards,
        mesh=mesh,
        in_specs=(
            P("dp", "context", None),
            P("dp", "context"),
            P(),
            P(None, "tensor"),
            P(None, "tensor", None),
            P("tensor", None),
            P(),
            P(None, None, "tensor"),
            P("tensor", None),
            P("dp", "context", None),
        ),
        out_specs=(
            P("dp", "context", None),
            P("dp", "context", None),
            P(("dp", "context")),
            P(("dp", "context"), "tensor"),
            P(("dp", "context"), "tensor", None),
            P("tensor", ("dp", "context")),
            P(("dp", "context")),
            P(("dp", "context"), None, "tensor"),
            P("tensor", ("dp", "context")),
        ),
        check_vma=False,
    )
```

```python
import functools
import types

import jax
import jax.numpy as jnp
import numpy as np
from jax import lax
from jax.experimental import pallas as pl
from jax.experimental.pallas import tpu as pltpu
from jax.sharding import PartitionSpec as P

HD = 64


epsilon = 1e-05
neg_large = -1e30


MESH = pl.DeviceIdType.MESH
MIB = 1 << 20
log2_e = 1.4426950408889634


def dot(left, right):
    return jnp.dot(left, right, preferred_element_type=jnp.float32)


def dot_t(left, right):
    return lax.dot_general(left, right, (((1,), (1,)), ((), ())), preferred_element_type=jnp.float32)


def lanes(shape):
    return lax.broadcasted_iota(jnp.int32, shape, len(shape) - 1)


def turn_of(n, size):
    return n % size if isinstance(n, int) else lax.rem(n, size)


def aligned(index, size):
    if isinstance(index, int):
        return pl.ds(index * size, size)
    return pl.ds(pl.multiple_of(index * size, size), size)


def turn(values, cosine, sine):
    low_half = lax.rem(lanes(values.shape), 64) < 32
    swapped = jnp.where(low_half, pltpu.roll(values, 96, 1), pltpu.roll(values, 32, 1))
    return values * cosine + swapped * sine


def cos_sin(phase):
    count = jnp.floor(phase * 0.6366197723675814 + 0.5)
    rest = phase - count * 1.5703125
    rest = rest - count * 0.0004837512969970703
    rest = rest - count * 7.549789954e-08
    square = rest * rest
    sine = rest + rest * square * (
        -0.16666666666 + square * (0.0083333333333 + square * -0.0001984126984)
    )
    cosine = 1.0 + square * (
        -0.5 + square * (0.041666666666 + square * (-0.0013888888889 + square * 2.48015873e-05))
    )
    place = count - 4.0 * jnp.floor(count * 0.25)
    odd = (place == 1.0) | (place == 3.0)
    first, second = jnp.where(odd, sine, cosine), jnp.where(odd, cosine, sine)
    return (
        jnp.where((place == 1.0) | (place == 2.0), -first, first),
        jnp.where(place >= 2.0, -second, second),
    )


def layer_kernel(names, swap, *refs):
    r = types.SimpleNamespace(**dict(zip(names, refs, strict=True)))
    rows, width = r.x_n2.shape
    quarter = rows // 4
    units = r.hid.shape[1]
    heads_width = r.q.shape[1]
    f32, bf16 = jnp.float32, jnp.bfloat16
    tensor = lax.axis_index("tensor")
    place = lax.axis_index("context")
    core, chip = lax.rem(tensor, 2), lax.div(tensor, 2)
    core_mate = {"tensor": chip * 2 + 1 - core}
    chip_mate = {"tensor": (1 - chip) * 2 + core}
    mates = [core_mate, chip_mate, *({"context": lax.rem(place + k, 4)} for k in (1, 2, 3))]
    if swap:
        side = lax.axis_index("dp")
        dp_mate = {"dp": 1 - side}
        mates.append(dp_mate)
    mine = aligned(tensor, quarter)
    key_lane = lanes((rows, 128)) < 64
    qkv = heads_width + 128
    bf = lambda *shape: pltpu.VMEM(shape, bf16)
    fl = lambda *shape: pltpu.VMEM(shape, f32)

    barrier = pltpu.get_barrier_semaphore()
    for mate in mates:
        pl.semaphore_signal(barrier, inc=1, device_id=mate, device_id_type=MESH)

    def remote(src, dst, send, recv, mate):
        return pltpu.make_async_remote_copy(
            src_ref=src, dst_ref=dst, send_sem=send, recv_sem=recv, device_id=mate,
            device_id_type=MESH,
        )

    loads, stores = [], []

    def load(src, dst):
        copy = pltpu.make_async_copy(src, dst, r.load_sem.at[len(loads)])
        loads.append(copy)
        copy.start()
        return copy

    def store_copy(i):
        return pltpu.make_async_copy(*stores[i], r.store_sem.at[i])

    def store(src, dst):
        stores.append((src, dst))
        store_copy(len(stores) - 1).start()

    swaps = []

    def swap_copy(src, dst):
        i = len(swaps)
        swaps.append(remote(src, dst, r.dp_send.at[i], r.dp_recv.at[i], dp_mate))
        return swaps[i]

    if swap:
        half = width // 2
        theirs_cols, mine_cols = aligned(1 - side, half), aligned(side, half)
        swap_n1 = swap_copy(r.n1_gb.at[:, theirs_cols], r.n1_o)
        swap_low = swap_copy(r.att_low, r.low_o)
        swap_gb = swap_copy(r.n1_gb.at[:, theirs_cols], r.gb_o)
        swap_gqkv = swap_copy(r.gqkv, r.gqkv_o)

    low_side = place < 2
    beside = place + 1 - 2 * lax.rem(place, 2)
    peers = (beside, jnp.where(low_side, 2, 1), jnp.where(low_side, 3, 0))
    other_quarter = aligned(chip_mate["tensor"], quarter)

    def line_parts(i):
        return (mine, other_quarter) if i == 0 else (mine,)

    def line_sent(a, i, part):
        src, dst = ((r.g_hbm, r.g_z), (r.n2_z.at[place], r.n2_z))[a]
        step = lax.rem(peers[i] - place + 4, 4)
        at = line_parts(i)[part]
        return remote(
            src.at[at, :], dst.at[place, at, :], r.line_send.at[a, step, part],
            r.line_recv.at[a, step, part], {"context": peers[i]},
        )

    def line_got(a, i, part):
        dst = (r.g_z, r.n2_z)[a].at[peers[i], line_parts(i)[part], :]
        step = lax.rem(place - peers[i] + 4, 4)
        return remote(
            dst, dst, r.line_send.at[a, step, part], r.line_recv.at[a, step, part],
            {"context": peers[i]},
        )

    def spread(a, i):
        block = (r.g_z, r.n2_z)[a].at[peers[i]]
        slot = 4 + a * 3 + i
        if i > 0:
            return gather(slot, block.at[mine, :], block)
        return tuple(
            remote(
                block.at[at, :], block.at[at, :], r.ag_send.at[slot, part],
                r.ag_recv.at[slot, part], core_mate,
            )
            for part, at in enumerate(line_parts(0))
        )

    def spread_start(a, i):
        copies = spread(a, i)
        for part in range(len(line_parts(i))):
            line_got(a, i, part).wait_recv()
        for copy in copies[:2]:
            copy.start()

    def spread_onward(a, i):
        if i > 0:
            copies = spread(a, i)
            copies[0].wait_recv()
            copies[2].start()

    def spread_wait(a, i):
        copies = spread(a, i)
        for copy in copies[1:] if i > 0 else copies:
            copy.wait_recv()

    chunks = r.own_fin.shape[1]
    span = r.own_fin.shape[3]

    def core_copy(b, c):
        return remote(
            r.stage_core.at[b, c], r.got_core.at[b, c], r.core_send.at[b, c],
            r.core_recv.at[b, c], core_mate,
        )

    def x_copy(b, c):
        return remote(
            r.stage_x.at[b, c], r.got_x.at[b, c], r.x_send.at[b, c], r.x_recv.at[b, c], chip_mate
        )

    def start_sum(b, tile, product, first=False):
        if not first:
            pl.semaphore_wait(r.core_credit, 1)
            pl.semaphore_wait(r.x_credit, 1)

        def put(ref, index, at, value):
            ref[(*index, slice(None), at)] = value.astype(ref.dtype)

        routes = (
            ((1 - chip) * 2 + 1 - core, lambda c, at, v: put(r.stage_core, (b, c, 0), at, v)),
            (chip * 2 + 1 - core, lambda c, at, v: put(r.stage_core, (b, c, 1), at, v)),
            ((1 - chip) * 2 + core, lambda c, at, v: put(r.own_fwd, (c,), at, v)),
            (chip * 2 + core, lambda c, at, v: put(r.own_fin, (b, c), at, v)),
        )

        def forward_chunk(c):
            core_copy(b, c).wait_recv()
            total = r.own_fwd[c].astype(f32) + r.got_core[b, c, 0].astype(f32)
            r.stage_x[b, c] = total.astype(bf16)
            x_copy(b, c).start()

        @pl.loop(0, chunks)
        def _(c):
            for t in range(span // 256):
                n = c * (span // 256) + t
                if tile is not None:
                    tile(n).wait()
                r.tmp[...] = product(n)
                for owner, route in routes:
                    route(c, slice(t * 256, t * 256 + 256), r.tmp[aligned(owner, quarter), :])
                if tile is not None:

                    @pl.when(n + 3 < width // 256)
                    def _():
                        tile(n + 3).start()

            core_copy(b, c).start()
            pl.when(c > 0)(lambda: forward_chunk(c - 1))

        forward_chunk(chunks - 1)

    def finish_sum(b, last=False):
        for c in range(chunks):
            x_copy(b, c).wait_recv()
            r.own_fin[b, c] = (
                r.own_fin[b, c] + r.got_core[b, c, 1].astype(f32) + r.got_x[b, c].astype(f32)
            )
        for c in range(chunks):
            core_copy(b, c).wait_send()
            x_copy(b, c).wait_send()
        if not last:
            pl.semaphore_signal(r.core_credit, inc=1, device_id=core_mate, device_id_type=MESH)
            pl.semaphore_signal(r.x_credit, inc=1, device_id=chip_mate, device_id_type=MESH)

    def gather(i, src, dst):
        def copy(slot, src, owner, mate):
            return remote(
                src, dst.at[aligned(owner, quarter), :], r.ag_send.at[i, slot],
                r.ag_recv.at[i, slot], mate,
            )

        other = chip_mate["tensor"]
        return (
            copy(0, src, tensor, chip_mate),
            copy(1, src, tensor, core_mate),
            copy(2, dst.at[aligned(other, quarter), :], other, core_mate),
        )

    def mask(bias, k, first):
        key_index = (place - k) * rows + lax.broadcasted_iota(jnp.int32, (rows, rows), 0)
        allowed = key_index >= r.seg[...]
        if first:
            query_index = place * rows + lax.broadcasted_iota(jnp.int32, (rows, rows), 1)
            allowed = allowed & (key_index <= query_index)
        bias[...] = jnp.where(allowed, 0.0, neg_large)

    def pad_keys(keys, block):
        keys[0] = jnp.where(key_lane, block, 0.0).astype(bf16)
        keys[1] = jnp.where(key_lane, 0.0, pltpu.roll(block, 64, 1)).astype(bf16)

    def kv_copy(k):
        return remote(
            r.kv.at[0], r.kv.at[k], r.kv_send.at[k], r.kv_recv.at[k],
            {"context": lax.rem(place + k, 4)},
        )

    def dkv_copy(k, mate):
        return remote(
            r.kv.at[k], r.got_kv.at[k], r.dkv_send.at[k], r.dkv_recv.at[k], {"context": mate}
        )

    def attention(wgu, raw, wq, wkv, keys, vals_t, bias):
        load_x = load(r.x_hbm, r.x_n2)
        load_wkv = load(r.wkv_hbm, wkv)
        load_wq = load(r.wq_hbm, wq)
        ring = raw.shape[0]

        def raw_copy(i):
            slot = turn_of(i, ring)
            return pltpu.make_async_copy(
                r.wgateup_hbm.at[aligned(i, 128)], raw.at[slot], r.raw_sem.at[slot]
            )

        for i in range(ring):
            raw_copy(i).start()

        position = place * rows + lanes((1, rows)) - r.seg[...]
        cosine, sine = cos_sin(r.freqs[...] * position.astype(f32))
        r.cos[...] = jnp.concatenate([cosine] * 4, 0).T
        r.sin[...] = jnp.concatenate([-sine, sine] * 2, 0).T

        load_x.wait()

        @pl.loop(0, rows // 64)
        def _(i):
            at = aligned(i, 64)
            values = r.x_n2[at, :].astype(f32)
            inverse = lax.rsqrt(jnp.mean(values * values, -1, keepdims=True) + epsilon)
            r.n1_gb[at, :] = (values * inverse * r.gain_one[...]).astype(bf16)

        store(r.n1_gb, r.n1_out)

        load_wkv.wait()
        r.kv[0] = turn(
            dot(r.n1_gb[...], wkv[...]),
            jnp.where(key_lane, r.cos[...], 1.0),
            jnp.where(key_lane, r.sin[...], 0.0),
        ).astype(bf16)
        pl.semaphore_wait(barrier, len(mates))
        for k in (1, 2, 3):
            pl.when(place + k < 4)(kv_copy(k).start)
        if swap:
            swap_n1.start()
            for i in range(3):
                for part in range(len(line_parts(i))):
                    line_sent(0, i, part).start()

        load_wq.wait()

        @pl.loop(0, heads_width // 256)
        def _(i):
            wide = dot(r.n1_gb[...], wq[:, aligned(i, 256)])
            for part in range(2):
                turned = turn(wide[:, 128 * part : 128 * part + 128], r.cos[...], r.sin[...])
                at = pl.ds(pl.multiple_of(i * 256 + 128 * part, 128), 128)
                r.q[:, at] = (turned * (0.125 * log2_e)).astype(bf16)

        def attend_block(k, first):
            mask(bias, k, first)
            block = r.kv[k].astype(f32)
            pad_keys(keys, block)
            vals_t[...] = block.T[64:].astype(bf16)

            @pl.loop(0, heads_width // 128)
            def _(pair):
                pair_q = r.q[:, aligned(pair, 128)]
                for e in range(2):
                    head = pair * 2 + e
                    scores = dot_t(keys[e], pair_q) + bias[...]
                    top = jnp.max(scores, 0, keepdims=True)
                    at = aligned(head, 64)
                    if first:
                        weights = jnp.exp2(scores - top)
                        r.run_sum[head] = jnp.sum(weights, 0, keepdims=True)
                        r.att[at, :] = dot(vals_t[...], weights.astype(bf16))
                    else:
                        old = r.lse[head]
                        top = jnp.maximum(top, old)
                        fade = jnp.exp2(old - top)
                        weights = jnp.exp2(scores - top)
                        r.run_sum[head] = r.run_sum[head] * fade + jnp.sum(weights, 0, keepdims=True)
                        r.att[at, :] = r.att[at, :] * fade + dot(vals_t[...], weights.astype(bf16))
                    r.lse[head] = top

        attend_block(0, True)

        row = lax.broadcasted_iota(jnp.int32, (256, 256), 0)
        column = lax.broadcasted_iota(jnp.int32, (256, 256), 1)
        source = jnp.where(row < 128, 2 * row, 2 * row - 255)
        order = (column == source).astype(bf16)

        @pl.loop(0, width // 128)
        def _(i):
            raw_copy(i).wait()
            at = aligned(i, 128)
            split = dot(order, raw[turn_of(i, ring)].reshape(256, units)).astype(bf16)
            for b in range(units // 128):
                wgu[at, 256 * b : 256 * b + 128] = split[:128, 128 * b : 128 * b + 128]
                wgu[at, 256 * b + 128 : 256 * b + 256] = split[128:, 128 * b : 128 * b + 128]

            @pl.when(i + ring < width // 128)
            def _():
                raw_copy(i + ring).start()

        @pl.loop(1, place + 1)
        def _(k):
            kv_copy(k).wait_recv()
            attend_block(k, False)

        for k in (1, 2, 3):
            pl.when(place + k < 4)(kv_copy(k).wait_send)

        @pl.loop(0, heads_width // 128)
        def _(pair):
            for e in range(2):
                head = pair * 2 + e
                at = aligned(head, 64)
                r.att[at, :] = r.att[at, :] * (1.0 / r.run_sum[head])
                r.lse[head] = r.lse[head] + jnp.log2(r.run_sum[head])
            at = aligned(pair, 128)
            r.att_low[:, at] = r.att[at, :].T.astype(bf16)

    def feed_forward(wgu, g, wdown, acc_gu, acc_down, t_n2, t_g):
        gh = acc_down
        r.t_n2 = t_n2
        load_g = load(r.g_hbm, g)
        load_wdown = load(r.wdown_hbm, wdown)
        load_wout.wait()
        start_sum(0, None, lambda n: dot(r.att_low[...], r.wout[:, aligned(n, 256)]), first=True)
        if swap:
            swap_low.start()

        load_g.wait()
        load_wdown.wait()

        @pl.loop(0, units // 128)
        def _(b):
            at = aligned(b, 128)
            gh[:, at] = dot_t(g[...], wdown[at, :])

        finish_sum(0)
        load_x_own.wait()
        square = jnp.zeros((quarter, 1), f32)
        for c in range(chunks):
            at = slice(c * span, (c + 1) * span)
            part = r.own_fin[0, c] + r.x_own[:, at].astype(f32)
            r.resid[:, at] = part
            square = square + jnp.sum(part * part, -1, keepdims=True)
        inverse = lax.rsqrt(square / width + epsilon)
        r.x_n2[mine, :] = (r.resid[...] * inverse * r.gain_two[...]).astype(bf16)
        to_chip, to_core, onward = gather(3, r.x_n2.at[mine, :], r.x_n2)
        to_chip.start()
        to_core.start()

        def own_to_line(part):
            at = line_parts(0)[part]
            return pltpu.make_async_copy(
                r.x_n2.at[at, :], r.n2_z.at[place, at, :], r.own_sem.at[part]
            )

        if swap:
            own_to_line(0).start()
            own_to_line(0).wait()
            for i in range(3):
                line_sent(1, i, 0).start()

        def activations(gate, up, grad):
            sigmoid = 1.0 / (1.0 + jnp.exp(-gate))
            active = gate * sigmoid
            grad_gate = grad * up * (sigmoid * (1.0 + gate * (1.0 - sigmoid)))
            both = jnp.concatenate([grad_gate, grad * active], 1)
            return (active * up).astype(bf16), both.astype(bf16)

        def units_of(at):
            @pl.loop(0, units // 128)
            def _(b):
                wide = dot(r.x_n2[at, :], wgu[:, aligned(b, 256)])
                hid, gg = activations(wide[:, :128], wide[:, 128:], gh[at, aligned(b, 128)])
                r.hid[at, aligned(b, 128)] = hid
                r.gg[at, aligned(b, 256)] = gg

        to_core.wait_recv()
        units_of(aligned(chip, 2 * quarter))
        to_chip.wait_recv()
        onward.start()
        if swap:
            own_to_line(1).start()
            own_to_line(1).wait()
            line_sent(1, 0, 1).start()
        onward.wait_recv()
        units_of(aligned(1 - chip, 2 * quarter))
        if not swap:
            store(r.x_n2, r.n2_out)
            store(r.hid, r.hid_out)
            store(r.gg, r.gg_out)
            store(r.att_low, r.low_out)
        for copy in (to_chip, to_core, onward):
            copy.wait_send()
        if swap:
            spread_start(0, 1)

        steps = [(at, min(256, units - at)) for at in range(0, units, 256)]
        whole = units // 256

        def each_step(body):
            @pl.loop(0, whole)
            def _(step):
                body(pl.multiple_of(step * 256, 256), 256, step)

            if units % 256:
                body(whole * 256, units - whole * 256, whole)

        def turn_block():
            for t, ref in ((t_n2, r.x_n2), (t_g, g)):
                for i, owner in enumerate((side, 1 - side)):
                    columns = aligned(owner * 4 + place, 256)
                    t[i * 256 : i * 256 + 256, :] = ref[:, columns].astype(f32).T.astype(bf16)

        def own_block():
            turn_block()

            def body(offset, size, step):
                gu, down = pl.ds(2 * offset, 2 * size), pl.ds(offset, size)
                acc_gu[:, gu] = dot(t_n2[...], r.gg[:, gu])
                acc_down[:, down] = dot(t_g[...], r.hid[:, down])

            each_step(body)

        def block_loads(i):
            return (
                pltpu.make_async_copy(r.n2_z.at[peers[i]], r.x_n2, r.block_sem.at[0]),
                pltpu.make_async_copy(r.g_z.at[peers[i]], g, r.block_sem.at[1]),
            )

        def exchange(step, size):
            offset = step * 256
            gu, down = pl.ds(2 * offset, 2 * size), pl.ds(offset, size)
            return tuple(
                remote(
                    ref.at[0:256, at], ref.at[256:512, at], r.side_send.at[step, i],
                    r.side_recv.at[step, i], dp_mate,
                )
                for i, (ref, at) in enumerate(((r.gg, gu), (r.hid, down)))
            )

        def other_block(i, last=False):
            for a in range(2):
                spread_wait(a, i)
            for copy in block_loads(i):
                copy.start()
            for copy in block_loads(i):
                copy.wait()
            turn_block()
            if last:
                pl.semaphore_wait(r.side_credit, 1)

            def body(offset, size, step):
                gu, down = pl.ds(2 * offset, 2 * size), pl.ds(offset, size)
                wide = dot(r.x_n2[...], wgu[:, gu])
                grad = dot_t(g[...], wdown[down, :])
                parts = [
                    activations(
                        wide[:, 2 * q : 2 * q + 128],
                        wide[:, 2 * q + 128 : 2 * q + 256],
                        grad[:, q : q + 128],
                    )
                    for q in range(0, size, 128)
                ]
                hid = jnp.concatenate([part[0] for part in parts], 1)
                gg = jnp.concatenate([part[1] for part in parts], 1)
                acc_gu[:, gu] += dot(t_n2[...], gg)
                acc_down[:, down] += dot(t_g[...], hid)
                if last:
                    r.gg[0:256, gu] = acc_gu[256:512, gu].astype(bf16)
                    r.hid[0:256, down] = acc_down[256:512, down].astype(bf16)

                    @pl.when(step < len(steps) - 1)
                    def _():
                        for copy in exchange(step, size):
                            copy.start()

            each_step(body)

        def last_exchange():
            for copy in exchange(len(steps) - 1, steps[-1][1]):
                copy.start()

        def own_share(first, stop):
            for step in range(first, stop):
                offset, size = steps[step]
                for copy in exchange(step, size):
                    copy.wait_recv()
                gu, down = slice(2 * offset, 2 * (offset + size)), slice(offset, offset + size)
                acc_gu[0:256, gu] += r.gg[256:512, gu].astype(f32)
                acc_down[0:256, down] += r.hid[256:512, down].astype(f32)
                for copy in share_stores(step, offset, size):
                    copy.start()

        def share_stores(step, offset, size):
            gu, down = pl.ds(2 * offset, 2 * size), pl.ds(offset, size)
            return (
                pltpu.make_async_copy(
                    acc_gu.at[0:256, gu], r.dgu_out.at[:, gu], r.share_sem.at[step, 0]
                ),
                pltpu.make_async_copy(
                    acc_down.at[0:256, down], r.dwdown_out.at[:, down], r.share_sem.at[step, 1]
                ),
            )

        def finish_shares():
            for step, (offset, size) in enumerate(steps):
                for copy in exchange(step, size):
                    copy.wait_send()
                for copy in share_stores(step, offset, size):
                    copy.wait()

        store_copy(0).wait()
        if swap:
            swap_n1.wait_send()
        start_sum(0, None, lambda n: dot_t(r.gg[...], wgu[aligned(n, 256), :]))
        if swap:
            own_block()
            for a in range(2):
                spread_start(a, 0)
        r.share_tools = (last_exchange, own_share, finish_shares, len(steps) - 1)
        rest(wdown, other_block)

    def first_half(wgu):
        pl.run_scoped(
            functools.partial(attention, wgu),
            raw=bf(4, 128, 2, units),
            wq=bf(width, heads_width),
            wkv=bf(width, 128),
            keys=bf(2, rows, 128),
            vals_t=bf(64, rows),
            bias=pltpu.VMEM((rows, rows), f32),
        )
        pl.run_scoped(
            functools.partial(feed_forward, wgu),
            g=bf(rows, width),
            wdown=bf(units, width),
            acc_gu=pltpu.VMEM((rows, 2 * units), f32),
            acc_down=pltpu.VMEM((rows, units), f32),
            t_n2=bf(512, rows),
            t_g=bf(512, rows),
        )

    def slot_qkv(n):
        return pl.multiple_of(turn_of(n, 3) * qkv, 128)

    def tile_qkv(n):
        at, first = aligned(n, 256), slot_qkv(n)
        copies = (
            pltpu.make_async_copy(
                r.wq_hbm.at[at],
                r.wout.at[0:256, pl.ds(first, heads_width)],
                r.w_rows_sem.at[turn_of(n, 3)],
            ),
            pltpu.make_async_copy(
                r.wkv_hbm.at[at],
                r.wout.at[0:256, pl.ds(pl.multiple_of(first + heads_width, 128), 128)],
                r.w_kv_sem.at[turn_of(n, 3)],
            ),
        )
        return types.SimpleNamespace(
            start=lambda: [copy.start() for copy in copies],
            wait=lambda: [copy.wait() for copy in copies],
        )

    def back_through_norm(b, values, gain_ref, gain_row, emit):
        square = jnp.zeros((quarter, 1), f32)
        inner = jnp.zeros((quarter, 1), f32)
        for c in range(chunks):
            at = slice(c * span, (c + 1) * span)
            v = values[:, at].astype(f32)
            square = square + jnp.sum(v * v, -1, keepdims=True)
            inner = inner + jnp.sum(r.own_fin[b, c] * gain_ref[:, at] * v, -1, keepdims=True)
        inverse = lax.rsqrt(square / width + epsilon)
        slope = inner / width * (inverse * inverse * inverse)
        for c in range(chunks):
            at = slice(c * span, (c + 1) * span)
            v = values[:, at].astype(f32)
            dn = r.own_fin[b, c]
            r.gain_sum[0, gain_row : gain_row + 1, at] = jnp.sum(
                dn * v * inverse, 0, keepdims=True
            )
            emit(at, inverse * dn * gain_ref[:, at] - v * slope)

    if swap:
        is_end = (place == 0) | (place == 3)
        is_mid = jnp.logical_not(is_end)
        io_mate, across_mate = {"context": beside}, {"context": 3 - place}
        sets = 2

        def unit(u):
            if u == 0:
                cut = (r.n1_gb.at[:, mine_cols], r.gb_o)
                other = r.other_kept.at[:, 0:heads_width]
                return (cut, r.att_low, other, heads_width, r.dwout_out)
            cut = (r.n1_out.at[:, mine_cols], r.n1_o)
            return (cut, r.gqkv, r.other_kept, qkv, r.dwqkv_out)

        def cut_loads(u):
            own, other = unit(u)[0]
            return (
                pltpu.make_async_copy(own, r.cut.at[0:rows], r.cut_sem.at[0]),
                pltpu.make_async_copy(other, r.cut.at[rows : 2 * rows], r.cut_sem.at[1]),
            )

        def piece(ref, s, j, u):
            return ref.at[s, j, :, 0 : unit(u)[3]]

        def line_copy(u, j, slot, mate):
            s = u % sets
            return remote(
                piece(r.stage, s, j, u), (r.got_out, r.got_qkv)[u].at[slot], r.unit_send.at[s, j],
                r.unit_recv.at[s, slot], mate,
            )

        def result(u):
            return pltpu.make_async_copy(
                r.sums.at[u % sets, :, 0 : unit(u)[3]], unit(u)[4], r.sums_sem.at[u % sets]
            )

        def prepare(u):
            s = u % sets
            own, other, width_u = unit(u)[1], unit(u)[2], unit(u)[3]
            for copy in cut_loads(u):
                copy.wait()

            @pl.loop(0, 4)
            def _(j):
                chunk = jnp.where(
                    j == 0,
                    jnp.where(low_side, 3, 0),
                    jnp.where(
                        j == 1, jnp.where(low_side, 2, 1), jnp.where(j == 2, beside, place)
                    ),
                )
                for i in range(2):
                    cut = r.cut[i * rows : (i + 1) * rows, aligned(chunk, 256)]
                    r.t_n2[i * 256 : i * 256 + 256, :] = cut.astype(f32).T.astype(bf16)

                def block(at):
                    term = dot(r.t_n2[0:256], own[:, at]) + dot(
                        r.t_n2[256:512], other[:, at]
                    )

                    @pl.when(j < 3)
                    def _():
                        r.stage[s, j, :, at] = term.astype(bf16)

                    @pl.when(j == 3)
                    def _():
                        r.sums[s, :, at] = term

                @pl.loop(0, width_u // 256)
                def _(tile):
                    block(aligned(tile, 256))

                if width_u % 256:
                    block(slice(width_u - width_u % 256, width_u))

                @pl.when((j < 3) & is_end)
                def _():
                    line_copy(u, j, j, io_mate).start()

        def add_in(u, j, slot):
            width_u, s = unit(u)[3], u % sets
            line_copy(u, 0, slot, io_mate).wait_recv()

            @pl.loop(0, 4)
            def _(i):
                at = aligned(i, 64)
                total = r.stage[s, j, at, 0:width_u].astype(f32)
                total = total + (r.got_out, r.got_qkv)[u][slot, at, :].astype(f32)
                r.stage[s, j, at, 0:width_u] = total.astype(bf16)

        def pass_on(u, step):
            @pl.when(is_mid)
            def _():
                if step < 2:
                    add_in(u, step, step)
                    line_copy(u, step, 3 + step, across_mate).start()
                else:
                    add_in(u, 2, 3)
                    line_copy(u, 2, 0, io_mate).start()

        def complete(u):
            width_u, s = unit(u)[3], u % sets

            def take(slots):
                for slot in slots:
                    line_copy(u, 0, slot, io_mate).wait_recv()

                @pl.loop(0, 4)
                def _(i):
                    at = aligned(i, 64)
                    total = r.sums[s, at, 0:width_u]
                    for slot in slots:
                        total = total + (r.got_out, r.got_qkv)[u][slot, at, :].astype(f32)
                    r.sums[s, at, 0:width_u] = total

            @pl.when(is_end)
            def _():
                take((0,))

            @pl.when(is_mid)
            def _():
                take((2, 4))

            result(u).start()

    def rest(wdown, other_block):
        r.gain_sum[...] = jnp.zeros_like(r.gain_sum)

        finish_sum(0)
        load_g_own.wait()
        for i in range(1, len(stores)):
            store_copy(i).wait()

        def keep_resid(at, grad):
            r.n1_gb[mine, at] = (r.g_own[:, at].astype(f32) + grad).astype(bf16)

        back_through_norm(0, r.resid, r.gain_two, 1, keep_resid)
        gb_chip, gb_core, gb_onward = gather(0, r.n1_gb.at[mine, :], r.n1_gb)
        gb_chip.start()
        gb_core.start()
        start_sum(0, None, lambda n: dot(r.hid[...], wdown[:, aligned(n, 256)]))
        if swap:
            pl.semaphore_signal(r.side_credit, inc=1, device_id=dp_mate, device_id_type=MESH)
            other_block(0)
        gb_chip.wait_recv()
        gb_onward.start()
        if swap:
            spread_onward(0, 1)
            for a, i in ((1, 1), (0, 2), (1, 2)):
                spread_start(a, i)
        gb_core.wait_recv()
        gb_onward.wait_recv()
        if swap:
            swap_gb.start()
        else:
            gb_store = pltpu.make_async_copy(r.n1_gb, r.gb_out, r.cut_sem.at[0])
            gb_store.start()
        pl.run_scoped(
            attention_back,
            ga=bf(rows, heads_width),
            bias=fl(rows, rows),
            delta=fl(heads_width // HD, 1, rows),
            keys=bf(2, rows, 128),
            vals=bf(2, rows, 128),
            keys_t=bf(HD, rows),
            dk=fl(2, rows, 128),
            dv=fl(2, rows, 128),
        )
        for n in range(3):
            tile_qkv(n).start()
        last_part = functools.partial(
            closing, other_block, gb_chip, gb_core, gb_onward
        )
        if swap:
            pl.run_scoped(
                last_part,
                other_kept=bf(rows, qkv),
                cut=bf(2 * rows, width // 2),
                stage=bf(2, 3, 256, qkv),
                sums=fl(2, 256, qkv),
            )
        else:
            last_part()
            gb_store.wait()

    def attention_back(**scoped):
        vars(r).update(scoped)

        for i in range(heads_width // 256):
            at = slice(i * 256, i * 256 + 256)
            r.ga[:, at] = dot_t(r.n1_gb[...], r.wout[at, :]).astype(bf16)

        @pl.loop(0, heads_width // 128)
        def _(pair):
            at = aligned(pair, 128)
            product = r.ga[:, at].astype(f32).T * r.att[at, :]
            for e in range(2):
                r.delta[pair * 2 + e] = jnp.sum(product[64 * e : 64 * e + 64], 0, keepdims=True)

        r.att[...] = jnp.zeros_like(r.att)

        def back_block(k, first):
            mask(r.bias, k, first)
            block = r.kv[k].astype(f32)
            rolled = pltpu.roll(block, 64, 1)
            pad_keys(r.keys, block)
            r.vals[0] = jnp.where(key_lane, rolled, 0.0).astype(bf16)
            r.vals[1] = jnp.where(key_lane, 0.0, block).astype(bf16)
            r.keys_t[...] = block.T[:64].astype(bf16)
            r.dk[...] = jnp.zeros_like(r.dk)
            r.dv[...] = jnp.zeros_like(r.dv)

            @pl.loop(0, heads_width // 128)
            def _(pair):
                pair_q = r.q[:, aligned(pair, 128)]
                pair_ga = r.ga[:, aligned(pair, 128)]
                for e in range(2):
                    head = pair * 2 + e
                    probs = jnp.exp2(dot_t(r.keys[e], pair_q) + r.bias[...] - r.lse[head])
                    grad_probs = dot_t(r.vals[e], pair_ga)
                    grad_scores = (probs * (grad_probs - r.delta[head])).astype(bf16)
                    r.dv[e] += dot(probs.astype(bf16), pair_ga)
                    r.dk[e] += dot(grad_scores, pair_q)
                    r.att[aligned(head, 64), :] += dot(r.keys_t[...], grad_scores)

            return jnp.where(
                key_lane,
                (r.dk[0] + pltpu.roll(r.dk[1], 64, 1)) * (1.0 / log2_e),
                r.dv[1] + pltpu.roll(r.dv[0], 64, 1),
            )

        @pl.loop(0, place)
        def _(i):
            k = place - i
            r.kv[k] = back_block(k, False).astype(bf16)
            dkv_copy(k, i).start()

        r.tmp[:, 0:128] = back_block(0, True)

    def closing(other_block, gb_chip, gb_core, gb_onward, **scoped):
        vars(r).update(scoped)
        last_exchange, own_share, finish_shares, last_step = r.share_tools
        if swap:
            spread_onward(1, 1)
            swap_low.wait_recv()
            low_load = pltpu.make_async_copy(
                r.low_o, r.other_kept.at[:, 0:heads_width], r.late_sem
            )
            low_load.start()

        @pl.loop(0, heads_width // 128)
        def _(pair):
            at = aligned(pair, 128)
            turned = turn(r.att[at, :].T * 0.125, r.cos[...], -r.sin[...])
            r.gqkv[:, at] = turned.astype(bf16)

        for k in (1, 2, 3):

            @pl.when(place + k < 4)
            def _():
                dkv_copy(k, 0).wait_recv()
                r.tmp[:, 0:128] += r.got_kv[k].astype(f32)

        r.gqkv[:, heads_width : heads_width + 128] = turn(
            r.tmp[:, 0:128],
            jnp.where(key_lane, r.cos[...], 1.0),
            jnp.where(key_lane, -r.sin[...], 0.0),
        ).astype(bf16)
        if swap:
            swap_gqkv.start()
        else:
            gqkv_store = pltpu.make_async_copy(r.gqkv, r.gqkv_out, r.cut_sem.at[1])
            gqkv_store.start()

        finish_sum(0)
        for c in range(chunks):
            at = slice(c * span, (c + 1) * span)
            r.g_own[:, at] = (r.resid[:, at] + r.own_fin[0, c]).astype(bf16)
        mixed_chip, mixed_core, mixed_onward = gather(1, r.g_own, r.mixed_out)
        mixed_store = pltpu.make_async_copy(r.g_own, r.mixed_out.at[mine, :], r.out_sem.at[0])

        start_sum(0, tile_qkv, lambda n: dot_t(r.gqkv[...], r.wout[0:256, pl.ds(slot_qkv(n), qkv)]))
        if swap:
            spread_onward(0, 2)
            swap_gb.wait_recv()
            low_load.wait()
            for copy in cut_loads(0):
                copy.start()
            prepare(0)
            swap_n1.wait_recv()
            for copy in cut_loads(1):
                copy.start()
            other_block(1)
            spread_onward(1, 2)
            pass_on(0, 0)
            swap_gqkv.wait_recv()
            gqkv_load = pltpu.make_async_copy(r.gqkv_o, r.other_kept, r.late_sem)
            gqkv_load.start()
            gqkv_load.wait()
            prepare(1)
            pass_on(0, 1)
            other_block(2, last=True)
            pass_on(0, 2)
            pass_on(1, 0)

        finish_sum(0, last=True)

        def keep_tokens(at, grad):
            r.x_own[:, at] = (r.n1_gb[mine, at].astype(f32) + grad).astype(bf16)

        back_through_norm(0, r.x_own, r.gain_one, 0, keep_tokens)
        tokens_chip, tokens_core, tokens_onward = gather(2, r.x_own, r.tokens_out)
        tokens_store = pltpu.make_async_copy(r.x_own, r.tokens_out.at[mine, :], r.out_sem.at[1])

        def gain_copy(i):
            mate = (core_mate, chip_mate)[i]
            return remote(
                r.gain_sum.at[i], r.gain_got.at[i], r.gain_send.at[i], r.gain_recv.at[i], mate
            )

        def gain_add(i):
            gain_copy(i).wait()
            r.gain_sum[i + 1] = r.gain_sum[i] + r.gain_got[i]

        gain_copy(0).start()
        for copy in (tokens_chip, tokens_core, tokens_store, mixed_chip, mixed_core, mixed_store):
            copy.start()
        if swap:
            pass_on(1, 1)
        gain_add(0)
        gain_copy(1).start()
        if swap:
            complete(0)
            pass_on(1, 2)
        gain_add(1)
        if swap:
            across = remote(
                r.gain_sum.at[2, :, theirs_cols], r.gain_half.at[0], r.gain_send.at[2],
                r.gain_recv.at[2], dp_mate,
            )
            across.start()
            last_exchange()
            own_share(0, 2)
            complete(1)
        else:
            r.gains_out[...] = r.gain_sum[2]
        tokens_chip.wait_recv()
        tokens_onward.start()
        mixed_chip.wait_recv()
        mixed_onward.start()
        if swap:
            own_share(2, last_step)
            across.wait()
            r.gain_half[1] = r.gain_sum[2, :, mine_cols] + r.gain_half[0]
            part = half // 4
            pieces = [
                remote(
                    r.gain_half.at[1, :, aligned(lax.rem(place + k, 4), part)],
                    r.gain_piece.at[k], r.gain_send.at[2 + k], r.gain_recv.at[2 + k],
                    {"context": lax.rem(place + k, 4)},
                )
                for k in (1, 2, 3)
            ]
            for copy in pieces:
                copy.start()
            own_share(last_step, last_step + 1)
            for copy in pieces:
                copy.wait()
            r.gains_out[...] = (
                r.gain_half[1, :, aligned(place, part)]
                + r.gain_piece[1]
                + r.gain_piece[2]
                + r.gain_piece[3]
            )

        for copy in (mixed_core, mixed_onward, tokens_core, tokens_onward):
            copy.wait_recv()
        for copy in (
            gb_chip, gb_core, gb_onward, mixed_chip, mixed_core, mixed_onward, tokens_chip,
            tokens_core, tokens_onward,
        ):
            copy.wait_send()
        mixed_store.wait()
        tokens_store.wait()
        for k in (1, 2, 3):
            pl.when(place >= k)(dkv_copy(k, 0).wait_send)
        if swap:
            for copy in (swap_low, swap_gb, swap_gqkv):
                copy.wait_send()
            for a in range(2):
                for i in range(3):
                    for copy in spread(a, i):
                        copy.wait_send()
                    for part in range(len(line_parts(i))):
                        line_sent(a, i, part).wait_send()
            finish_shares()
            for u in range(2):
                for j in range(3):
                    line_copy(u, j, 0, io_mate).wait_send()
                result(u).wait()
        else:
            gqkv_store.wait()

    load_wout = load(r.wout_hbm, r.wout)
    load_x_own = load(r.x_hbm.at[mine, :], r.x_own)
    load_g_own = load(r.g_hbm.at[mine, :], r.g_own)
    pl.run_scoped(first_half, pltpu.VMEM((width, 2 * units), bf16))


def layer(swap, inputs, rows, width, units, heads):
    bf16, f32 = jnp.bfloat16, jnp.float32
    quarter = rows // 4
    chunks = 4
    span = width // chunks
    wide = heads * HD
    qkv = wide + 2 * HD
    outs = {
        "mixed_out": ((rows, width), bf16),
        "tokens_out": ((rows, width), bf16),
        "gains_out": ((8, width // 8 if swap else width), f32),
        "n1_out": ((rows, width), bf16),
    }
    if swap:
        outs |= {
            "dwdown_out": ((width // 8, units), f32),
            "dgu_out": ((width // 8, 2 * units), f32),
            "dwout_out": ((width // 8, wide), f32),
            "dwqkv_out": ((width // 8, qkv), f32),
            "g_z": ((4, rows, width), bf16),
            "n2_z": ((4, rows, width), bf16),
            "low_o": ((rows, wide), bf16),
            "gqkv_o": ((rows, qkv), bf16),
            "gb_o": ((rows, width // 2), bf16),
            "n1_o": ((rows, width // 2), bf16),
        }
    else:
        outs |= {
            "gb_out": ((rows, width), bf16),
            "gqkv_out": ((rows, qkv), bf16),
            "n2_out": ((rows, width), bf16),
            "hid_out": ((rows, units), bf16),
            "gg_out": ((rows, 2 * units), bf16),
            "low_out": ((rows, wide), bf16),
        }
    scratch = {
        "x_n2": ((rows, width), bf16),
        "n1_gb": ((rows, width), bf16),
        "wout": ((wide, width), bf16),
        "q": ((rows, wide), bf16),
        "kv": ((4, rows, 2 * HD), bf16),
        "att": ((wide, rows), f32),
        "att_low": ((rows, wide), bf16),
        "lse": ((heads, 1, rows), f32),
        "run_sum": ((heads, 1, rows), f32),
        "cos": ((rows, 2 * HD), f32),
        "sin": ((rows, 2 * HD), f32),
        "resid": ((quarter, width), f32),
        "g_own": ((quarter, width), bf16),
        "x_own": ((quarter, width), bf16),
        "hid": ((rows, units), bf16),
        "gg": ((rows, 2 * units), bf16),
        "tmp": ((rows, 256), f32),
        "stage_core": ((1, chunks, 2, quarter, span), bf16),
        "got_core": ((1, chunks, 2, quarter, span), bf16),
        "own_fwd": ((chunks, quarter, span), bf16),
        "own_fin": ((1, chunks, quarter, span), f32),
        "stage_x": ((1, chunks, quarter, span), bf16),
        "got_x": ((1, chunks, quarter, span), bf16),
        "got_kv": ((4, rows, 2 * HD), bf16),
        "gqkv": ((rows, qkv), bf16),
        "gain_sum": ((3, 8, width), f32),
        "gain_got": ((2, 8, width), f32),
    }
    if swap:
        scratch |= {
            "got_out": ((5, width // 8, wide), bf16),
            "got_qkv": ((5, width // 8, qkv), bf16),
            "gain_half": ((2, 8, width // 2), f32),
            "gain_piece": ((4, 8, width // 8), f32),
        }
    sems = {
        "load_sem": (8,),
        "store_sem": (5,),
        "raw_sem": (4,),
        "w_rows_sem": (3,),
        "w_kv_sem": (3,),
        "core_send": (1, chunks),
        "core_recv": (1, chunks),
        "x_send": (1, chunks),
        "x_recv": (1, chunks),
        "ag_send": (10, 3),
        "ag_recv": (10, 3),
        "kv_send": (4,),
        "kv_recv": (4,),
        "dkv_send": (4,),
        "dkv_recv": (4,),
        "gain_send": (6,),
        "gain_recv": (6,),
        "out_sem": (2,),
        "cut_sem": (2,),
        "late_sem": (),
    }
    if swap:
        sems |= {
            "dp_send": (4,),
            "dp_recv": (4,),
            "line_send": (2, 4, 2),
            "line_recv": (2, 4, 2),
            "own_sem": (2,),
            "block_sem": (2,),
            "side_send": (-(-units // 256), 2),
            "side_recv": (-(-units // 256), 2),
            "share_sem": (-(-units // 256), 2),
            "unit_send": (2, 3),
            "unit_recv": (2, 5),
            "sums_sem": (2,),
        }
    credits = ["core_credit", "x_credit", *(["side_credit"] if swap else [])]
    names = [*inputs, *outs, *scratch, *sems, *credits]
    anywhere = pl.BlockSpec(memory_space=pl.ANY)
    inside = pl.BlockSpec(memory_space=pltpu.VMEM)
    results = pl.pallas_call(
        functools.partial(layer_kernel, names, swap),
        out_shape=[jax.ShapeDtypeStruct(*out) for out in outs.values()],
        in_specs=[anywhere if name.endswith("_hbm") else inside for name in inputs],
        out_specs=[inside if name == "gains_out" else anywhere for name in outs],
        scratch_shapes=[
            *(pltpu.VMEM(*shape) for shape in scratch.values()),
            *(pltpu.SemaphoreType.DMA(shape) for shape in sems.values()),
            *(pltpu.SemaphoreType.REGULAR for _ in credits),
        ],
        compiler_params=pltpu.CompilerParams(
            collective_id=0, has_side_effects=True, vmem_limit_bytes=int(63.5 * MIB)
        ),
        name="layer",
    )(*inputs.values())
    return dict(zip(outs, results, strict=True))


def finish_kernel(
    down_hbm, gateup_hbm, out_hbm, qkv_hbm, tokens_hbm, mixed_hbm, gains,
    down_o, gateup_o, out_o, q_o, kv_o, tokens_o, mixed_o, gain_one_o, gain_two_o,
    down, gateup, out, qkv, tokens, mixed, down_t, gateup_t, out_t, kv_t, tokens_t,
    load_sem, store_sem,
):
    wide = q_o.shape[1]
    parts = 4
    loads, stores = [], []

    def load(src, dst):
        copy = pltpu.make_async_copy(src, dst, load_sem.at[len(loads)])
        copy.start()
        loads.append(copy)
        return copy

    def store(src, dst):
        copy = pltpu.make_async_copy(src, dst, store_sem.at[len(stores)])
        copy.start()
        stores.append(copy)

    def piece(ref, i):
        size = ref.shape[0] // parts
        return ref.at[i * size : (i + 1) * size]

    gain_one_o[...] = gains[0:1, :]
    gain_two_o[...] = gains[1:2, :]
    token_loads = [load(piece(tokens_hbm, i), piece(tokens, i)) for i in range(parts)]
    gateup_loads = [load(piece(gateup_hbm, i), piece(gateup, i)) for i in range(parts)]
    load_mixed = load(mixed_hbm, mixed)
    load_down = load(down_hbm, down)
    load_qkv = load(qkv_hbm, qkv)
    load_out = load(out_hbm, out)
    for i in range(parts):
        token_loads[i].wait()
        piece(tokens_t, i)[...] = piece(tokens, i)[...].astype(jnp.float32)
        store(piece(tokens_t, i), piece(tokens_o, i))
    for i in range(parts):
        gateup_loads[i].wait()
        values, target = piece(gateup, i), piece(gateup_t, i)
        for b in range(gateup.shape[1] // 256):
            at = slice(b * 128, b * 128 + 128)
            target[:, 0, at] = values[:, b * 256 : b * 256 + 128]
            target[:, 1, at] = values[:, b * 256 + 128 : b * 256 + 256]
        store(target, piece(gateup_o, i))
    load_mixed.wait()
    store(mixed, mixed_o)
    load_down.wait()
    for i in range(down.shape[1] // 128):
        at = slice(i * 128, i * 128 + 128)
        down_t[at, :] = down[:, at].T
    store(down_t, down_o)
    load_qkv.wait()
    store(qkv.at[:, 0:wide], q_o)
    kv_t[:, 0, :] = qkv[:, wide:]
    store(kv_t, kv_o)
    load_out.wait()
    for i in range(wide // 128):
        at = slice(i * 128, i * 128 + 128)
        out_t[at, :] = out[:, at].T
    store(out_t, out_o)
    for copy in stores:
        copy.wait()


def finish(down, gateup, out, qkv, tokens, mixed, gains):
    depth, units = down.shape
    wide = out.shape[1]
    rows, width = tokens.shape
    bf16, f32 = jnp.bfloat16, jnp.float32
    outs = [
        ((units, depth), f32),
        ((depth, 2, units), f32),
        ((wide, depth), f32),
        ((depth, wide), f32),
        ((depth, 1, 2 * HD), f32),
        ((rows, width), f32),
        ((rows, width), bf16),
        ((1, depth), f32),
        ((1, depth), f32),
    ]
    scratch = [
        *((array.shape, array.dtype) for array in (down, gateup, out, qkv, tokens, mixed)),
        *outs[:3],
        *outs[4:6],
    ]
    anywhere = pl.BlockSpec(memory_space=pl.ANY)
    inside = pl.BlockSpec(memory_space=pltpu.VMEM)
    return pl.pallas_call(
        finish_kernel,
        out_shape=[jax.ShapeDtypeStruct(*entry) for entry in outs],
        in_specs=[*[anywhere] * 6, inside],
        out_specs=[*[anywhere] * 7, inside, inside],
        scratch_shapes=[
            *(pltpu.VMEM(*entry) for entry in scratch),
            pltpu.SemaphoreType.DMA((12,)),
            pltpu.SemaphoreType.DMA((13,)),
        ],
        compiler_params=pltpu.CompilerParams(vmem_limit_bytes=62 * MIB),
        name="finish",
    )(down, gateup, out, qkv, tokens, mixed, gains)


def pick(array, index, axis):
    return lax.dynamic_index_in_dim(array, index, axis, keepdims=False)


def line_sum(part):
    place = lax.axis_index("context")
    order = jnp.array([[3, 2, 1, 0], [3, 2, 0, 1], [0, 1, 3, 2], [0, 1, 2, 3]], jnp.int32)[place]
    first, second, third, own = (part(order[i]) for i in range(4))

    def inward(array):
        return lax.ppermute(array.astype(jnp.bfloat16), "context", [(0, 1), (3, 2)])

    def across(array):
        return lax.ppermute(array.astype(jnp.bfloat16), "context", [(1, 2), (2, 1)])

    def outward(array):
        return lax.ppermute(array.astype(jnp.bfloat16), "context", [(1, 0), (2, 3)])

    in_one, in_two, in_three = inward(first), inward(second), inward(third)
    over_two = across(first + in_one.astype(jnp.float32))
    over_three = across(second + in_two.astype(jnp.float32))
    out_three = outward(third + over_two.astype(jnp.float32))
    return (
        own
        + in_three.astype(jnp.float32)
        + over_three.astype(jnp.float32)
        + out_three.astype(jnp.float32)
    )


def weight_grad(left, right, axis):
    whole = lax.dot_general(
        left, right, (((0,), (0,)), ((), ())), preferred_element_type=jnp.float32
    )
    mine = lax.psum_scatter(
        whole.astype(jnp.bfloat16), "dp", scatter_dimension=axis, tiled=True
    )
    step = mine.shape[axis] // 4
    return line_sum(
        lambda chunk: lax.dynamic_slice_in_dim(mine, chunk * step, step, axis).astype(jnp.float32)
    )


def shards(
    tokens, segments, gain_one, w_query, w_keyval, w_out, gain_two, w_gateup, w_down, cotangent
):
    num_seqs, tok_count, model_width = tokens.shape
    heads_kv = w_keyval.shape[1]
    width_q = w_query.shape[1]
    units = w_down.shape[0]
    swap = lax.axis_size("dp") == 2
    freqs = 10000.0 ** (-(np.arange(HD // 2, dtype=np.float32) * 2.0) / HD)
    g = cotangent.reshape(tok_count, model_width)
    inputs = {
        "seg": segments,
        "freqs": jnp.asarray(freqs.astype(np.float32)[:, None]),
        "gain_one": gain_one[None],
        "gain_two": gain_two[None],
        "x_hbm": tokens.reshape(tok_count, model_width),
        "g_hbm": g,
        "wq_hbm": w_query,
        "wkv_hbm": w_keyval.reshape(model_width, 2 * HD),
        "wout_hbm": w_out,
        "wgateup_hbm": w_gateup,
        "wdown_hbm": w_down,
    }
    out = layer(swap, inputs, tok_count, model_width, units, width_q // HD)
    if swap:
        sent_wdown, sent_gateup, sent_wout, sent_wq, sent_wkv, grad_tokens, mixed, *gains = finish(
            *(out[name] for name in ("dwdown_out", "dgu_out", "dwout_out", "dwqkv_out")),
            *(out[name] for name in ("tokens_out", "mixed_out", "gains_out")),
        )
    else:
        gains = lax.psum_scatter(
            out["gains_out"], ("dp", "context"), scatter_dimension=1, tiled=True
        )
        sent_wdown = weight_grad(out["hid_out"], g, 1)
        sent_gateup = weight_grad(out["n2_out"], out["gg_out"], 0)
        sent_wout = weight_grad(out["low_out"], out["gb_out"], 1)
        sent_wqkv = weight_grad(out["n1_out"], out["gqkv_out"], 0)
        sent_wq, sent_wkv = sent_wqkv[:, :width_q], sent_wqkv[:, width_q:]
        sent_gateup = sent_gateup.reshape(-1, units // 128, 2, 128).transpose(0, 2, 1, 3)
        grad_tokens, mixed = out["tokens_out"].astype(jnp.float32), out["mixed_out"]
    return (
        mixed.reshape(tokens.shape),
        grad_tokens.reshape(tokens.shape),
        gains[0].reshape(-1),
        sent_wq,
        sent_wkv.reshape(-1, heads_kv, 2 * HD),
        sent_wout,
        gains[1].reshape(-1),
        sent_gateup.reshape(-1, 2, units),
        sent_wdown,
    )


def solution(mesh):
    return jax.shard_map(
        shards,
        mesh=mesh,
        in_specs=(
            P("dp", "context", None),
            P("dp", "context"),
            P(),
            P(None, "tensor"),
            P(None, "tensor", None),
            P("tensor", None),
            P(),
            P(None, None, "tensor"),
            P("tensor", None),
            P("dp", "context", None),
        ),
        out_specs=(
            P("dp", "context", None),
            P("dp", "context", None),
            P(("dp", "context")),
            P(("dp", "context"), "tensor"),
            P(("dp", "context"), "tensor", None),
            P("tensor", ("dp", "context")),
            P(("dp", "context")),
            P(("dp", "context"), None, "tensor"),
            P("tensor", ("dp", "context")),
        ),
        check_vma=False,
    )
```

```python
import functools
import types

import jax
import jax.numpy as jnp
import numpy as np
from jax import lax
from jax.experimental import pallas as pl
from jax.experimental.pallas import tpu as pltpu
from jax.sharding import PartitionSpec as P

HD = 64


epsilon = 1e-05
neg_large = -1e30


MESH = pl.DeviceIdType.MESH
MIB = 1 << 20
log2_e = 1.4426950408889634


def dot(left, right):
    return jnp.dot(left, right, preferred_element_type=jnp.float32)


def dot_t(left, right):
    return lax.dot_general(left, right, (((1,), (1,)), ((), ())), preferred_element_type=jnp.float32)


def lanes(shape):
    return lax.broadcasted_iota(jnp.int32, shape, len(shape) - 1)


def turn_of(n, size):
    return n % size if isinstance(n, int) else lax.rem(n, size)


def aligned(index, size):
    if isinstance(index, int):
        return pl.ds(index * size, size)
    return pl.ds(pl.multiple_of(index * size, size), size)


def turn(values, cosine, sine):
    low_half = lax.rem(lanes(values.shape), 64) < 32
    swapped = jnp.where(low_half, pltpu.roll(values, 96, 1), pltpu.roll(values, 32, 1))
    return values * cosine + swapped * sine


def cos_sin(phase):
    count = jnp.floor(phase * 0.6366197723675814 + 0.5)
    rest = phase - count * 1.5703125
    rest = rest - count * 0.0004837512969970703
    rest = rest - count * 7.549789954e-08
    square = rest * rest
    sine = rest + rest * square * (
        -0.16666666666 + square * (0.0083333333333 + square * -0.0001984126984)
    )
    cosine = 1.0 + square * (
        -0.5 + square * (0.041666666666 + square * (-0.0013888888889 + square * 2.48015873e-05))
    )
    place = count - 4.0 * jnp.floor(count * 0.25)
    odd = (place == 1.0) | (place == 3.0)
    first, second = jnp.where(odd, sine, cosine), jnp.where(odd, cosine, sine)
    return (
        jnp.where((place == 1.0) | (place == 2.0), -first, first),
        jnp.where(place >= 2.0, -second, second),
    )


def layer_kernel(names, swap, *refs):
    r = types.SimpleNamespace(**dict(zip(names, refs, strict=True)))
    rows, width = r.x_n2.shape
    quarter = rows // 4
    units = r.hid.shape[1]
    heads_width = r.q.shape[1]
    f32, bf16 = jnp.float32, jnp.bfloat16
    tensor = lax.axis_index("tensor")
    place = lax.axis_index("context")
    core, chip = lax.rem(tensor, 2), lax.div(tensor, 2)
    core_mate = {"tensor": chip * 2 + 1 - core}
    chip_mate = {"tensor": (1 - chip) * 2 + core}
    tensor_mates = (core_mate, chip_mate, {"tensor": (1 - chip) * 2 + 1 - core})
    mates = [*tensor_mates, *({"context": lax.rem(place + k, 4)} for k in (1, 2, 3))]
    if swap:
        side = lax.axis_index("dp")
        dp_mate = {"dp": 1 - side}
        mates += [dp_mate]
        mates += [{"dp": 1 - side, "context": lax.rem(place + k, 4)} for k in (1, 2, 3)]
    mine = aligned(tensor, quarter)
    key_lane = lanes((rows, 128)) < 64
    qkv = heads_width + 128
    bf = lambda *shape: pltpu.VMEM(shape, bf16)
    fl = lambda *shape: pltpu.VMEM(shape, f32)

    barrier = pltpu.get_barrier_semaphore()
    for mate in mates:
        pl.semaphore_signal(barrier, inc=1, device_id=mate, device_id_type=MESH)

    def remote(src, dst, send, recv, mate):
        return pltpu.make_async_remote_copy(
            src_ref=src, dst_ref=dst, send_sem=send, recv_sem=recv, device_id=mate,
            device_id_type=MESH,
        )

    loads, stores = [], []

    def load(src, dst):
        copy = pltpu.make_async_copy(src, dst, r.load_sem.at[len(loads)])
        loads.append(copy)
        copy.start()
        return copy

    def store_copy(i):
        return pltpu.make_async_copy(*stores[i], r.store_sem.at[i])

    def store(src, dst):
        stores.append((src, dst))
        store_copy(len(stores) - 1).start()

    swaps = []

    def swap_copy(src, dst):
        i = len(swaps)
        swaps.append(remote(src, dst, r.dp_send.at[i], r.dp_recv.at[i], dp_mate))
        return swaps[i]

    if swap:
        half = width // 2
        theirs_cols, mine_cols = aligned(1 - side, half), aligned(side, half)
        swap_n1 = swap_copy(r.n1_gb.at[:, theirs_cols], r.n1_o)
        swap_low = swap_copy(r.att_low, r.low_o)
        swap_gb = swap_copy(r.n1_gb.at[:, theirs_cols], r.gb_o)
        swap_gqkv = swap_copy(r.gqkv, r.gqkv_o)

    is_end = (place == 0) | (place == 3)
    is_mid = jnp.logical_not(is_end)
    low_side = place < 2
    beside = place + 1 - 2 * lax.rem(place, 2)
    peers = (beside, jnp.where(low_side, 2, 1), jnp.where(low_side, 3, 0))
    other_quarter = aligned(chip_mate["tensor"], quarter)

    def line_parts(i):
        return (mine, other_quarter) if i == 0 else (mine,)

    def line_sent(a, i, part):
        src, dst = ((r.g_hbm, r.g_z), (r.n2_z.at[place], r.n2_z))[a]
        step = lax.rem(peers[i] - place + 4, 4)
        at = line_parts(i)[part]
        return remote(
            src.at[at, :], dst.at[place, at, :], r.line_send.at[a, step, part],
            r.line_recv.at[a, step, part], {"context": peers[i]},
        )

    def line_got(a, i, part):
        dst = (r.g_z, r.n2_z)[a].at[peers[i], line_parts(i)[part], :]
        step = lax.rem(place - peers[i] + 4, 4)
        return remote(
            dst, dst, r.line_send.at[a, step, part], r.line_recv.at[a, step, part],
            {"context": peers[i]},
        )

    def handed_on(a, i):
        block = (r.g_z, r.n2_z)[a].at[peers[i], mine, :]
        return remote(
            block, block, r.hand_send.at[a, i - 1], r.hand_recv.at[a, i - 1], {"context": beside}
        )

    def hand_on(a, i):
        @pl.when(is_mid)
        def _():
            line_got(a, i, 0).wait_recv()
            handed_on(a, i).start()

    def spread(a, i):
        block = (r.g_z, r.n2_z)[a].at[peers[i]]
        slot = 4 + a * 3 + i
        if i > 0:
            return gather(slot, block.at[mine, :], block)
        return tuple(
            remote(
                block.at[at, :], block.at[at, :], r.ag_send.at[slot, part],
                r.ag_recv.at[slot, part], core_mate,
            )
            for part, at in enumerate(line_parts(0))
        )

    def spread_start(a, i):
        copies = spread(a, i)
        if i > 0:
            pl.when(is_end)(handed_on(a, i).wait_recv)
        else:
            for part in range(2):
                line_got(a, 0, part).wait_recv()
        for copy in copies[:2]:
            copy.start()

    def spread_onward(a, i):
        if i > 0:
            copies = spread(a, i)
            copies[0].wait_recv()
            copies[2].start()

    def spread_wait(a, i):
        copies = spread(a, i)
        for copy in copies[1:] if i > 0 else copies:
            copy.wait_recv()

    chunks = r.own_fin.shape[1]
    span = r.own_fin.shape[3]

    def core_copy(b, c):
        return remote(
            r.stage_core.at[b, c], r.got_core.at[b, c], r.core_send.at[b, c],
            r.core_recv.at[b, c], core_mate,
        )

    def x_copy(b, c):
        return remote(
            r.stage_x.at[b, c], r.got_x.at[b, c], r.x_send.at[b, c], r.x_recv.at[b, c], chip_mate
        )

    def start_sum(b, tile, product, first=False):
        if not first:
            pl.semaphore_wait(r.core_credit, 1)
            pl.semaphore_wait(r.x_credit, 1)

        def put(ref, index, at, value):
            ref[(*index, slice(None), at)] = value.astype(ref.dtype)

        routes = (
            ((1 - chip) * 2 + 1 - core, lambda c, at, v: put(r.stage_core, (b, c, 0), at, v)),
            (chip * 2 + 1 - core, lambda c, at, v: put(r.stage_core, (b, c, 1), at, v)),
            ((1 - chip) * 2 + core, lambda c, at, v: put(r.own_fwd, (c,), at, v)),
            (chip * 2 + core, lambda c, at, v: put(r.own_fin, (b, c), at, v)),
        )

        def forward_chunk(c):
            core_copy(b, c).wait_recv()
            total = r.own_fwd[c].astype(f32) + r.got_core[b, c, 0].astype(f32)
            r.stage_x[b, c] = total.astype(bf16)
            x_copy(b, c).start()

        @pl.loop(0, chunks)
        def _(c):
            for t in range(span // 256):
                n = c * (span // 256) + t
                if tile is not None:
                    tile(n).wait()
                r.tmp[...] = product(n)
                for owner, route in routes:
                    route(c, slice(t * 256, t * 256 + 256), r.tmp[aligned(owner, quarter), :])
                if tile is not None:

                    @pl.when(n + 3 < width // 256)
                    def _():
                        tile(n + 3).start()

            core_copy(b, c).start()
            pl.when(c > 1)(lambda: forward_chunk(c - 2))

        forward_chunk(chunks - 2)
        forward_chunk(chunks - 1)

    def finish_sum(b, last=False):
        for c in range(chunks):
            x_copy(b, c).wait_recv()
            r.own_fin[b, c] = (
                r.own_fin[b, c] + r.got_core[b, c, 1].astype(f32) + r.got_x[b, c].astype(f32)
            )
        for c in range(chunks):
            core_copy(b, c).wait_send()
            x_copy(b, c).wait_send()
        if not last:
            pl.semaphore_signal(r.core_credit, inc=1, device_id=core_mate, device_id_type=MESH)
            pl.semaphore_signal(r.x_credit, inc=1, device_id=chip_mate, device_id_type=MESH)

    def gather(i, src, dst):
        def copy(slot, src, owner, mate):
            return remote(
                src, dst.at[aligned(owner, quarter), :], r.ag_send.at[i, slot],
                r.ag_recv.at[i, slot], mate,
            )

        other = chip_mate["tensor"]
        return (
            copy(0, src, tensor, chip_mate),
            copy(1, src, tensor, core_mate),
            copy(2, dst.at[aligned(other, quarter), :], other, core_mate),
        )

    def mask(bias, k, first):
        key_index = (place - k) * rows + lax.broadcasted_iota(jnp.int32, (rows, rows), 0)
        allowed = key_index >= r.seg[...]
        if first:
            query_index = place * rows + lax.broadcasted_iota(jnp.int32, (rows, rows), 1)
            allowed = allowed & (key_index <= query_index)
        bias[...] = jnp.where(allowed, 0.0, neg_large)

    def pad_keys(keys, block):
        keys[0] = jnp.where(key_lane, block, 0.0).astype(bf16)
        keys[1] = jnp.where(key_lane, 0.0, pltpu.roll(block, 64, 1)).astype(bf16)

    def kv_copy(k):
        return remote(
            r.kv.at[0], r.kv.at[k], r.kv_send.at[k], r.kv_recv.at[k],
            {"context": lax.rem(place + k, 4)},
        )

    def dkv_copy(k, mate):
        return remote(
            r.kv.at[k], r.got_kv.at[k], r.dkv_send.at[k], r.dkv_recv.at[k], {"context": mate}
        )

    def attention(wgu, raw, wq, wkv, keys, vals_t, bias):
        load_x = load(r.x_hbm, r.x_n2)
        load_wkv = load(r.wkv_hbm, wkv)
        load_wq = load(r.wq_hbm, wq)
        ring = raw.shape[0]

        def raw_copy(i):
            slot = turn_of(i, ring)
            return pltpu.make_async_copy(
                r.wgateup_hbm.at[aligned(i, 128)], raw.at[slot], r.raw_sem.at[slot]
            )

        for i in range(ring):
            raw_copy(i).start()

        position = place * rows + lanes((1, rows)) - r.seg[...]
        cosine, sine = cos_sin(r.freqs[...] * position.astype(f32))
        r.cos[...] = jnp.concatenate([cosine] * 4, 0).T
        r.sin[...] = jnp.concatenate([-sine, sine] * 2, 0).T

        load_x.wait()

        @pl.loop(0, rows // 64)
        def _(i):
            at = aligned(i, 64)
            values = r.x_n2[at, :].astype(f32)
            inverse = lax.rsqrt(jnp.mean(values * values, -1, keepdims=True) + epsilon)
            r.n1_gb[at, :] = (values * inverse * r.gain_one[...]).astype(bf16)

        store(r.n1_gb, r.n1_out)

        load_wkv.wait()
        r.kv[0] = turn(
            dot(r.n1_gb[...], wkv[...]),
            jnp.where(key_lane, r.cos[...], 1.0),
            jnp.where(key_lane, r.sin[...], 0.0),
        ).astype(bf16)
        pl.semaphore_wait(barrier, len(mates))
        for k in (1, 2, 3):
            pl.when(place + k < 4)(kv_copy(k).start)
        if swap:
            swap_n1.start()
            for i, part in ((0, 0), (0, 1), (1, 0)):
                line_sent(0, i, part).start()

        load_wq.wait()

        @pl.loop(0, heads_width // 256)
        def _(i):
            wide = dot(r.n1_gb[...], wq[:, aligned(i, 256)])
            for part in range(2):
                turned = turn(wide[:, 128 * part : 128 * part + 128], r.cos[...], r.sin[...])
                at = pl.ds(pl.multiple_of(i * 256 + 128 * part, 128), 128)
                r.q[:, at] = (turned * (0.125 * log2_e)).astype(bf16)

        def attend_block(k, first):
            mask(bias, k, first)
            block = r.kv[k].astype(f32)
            pad_keys(keys, block)
            vals_t[...] = block.T[64:].astype(bf16)

            @pl.loop(0, heads_width // 128)
            def _(pair):
                pair_q = r.q[:, aligned(pair, 128)]
                for e in range(2):
                    head = pair * 2 + e
                    scores = dot_t(keys[e], pair_q) + bias[...]
                    top = jnp.max(scores, 0, keepdims=True)
                    at = aligned(head, 64)
                    if first:
                        weights = jnp.exp2(scores - top)
                        r.run_sum[head] = jnp.sum(weights, 0, keepdims=True)
                        r.att[at, :] = dot(vals_t[...], weights.astype(bf16))
                    else:
                        old = r.lse[head]
                        top = jnp.maximum(top, old)
                        fade = jnp.exp2(old - top)
                        weights = jnp.exp2(scores - top)
                        r.run_sum[head] = r.run_sum[head] * fade + jnp.sum(weights, 0, keepdims=True)
                        r.att[at, :] = r.att[at, :] * fade + dot(vals_t[...], weights.astype(bf16))
                    r.lse[head] = top

        attend_block(0, True)

        row = lax.broadcasted_iota(jnp.int32, (256, 256), 0)
        column = lax.broadcasted_iota(jnp.int32, (256, 256), 1)
        source = jnp.where(row < 128, 2 * row, 2 * row - 255)
        order = (column == source).astype(bf16)

        @pl.loop(0, width // 128)
        def _(i):
            raw_copy(i).wait()
            at = aligned(i, 128)
            split = dot(order, raw[turn_of(i, ring)].reshape(256, units)).astype(bf16)
            for b in range(units // 128):
                wgu[at, 256 * b : 256 * b + 128] = split[:128, 128 * b : 128 * b + 128]
                wgu[at, 256 * b + 128 : 256 * b + 256] = split[128:, 128 * b : 128 * b + 128]

            @pl.when(i + ring < width // 128)
            def _():
                raw_copy(i + ring).start()

        @pl.loop(1, place + 1)
        def _(k):
            kv_copy(k).wait_recv()
            attend_block(k, False)

        for k in (1, 2, 3):
            pl.when(place + k < 4)(kv_copy(k).wait_send)

        @pl.loop(0, heads_width // 128)
        def _(pair):
            for e in range(2):
                head = pair * 2 + e
                at = aligned(head, 64)
                r.att[at, :] = r.att[at, :] * (1.0 / r.run_sum[head])
                r.lse[head] = r.lse[head] + jnp.log2(r.run_sum[head])
            at = aligned(pair, 128)
            r.att_low[:, at] = r.att[at, :].T.astype(bf16)

    def feed_forward(wgu, g, wdown, acc_gu, acc_down, t_n2, t_g):
        gh = acc_down
        r.t_n2 = t_n2
        load_g = load(r.g_hbm, g)
        load_wdown = load(r.wdown_hbm, wdown)
        load_wout.wait()
        start_sum(0, None, lambda n: dot(r.att_low[...], r.wout[:, aligned(n, 256)]), first=True)
        if swap:
            swap_low.start()

        load_g.wait()
        load_wdown.wait()

        @pl.loop(0, units // 128)
        def _(b):
            at = aligned(b, 128)
            gh[:, at] = dot_t(g[...], wdown[at, :])

        if swap:
            hand_on(0, 1)

        finish_sum(0)
        load_x_own.wait()
        square = jnp.zeros((quarter, 1), f32)
        for c in range(chunks):
            at = slice(c * span, (c + 1) * span)
            part = r.own_fin[0, c] + r.x_own[:, at].astype(f32)
            r.resid[:, at] = part
            square = square + jnp.sum(part * part, -1, keepdims=True)
        inverse = lax.rsqrt(square / width + epsilon)
        r.x_n2[mine, :] = (r.resid[...] * inverse * r.gain_two[...]).astype(bf16)
        to_chip, to_core, onward = gather(3, r.x_n2.at[mine, :], r.x_n2)
        to_chip.start()
        to_core.start()

        def own_to_line(part):
            at = line_parts(0)[part]
            return pltpu.make_async_copy(
                r.x_n2.at[at, :], r.n2_z.at[place, at, :], r.own_sem.at[part]
            )

        if swap:
            own_to_line(0).start()
            own_to_line(0).wait()
            line_sent(1, 0, 0).start()
            pl.when(is_mid)(line_sent(1, 1, 0).start)

        def activations(gate, up, grad):
            sigmoid = 0.5 * jnp.tanh(0.5 * gate) + 0.5
            active = gate * sigmoid
            grad_gate = (grad * up) * (sigmoid + active * (1.0 - sigmoid))
            both = jnp.concatenate([grad_gate, grad * active], 1)
            return (active * up).astype(bf16), both.astype(bf16)

        def units_of(at):
            @pl.loop(0, units // 128)
            def _(b):
                wide = dot(r.x_n2[at, :], wgu[:, aligned(b, 256)])
                hid, gg = activations(wide[:, :128], wide[:, 128:], gh[at, aligned(b, 128)])
                r.hid[at, aligned(b, 128)] = hid
                r.gg[at, aligned(b, 256)] = gg

        to_core.wait_recv()
        units_of(aligned(chip, 2 * quarter))
        to_chip.wait_recv()
        onward.start()
        if swap:
            own_to_line(1).start()
            own_to_line(1).wait()
            line_sent(1, 0, 1).start()
            pl.when(is_end)(line_sent(1, 1, 0).start)
        onward.wait_recv()
        units_of(aligned(1 - chip, 2 * quarter))
        if not swap:
            store(r.x_n2, r.n2_out)
            store(r.hid, r.hid_out)
            store(r.gg, r.gg_out)
            store(r.att_low, r.low_out)
        for copy in (to_chip, to_core, onward):
            copy.wait_send()
        if swap:
            hand_on(0, 2)

        steps = [(at, min(256, units - at)) for at in range(0, units, 256)]
        whole = units // 256

        def each_step(body):
            @pl.loop(0, whole)
            def _(step):
                body(pl.multiple_of(step * 256, 256), 256, step)

            if units % 256:
                body(whole * 256, units - whole * 256, whole)

        def turn_block():
            for t, ref in ((t_n2, r.x_n2), (t_g, g)):
                for i, owner in enumerate((side, 1 - side)):
                    columns = aligned(owner * 4 + place, 256)
                    t[i * 256 : i * 256 + 256, :] = ref[:, columns].astype(f32).T.astype(bf16)

        def own_block():
            turn_block()

            def body(offset, size, step):
                gu, down = pl.ds(2 * offset, 2 * size), pl.ds(offset, size)
                acc_gu[:, gu] = dot(t_n2[...], r.gg[:, gu])
                acc_down[:, down] = dot(t_g[...], r.hid[:, down])

            each_step(body)

        def block_loads(i):
            return (
                pltpu.make_async_copy(r.n2_z.at[peers[i]], r.x_n2, r.block_sem.at[0]),
                pltpu.make_async_copy(r.g_z.at[peers[i]], g, r.block_sem.at[1]),
            )

        def exchange(step, size):
            offset = step * 256
            gu, down = pl.ds(2 * offset, 2 * size), pl.ds(offset, size)
            return tuple(
                remote(
                    ref.at[0:256, at], ref.at[256:512, at], r.side_send.at[step, i],
                    r.side_recv.at[step, i], dp_mate,
                )
                for i, (ref, at) in enumerate(((r.gg, gu), (r.hid, down)))
            )

        def block_start(i):
            for a in range(2):
                spread_wait(a, i)
            for copy in block_loads(i):
                copy.start()

        def other_block(i, last=False):
            for copy in block_loads(i):
                copy.wait()
            turn_block()
            if last:
                pl.semaphore_wait(r.side_credit, 1)

            def body(offset, size, step):
                gu, down = pl.ds(2 * offset, 2 * size), pl.ds(offset, size)
                terms = []
                for h in range(2):
                    at = slice(h * 256, h * 256 + 256)
                    wide = dot(r.x_n2[at, :], wgu[:, gu])
                    grad = dot_t(g[at, :], wdown[down, :])
                    parts = [
                        activations(
                            wide[:, 2 * q : 2 * q + 128],
                            wide[:, 2 * q + 128 : 2 * q + 256],
                            grad[:, q : q + 128],
                        )
                        for q in range(0, size, 128)
                    ]
                    hid = jnp.concatenate([part[0] for part in parts], 1)
                    gg = jnp.concatenate([part[1] for part in parts], 1)
                    terms.append((dot(t_n2[:, at], gg), dot(t_g[:, at], hid)))
                acc_gu[:, gu] += terms[0][0] + terms[1][0]
                acc_down[:, down] += terms[0][1] + terms[1][1]
                if last:
                    r.gg[0:256, gu] = acc_gu[256:512, gu].astype(bf16)
                    r.hid[0:256, down] = acc_down[256:512, down].astype(bf16)

                    @pl.when(step < len(steps) - 1)
                    def _():
                        for copy in exchange(step, size):
                            copy.start()

            each_step(body)

        def last_exchange():
            for copy in exchange(len(steps) - 1, steps[-1][1]):
                copy.start()

        def own_share(first, stop):
            for step in range(first, stop):
                offset, size = steps[step]
                for copy in exchange(step, size):
                    copy.wait_recv()
                gu, down = slice(2 * offset, 2 * (offset + size)), slice(offset, offset + size)
                acc_gu[0:256, gu] += r.gg[256:512, gu].astype(f32)
                acc_down[0:256, down] += r.hid[256:512, down].astype(f32)
                for copy in share_stores(step, offset, size):
                    copy.start()

        def share_stores(step, offset, size):
            gu, down = pl.ds(2 * offset, 2 * size), pl.ds(offset, size)
            return (
                pltpu.make_async_copy(
                    acc_gu.at[0:256, gu], r.dgu_out.at[:, gu], r.share_sem.at[step, 0]
                ),
                pltpu.make_async_copy(
                    acc_down.at[0:256, down], r.dwdown_out.at[:, down], r.share_sem.at[step, 1]
                ),
            )

        def finish_shares():
            for step, (offset, size) in enumerate(steps):
                for copy in exchange(step, size):
                    copy.wait_send()
                for copy in share_stores(step, offset, size):
                    copy.wait()

        store_copy(0).wait()
        if swap:
            swap_n1.wait_send()
        start_sum(0, None, lambda n: dot_t(r.gg[...], wgu[aligned(n, 256), :]))
        if swap:
            own_block()
            hand_on(1, 1)
            spread_start(0, 0)
        r.share_tools = (last_exchange, own_share, finish_shares, len(steps) - 1)
        rest(wdown, block_start, other_block)

    def first_half(wgu):
        pl.run_scoped(
            functools.partial(attention, wgu),
            raw=bf(4, 128, 2, units),
            wq=bf(width, heads_width),
            wkv=bf(width, 128),
            keys=bf(2, rows, 128),
            vals_t=bf(64, rows),
            bias=pltpu.VMEM((rows, rows), f32),
        )
        pl.run_scoped(
            functools.partial(feed_forward, wgu),
            g=bf(rows, width),
            wdown=bf(units, width),
            acc_gu=pltpu.VMEM((rows, 2 * units), f32),
            acc_down=pltpu.VMEM((rows, units), f32),
            t_n2=bf(512, rows),
            t_g=bf(512, rows),
        )

    def slot_qkv(n):
        return pl.multiple_of(turn_of(n, 3) * qkv, 128)

    def tile_qkv(n):
        at, first = aligned(n, 256), slot_qkv(n)
        copies = (
            pltpu.make_async_copy(
                r.wq_hbm.at[at],
                r.wout.at[0:256, pl.ds(first, heads_width)],
                r.w_rows_sem.at[turn_of(n, 3)],
            ),
            pltpu.make_async_copy(
                r.wkv_hbm.at[at],
                r.wout.at[0:256, pl.ds(pl.multiple_of(first + heads_width, 128), 128)],
                r.w_kv_sem.at[turn_of(n, 3)],
            ),
        )
        return types.SimpleNamespace(
            start=lambda: [copy.start() for copy in copies],
            wait=lambda: [copy.wait() for copy in copies],
        )

    def back_through_norm(b, values, gain_ref, gain_row, emit):
        square = jnp.zeros((quarter, 1), f32)
        inner = jnp.zeros((quarter, 1), f32)
        for c in range(chunks):
            at = slice(c * span, (c + 1) * span)
            v = values[:, at].astype(f32)
            square = square + jnp.sum(v * v, -1, keepdims=True)
            inner = inner + jnp.sum(r.own_fin[b, c] * gain_ref[:, at] * v, -1, keepdims=True)
        inverse = lax.rsqrt(square / width + epsilon)
        slope = inner / width * (inverse * inverse * inverse)
        for c in range(chunks):
            at = slice(c * span, (c + 1) * span)
            v = values[:, at].astype(f32)
            dn = r.own_fin[b, c]
            r.gain_sum[0, gain_row : gain_row + 1, at] = jnp.sum(
                dn * v * inverse, 0, keepdims=True
            )
            emit(at, inverse * dn * gain_ref[:, at] - v * slope)

    if swap:
        io_mate, across_mate = {"context": beside}, {"context": 3 - place}
        sets = 2

        def unit(u):
            if u == 0:
                cut = (r.n1_gb.at[:, mine_cols], r.gb_o)
                other = r.other_kept.at[:, 0:heads_width]
                return (cut, r.att_low, other, heads_width, r.dwout_out)
            cut = (r.n1_out.at[:, mine_cols], r.n1_o)
            return (cut, r.gqkv, r.other_kept, qkv, r.dwqkv_out)

        def cut_loads(u):
            own, other = unit(u)[0]
            return (
                pltpu.make_async_copy(own, r.cut.at[0:rows], r.cut_sem.at[0]),
                pltpu.make_async_copy(other, r.cut.at[rows : 2 * rows], r.cut_sem.at[1]),
            )

        def piece(ref, s, j, u):
            return ref.at[s, j, :, 0 : unit(u)[3]]

        def line_copy(u, j, slot, mate):
            s = u % sets
            return remote(
                piece(r.stage, s, j, u), (r.got_out, r.got_qkv)[u].at[slot], r.unit_send.at[s, j],
                r.unit_recv.at[s, slot], mate,
            )

        def result(u):
            return pltpu.make_async_copy(
                r.sums.at[u % sets, :, 0 : unit(u)[3]], unit(u)[4], r.sums_sem.at[u % sets]
            )

        def prepare(u):
            s = u % sets
            own, other, width_u = unit(u)[1], unit(u)[2], unit(u)[3]
            for copy in cut_loads(u):
                copy.wait()

            @pl.loop(0, 4)
            def _(j):
                chunk = jnp.where(
                    j == 0,
                    jnp.where(low_side, 3, 0),
                    jnp.where(
                        j == 1, jnp.where(low_side, 2, 1), jnp.where(j == 2, beside, place)
                    ),
                )
                for i in range(2):
                    cut = r.cut[i * rows : (i + 1) * rows, aligned(chunk, 256)]
                    r.t_n2[i * 256 : i * 256 + 256, :] = cut.astype(f32).T.astype(bf16)

                def block(at):
                    term = dot(r.t_n2[0:256], own[:, at]) + dot(
                        r.t_n2[256:512], other[:, at]
                    )

                    @pl.when(j < 3)
                    def _():
                        r.stage[s, j, :, at] = term.astype(bf16)

                    @pl.when(j == 3)
                    def _():
                        r.sums[s, :, at] = term

                @pl.loop(0, width_u // 256)
                def _(tile):
                    block(aligned(tile, 256))

                if width_u % 256:
                    block(slice(width_u - width_u % 256, width_u))

                @pl.when((j < 3) & is_end)
                def _():
                    line_copy(u, j, j, io_mate).start()

        def add_in(u, j, slot):
            width_u, s = unit(u)[3], u % sets
            line_copy(u, 0, slot, io_mate).wait_recv()

            @pl.loop(0, 4)
            def _(i):
                at = aligned(i, 64)
                total = r.stage[s, j, at, 0:width_u].astype(f32)
                total = total + (r.got_out, r.got_qkv)[u][slot, at, :].astype(f32)
                r.stage[s, j, at, 0:width_u] = total.astype(bf16)

        def pass_on(u, step):
            @pl.when(is_mid)
            def _():
                if step < 2:
                    add_in(u, step, step)
                    line_copy(u, step, 3 + step, across_mate).start()
                else:
                    add_in(u, 2, 3)
                    line_copy(u, 2, 0, io_mate).start()

        def complete(u):
            width_u, s = unit(u)[3], u % sets

            def take(slots):
                for slot in slots:
                    line_copy(u, 0, slot, io_mate).wait_recv()

                @pl.loop(0, 4)
                def _(i):
                    at = aligned(i, 64)
                    total = r.sums[s, at, 0:width_u]
                    for slot in slots:
                        total = total + (r.got_out, r.got_qkv)[u][slot, at, :].astype(f32)
                    r.sums[s, at, 0:width_u] = total

            @pl.when(is_end)
            def _():
                take((0,))

            @pl.when(is_mid)
            def _():
                take((2, 4))

            result(u).start()

    def rest(wdown, block_start, other_block):
        r.wdown = wdown
        r.gain_sum[...] = jnp.zeros_like(r.gain_sum)

        finish_sum(0)
        load_g_own.wait()
        for i in range(1, len(stores)):
            store_copy(i).wait()

        def keep_resid(at, grad):
            r.n1_gb[mine, at] = (r.g_own[:, at].astype(f32) + grad).astype(bf16)

        back_through_norm(0, r.resid, r.gain_two, 1, keep_resid)
        gb_chip, gb_core, gb_onward = gather(0, r.n1_gb.at[mine, :], r.n1_gb)
        gb_chip.start()
        gb_core.start()
        if swap:
            spread_start(1, 0)
        start_sum(0, None, lambda n: dot(r.hid[...], r.wdown[:, aligned(n, 256)]))
        if swap:
            pl.semaphore_signal(r.side_credit, inc=1, device_id=dp_mate, device_id_type=MESH)
            block_start(0)
            other_block(0)
            hand_on(1, 2)
        gb_chip.wait_recv()
        gb_onward.start()
        if swap:
            spread_start(0, 1)
            spread_start(1, 1)
            spread_start(0, 2)
        gb_core.wait_recv()
        gb_onward.wait_recv()
        if swap:
            swap_gb.start()
        else:
            gb_store = pltpu.make_async_copy(r.n1_gb, r.gb_out, r.cut_sem.at[0])
            gb_store.start()
        pl.run_scoped(
            attention_back,
            ga=bf(rows, heads_width),
            bias=fl(rows, rows),
            delta=fl(heads_width // HD, 1, rows),
            keys=bf(2, rows, 128),
            vals=bf(2, rows, 128),
            keys_t=bf(HD, rows),
            dk=fl(2, rows, 128),
            dv=fl(2, rows, 128),
        )
        for n in range(3):
            tile_qkv(n).start()
        last_part = functools.partial(
            closing, block_start, other_block, gb_chip, gb_core, gb_onward
        )
        if swap:
            pl.run_scoped(
                last_part,
                other_kept=bf(rows, qkv),
                cut=bf(2 * rows, width // 2),
                stage=bf(2, 3, 256, qkv),
                sums=fl(2, 256, qkv),
            )
        else:
            last_part()
            gb_store.wait()

    def attention_back(**scoped):
        vars(r).update(scoped)

        for i in range(heads_width // 256):
            at = slice(i * 256, i * 256 + 256)
            r.ga[:, at] = dot_t(r.n1_gb[...], r.wout[at, :]).astype(bf16)

        @pl.loop(0, heads_width // 128)
        def _(pair):
            at = aligned(pair, 128)
            product = r.ga[:, at].astype(f32).T * r.att[at, :]
            for e in range(2):
                r.delta[pair * 2 + e] = jnp.sum(product[64 * e : 64 * e + 64], 0, keepdims=True)

        r.att[...] = jnp.zeros_like(r.att)

        def back_block(k, first):
            mask(r.bias, k, first)
            block = r.kv[k].astype(f32)
            rolled = pltpu.roll(block, 64, 1)
            pad_keys(r.keys, block)
            r.vals[0] = jnp.where(key_lane, rolled, 0.0).astype(bf16)
            r.vals[1] = jnp.where(key_lane, 0.0, block).astype(bf16)
            r.keys_t[...] = block.T[:64].astype(bf16)
            r.dk[...] = jnp.zeros_like(r.dk)
            r.dv[...] = jnp.zeros_like(r.dv)

            @pl.loop(0, heads_width // 128)
            def _(pair):
                pair_q = r.q[:, aligned(pair, 128)]
                pair_ga = r.ga[:, aligned(pair, 128)]
                for e in range(2):
                    head = pair * 2 + e
                    probs = jnp.exp2(dot_t(r.keys[e], pair_q) + r.bias[...] - r.lse[head])
                    grad_probs = dot_t(r.vals[e], pair_ga)
                    grad_scores = (probs * (grad_probs - r.delta[head])).astype(bf16)
                    r.dv[e] += dot(probs.astype(bf16), pair_ga)
                    r.dk[e] += dot(grad_scores, pair_q)
                    r.att[aligned(head, 64), :] += dot(r.keys_t[...], grad_scores)

            return jnp.where(
                key_lane,
                (r.dk[0] + pltpu.roll(r.dk[1], 64, 1)) * (1.0 / log2_e),
                r.dv[1] + pltpu.roll(r.dv[0], 64, 1),
            )

        @pl.loop(0, place)
        def _(i):
            k = place - i
            r.kv[k] = back_block(k, False).astype(bf16)
            dkv_copy(k, i).start()

        r.tmp[:, 0:128] = back_block(0, True)

    def closing(block_start, other_block, gb_chip, gb_core, gb_onward, **scoped):
        vars(r).update(scoped)
        last_exchange, own_share, finish_shares, last_step = r.share_tools
        if swap:
            spread_onward(0, 1)
            spread_start(1, 2)
            swap_low.wait_recv()
            low_load = pltpu.make_async_copy(
                r.low_o, r.other_kept.at[:, 0:heads_width], r.late_sem
            )
            low_load.start()

        @pl.loop(0, heads_width // 128)
        def _(pair):
            at = aligned(pair, 128)
            turned = turn(r.att[at, :].T * 0.125, r.cos[...], -r.sin[...])
            r.gqkv[:, at] = turned.astype(bf16)

        for k in (1, 2, 3):

            @pl.when(place + k < 4)
            def _():
                dkv_copy(k, 0).wait_recv()
                r.tmp[:, 0:128] += r.got_kv[k].astype(f32)

        r.gqkv[:, heads_width : heads_width + 128] = turn(
            r.tmp[:, 0:128],
            jnp.where(key_lane, r.cos[...], 1.0),
            jnp.where(key_lane, -r.sin[...], 0.0),
        ).astype(bf16)
        if swap:
            swap_gqkv.start()
        else:
            gqkv_store = pltpu.make_async_copy(r.gqkv, r.gqkv_out, r.cut_sem.at[1])
            gqkv_store.start()

        if swap:
            spread_onward(1, 1)
            swap_gb.wait_recv()
            for copy in cut_loads(0):
                copy.start()
        finish_sum(0)
        for c in range(chunks):
            at = slice(c * span, (c + 1) * span)
            r.g_own[:, at] = (r.resid[:, at] + r.own_fin[0, c]).astype(bf16)
        mixed_chip, mixed_core, mixed_onward = gather(1, r.g_own, r.mixed_out)
        mixed_store = pltpu.make_async_copy(r.g_own, r.mixed_out.at[mine, :], r.out_sem.at[0])

        start_sum(0, tile_qkv, lambda n: dot_t(r.gqkv[...], r.wout[0:256, pl.ds(slot_qkv(n), qkv)]))
        if swap:
            block_start(1)
            spread_onward(0, 2)
            low_load.wait()
            prepare(0)
            swap_n1.wait_recv()
            for copy in cut_loads(1):
                copy.start()
            other_block(1)
            spread_onward(1, 2)
            swap_gqkv.wait_recv()
            gqkv_load = pltpu.make_async_copy(r.gqkv_o, r.other_kept, r.late_sem)
            gqkv_load.start()
            gqkv_load.wait()
            prepare(1)
            block_start(2)
            pass_on(0, 0)
            other_block(2, last=True)
            pass_on(0, 1)
            pass_on(1, 0)

        finish_sum(0, last=True)

        def keep_tokens(at, grad):
            r.x_own[:, at] = (r.n1_gb[mine, at].astype(f32) + grad).astype(bf16)

        back_through_norm(0, r.x_own, r.gain_one, 0, keep_tokens)
        tokens_chip, tokens_core, tokens_onward = gather(2, r.x_own, r.tokens_out)
        tokens_store = pltpu.make_async_copy(r.x_own, r.tokens_out.at[mine, :], r.out_sem.at[1])

        across_tensor = [
            remote(
                r.gain_sum.at[0], r.gain_got.at[i], r.gain_send.at[i], r.gain_recv.at[i], mate
            )
            for i, mate in enumerate(tensor_mates)
        ]
        for copy in across_tensor:
            copy.start()
        for copy in (tokens_chip, tokens_core, tokens_store, mixed_chip, mixed_core, mixed_store):
            copy.start()
        if swap:
            pass_on(1, 1)
        for copy in across_tensor:
            copy.wait()
        r.gain_sum[1] = (r.gain_sum[0] + r.gain_got[0]) + (r.gain_got[1] + r.gain_got[2])
        if swap:
            part = width // 8
            pieces = []
            for i in range(1, 8):
                to_side = side if i < 4 else 1 - side
                to_place = lax.rem(place + i, 4)
                pieces.append(
                    remote(
                        r.gain_sum.at[1, :, aligned(to_side * 4 + to_place, part)],
                        r.gain_piece.at[i], r.gain_send.at[2 + i], r.gain_recv.at[2 + i],
                        {"dp": to_side, "context": to_place},
                    )
                )
            for copy in pieces:
                copy.start()
            last_exchange()
            pass_on(0, 2)
        else:
            r.gains_out[...] = r.gain_sum[1]
        tokens_chip.wait_recv()
        tokens_onward.start()
        if swap:
            pass_on(1, 2)
            complete(0)
        mixed_chip.wait_recv()
        mixed_onward.start()
        if swap:
            own_share(0, 2)
            complete(1)
            own_share(2, last_step + 1)
            for copy in pieces:
                copy.wait()
            total = r.gain_sum[1, :, aligned(side * 4 + place, part)]
            for i in range(1, 8):
                total = total + r.gain_piece[i]
            r.gains_out[...] = total

        for copy in (mixed_core, mixed_onward, tokens_core, tokens_onward):
            copy.wait_recv()
        for copy in (
            gb_chip, gb_core, gb_onward, mixed_chip, mixed_core, mixed_onward, tokens_chip,
            tokens_core, tokens_onward,
        ):
            copy.wait_send()
        mixed_store.wait()
        tokens_store.wait()
        for k in (1, 2, 3):
            pl.when(place >= k)(dkv_copy(k, 0).wait_send)
        if swap:
            for copy in (swap_low, swap_gb, swap_gqkv):
                copy.wait_send()
            for a in range(2):
                for i in range(3):
                    for copy in spread(a, i):
                        copy.wait_send()
                for i, part in ((0, 0), (0, 1), (1, 0)):
                    line_sent(a, i, part).wait_send()
                for i in (1, 2):
                    pl.when(is_mid)(handed_on(a, i).wait_send)
            finish_shares()
            for u in range(2):
                for j in range(3):
                    line_copy(u, j, 0, io_mate).wait_send()
                result(u).wait()
        else:
            gqkv_store.wait()

    load_wout = load(r.wout_hbm, r.wout)
    load_x_own = load(r.x_hbm.at[mine, :], r.x_own)
    load_g_own = load(r.g_hbm.at[mine, :], r.g_own)
    pl.run_scoped(first_half, pltpu.VMEM((width, 2 * units), bf16))


def layer(swap, inputs, rows, width, units, heads):
    bf16, f32 = jnp.bfloat16, jnp.float32
    quarter = rows // 4
    chunks = 4
    span = width // chunks
    wide = heads * HD
    qkv = wide + 2 * HD
    outs = {
        "mixed_out": ((rows, width), bf16),
        "tokens_out": ((rows, width), bf16),
        "gains_out": ((8, width // 8 if swap else width), f32),
        "n1_out": ((rows, width), bf16),
    }
    if swap:
        outs |= {
            "dwdown_out": ((width // 8, units), f32),
            "dgu_out": ((width // 8, 2 * units), f32),
            "dwout_out": ((width // 8, wide), f32),
            "dwqkv_out": ((width // 8, qkv), f32),
            "g_z": ((4, rows, width), bf16),
            "n2_z": ((4, rows, width), bf16),
            "low_o": ((rows, wide), bf16),
            "gqkv_o": ((rows, qkv), bf16),
            "gb_o": ((rows, width // 2), bf16),
            "n1_o": ((rows, width // 2), bf16),
        }
    else:
        outs |= {
            "gb_out": ((rows, width), bf16),
            "gqkv_out": ((rows, qkv), bf16),
            "n2_out": ((rows, width), bf16),
            "hid_out": ((rows, units), bf16),
            "gg_out": ((rows, 2 * units), bf16),
            "low_out": ((rows, wide), bf16),
        }
    scratch = {
        "x_n2": ((rows, width), bf16),
        "n1_gb": ((rows, width), bf16),
        "wout": ((wide, width), bf16),
        "q": ((rows, wide), bf16),
        "kv": ((4, rows, 2 * HD), bf16),
        "att": ((wide, rows), f32),
        "att_low": ((rows, wide), bf16),
        "lse": ((heads, 1, rows), f32),
        "run_sum": ((heads, 1, rows), f32),
        "cos": ((rows, 2 * HD), f32),
        "sin": ((rows, 2 * HD), f32),
        "resid": ((quarter, width), f32),
        "g_own": ((quarter, width), bf16),
        "x_own": ((quarter, width), bf16),
        "hid": ((rows, units), bf16),
        "gg": ((rows, 2 * units), bf16),
        "tmp": ((rows, 256), f32),
        "stage_core": ((1, chunks, 2, quarter, span), bf16),
        "got_core": ((1, chunks, 2, quarter, span), bf16),
        "own_fwd": ((chunks, quarter, span), bf16),
        "own_fin": ((1, chunks, quarter, span), f32),
        "stage_x": ((1, chunks, quarter, span), bf16),
        "got_x": ((1, chunks, quarter, span), bf16),
        "got_kv": ((4, rows, 2 * HD), bf16),
        "gqkv": ((rows, qkv), bf16),
        "gain_sum": ((2, 8, width), f32),
        "gain_got": ((3, 8, width), f32),
    }
    if swap:
        scratch |= {
            "got_out": ((5, width // 8, wide), bf16),
            "got_qkv": ((5, width // 8, qkv), bf16),
            "gain_piece": ((8, 8, width // 8), f32),
        }
    sems = {
        "load_sem": (8,),
        "store_sem": (5,),
        "raw_sem": (4,),
        "w_rows_sem": (3,),
        "w_kv_sem": (3,),
        "core_send": (1, chunks),
        "core_recv": (1, chunks),
        "x_send": (1, chunks),
        "x_recv": (1, chunks),
        "ag_send": (10, 3),
        "ag_recv": (10, 3),
        "kv_send": (4,),
        "kv_recv": (4,),
        "dkv_send": (4,),
        "dkv_recv": (4,),
        "gain_send": (10,),
        "gain_recv": (10,),
        "out_sem": (2,),
        "cut_sem": (2,),
        "late_sem": (),
    }
    if swap:
        sems |= {
            "dp_send": (4,),
            "dp_recv": (4,),
            "line_send": (2, 4, 2),
            "line_recv": (2, 4, 2),
            "hand_send": (2, 2),
            "hand_recv": (2, 2),
            "own_sem": (2,),
            "block_sem": (2,),
            "side_send": (-(-units // 256), 2),
            "side_recv": (-(-units // 256), 2),
            "share_sem": (-(-units // 256), 2),
            "unit_send": (2, 3),
            "unit_recv": (2, 5),
            "sums_sem": (2,),
        }
    credits = ["core_credit", "x_credit", *(["side_credit"] if swap else [])]
    names = [*inputs, *outs, *scratch, *sems, *credits]
    anywhere = pl.BlockSpec(memory_space=pl.ANY)
    inside = pl.BlockSpec(memory_space=pltpu.VMEM)
    results = pl.pallas_call(
        functools.partial(layer_kernel, names, swap),
        out_shape=[jax.ShapeDtypeStruct(*out) for out in outs.values()],
        in_specs=[anywhere if name.endswith("_hbm") else inside for name in inputs],
        out_specs=[inside if name == "gains_out" else anywhere for name in outs],
        scratch_shapes=[
            *(pltpu.VMEM(*shape) for shape in scratch.values()),
            *(pltpu.SemaphoreType.DMA(shape) for shape in sems.values()),
            *(pltpu.SemaphoreType.REGULAR for _ in credits),
        ],
        compiler_params=pltpu.CompilerParams(
            collective_id=0, has_side_effects=True, vmem_limit_bytes=int(63.5 * MIB)
        ),
        name="layer",
    )(*inputs.values())
    return dict(zip(outs, results, strict=True))


def finish_kernel(
    down_hbm, gateup_hbm, out_hbm, qkv_hbm, tokens_hbm, mixed_hbm, gains,
    down_o, gateup_o, out_o, q_o, kv_o, tokens_o, mixed_o, gain_one_o, gain_two_o,
    down, gateup, out, qkv, tokens, mixed, down_t, gateup_t, out_t, kv_t, tokens_t,
    load_sem, store_sem,
):
    wide = q_o.shape[1]
    parts = 4
    loads, stores = [], []

    def load(src, dst):
        copy = pltpu.make_async_copy(src, dst, load_sem.at[len(loads)])
        copy.start()
        loads.append(copy)
        return copy

    def store(src, dst):
        copy = pltpu.make_async_copy(src, dst, store_sem.at[len(stores)])
        copy.start()
        stores.append(copy)

    def piece(ref, i):
        size = ref.shape[0] // parts
        return ref.at[i * size : (i + 1) * size]

    gain_one_o[...] = gains[0:1, :]
    gain_two_o[...] = gains[1:2, :]
    token_loads = [load(piece(tokens_hbm, i), piece(tokens, i)) for i in range(parts)]
    gateup_loads = [load(piece(gateup_hbm, i), piece(gateup, i)) for i in range(parts)]
    load_mixed = load(mixed_hbm, mixed)
    load_down = load(down_hbm, down)
    load_qkv = load(qkv_hbm, qkv)
    load_out = load(out_hbm, out)
    for i in range(parts):
        token_loads[i].wait()
        piece(tokens_t, i)[...] = piece(tokens, i)[...].astype(jnp.float32)
        store(piece(tokens_t, i), piece(tokens_o, i))
    for i in range(parts):
        gateup_loads[i].wait()
        values, target = piece(gateup, i), piece(gateup_t, i)
        for b in range(gateup.shape[1] // 256):
            at = slice(b * 128, b * 128 + 128)
            target[:, 0, at] = values[:, b * 256 : b * 256 + 128]
            target[:, 1, at] = values[:, b * 256 + 128 : b * 256 + 256]
        store(target, piece(gateup_o, i))
    load_mixed.wait()
    store(mixed, mixed_o)
    load_down.wait()
    for i in range(down.shape[1] // 128):
        at = slice(i * 128, i * 128 + 128)
        down_t[at, :] = down[:, at].T
    store(down_t, down_o)
    load_qkv.wait()
    store(qkv.at[:, 0:wide], q_o)
    kv_t[:, 0, :] = qkv[:, wide:]
    store(kv_t, kv_o)
    load_out.wait()
    for i in range(wide // 128):
        at = slice(i * 128, i * 128 + 128)
        out_t[at, :] = out[:, at].T
    store(out_t, out_o)
    for copy in stores:
        copy.wait()


def finish(down, gateup, out, qkv, tokens, mixed, gains):
    depth, units = down.shape
    wide = out.shape[1]
    rows, width = tokens.shape
    bf16, f32 = jnp.bfloat16, jnp.float32
    outs = [
        ((units, depth), f32),
        ((depth, 2, units), f32),
        ((wide, depth), f32),
        ((depth, wide), f32),
        ((depth, 1, 2 * HD), f32),
        ((rows, width), f32),
        ((rows, width), bf16),
        ((1, depth), f32),
        ((1, depth), f32),
    ]
    scratch = [
        *((array.shape, array.dtype) for array in (down, gateup, out, qkv, tokens, mixed)),
        *outs[:3],
        *outs[4:6],
    ]
    anywhere = pl.BlockSpec(memory_space=pl.ANY)
    inside = pl.BlockSpec(memory_space=pltpu.VMEM)
    return pl.pallas_call(
        finish_kernel,
        out_shape=[jax.ShapeDtypeStruct(*entry) for entry in outs],
        in_specs=[*[anywhere] * 6, inside],
        out_specs=[*[anywhere] * 7, inside, inside],
        scratch_shapes=[
            *(pltpu.VMEM(*entry) for entry in scratch),
            pltpu.SemaphoreType.DMA((12,)),
            pltpu.SemaphoreType.DMA((13,)),
        ],
        compiler_params=pltpu.CompilerParams(vmem_limit_bytes=62 * MIB),
        name="finish",
    )(down, gateup, out, qkv, tokens, mixed, gains)


def pick(array, index, axis):
    return lax.dynamic_index_in_dim(array, index, axis, keepdims=False)


def line_sum(part):
    place = lax.axis_index("context")
    order = jnp.array([[3, 2, 1, 0], [3, 2, 0, 1], [0, 1, 3, 2], [0, 1, 2, 3]], jnp.int32)[place]
    first, second, third, own = (part(order[i]) for i in range(4))

    def inward(array):
        return lax.ppermute(array.astype(jnp.bfloat16), "context", [(0, 1), (3, 2)])

    def across(array):
        return lax.ppermute(array.astype(jnp.bfloat16), "context", [(1, 2), (2, 1)])

    def outward(array):
        return lax.ppermute(array.astype(jnp.bfloat16), "context", [(1, 0), (2, 3)])

    in_one, in_two, in_three = inward(first), inward(second), inward(third)
    over_two = across(first + in_one.astype(jnp.float32))
    over_three = across(second + in_two.astype(jnp.float32))
    out_three = outward(third + over_two.astype(jnp.float32))
    return (
        own
        + in_three.astype(jnp.float32)
        + over_three.astype(jnp.float32)
        + out_three.astype(jnp.float32)
    )


def weight_grad(left, right, axis):
    whole = lax.dot_general(
        left, right, (((0,), (0,)), ((), ())), preferred_element_type=jnp.float32
    )
    mine = lax.psum_scatter(
        whole.astype(jnp.bfloat16), "dp", scatter_dimension=axis, tiled=True
    )
    step = mine.shape[axis] // 4
    return line_sum(
        lambda chunk: lax.dynamic_slice_in_dim(mine, chunk * step, step, axis).astype(jnp.float32)
    )


def shards(
    tokens, segments, gain_one, w_query, w_keyval, w_out, gain_two, w_gateup, w_down, cotangent
):
    num_seqs, tok_count, model_width = tokens.shape
    heads_kv = w_keyval.shape[1]
    width_q = w_query.shape[1]
    units = w_down.shape[0]
    swap = lax.axis_size("dp") == 2
    freqs = 10000.0 ** (-(np.arange(HD // 2, dtype=np.float32) * 2.0) / HD)
    g = cotangent.reshape(tok_count, model_width)
    inputs = {
        "seg": segments,
        "freqs": jnp.asarray(freqs.astype(np.float32)[:, None]),
        "gain_one": gain_one[None],
        "gain_two": gain_two[None],
        "x_hbm": tokens.reshape(tok_count, model_width),
        "g_hbm": g,
        "wq_hbm": w_query,
        "wkv_hbm": w_keyval.reshape(model_width, 2 * HD),
        "wout_hbm": w_out,
        "wgateup_hbm": w_gateup,
        "wdown_hbm": w_down,
    }
    out = layer(swap, inputs, tok_count, model_width, units, width_q // HD)
    if swap:
        sent_wdown, sent_gateup, sent_wout, sent_wq, sent_wkv, grad_tokens, mixed, *gains = finish(
            *(out[name] for name in ("dwdown_out", "dgu_out", "dwout_out", "dwqkv_out")),
            *(out[name] for name in ("tokens_out", "mixed_out", "gains_out")),
        )
    else:
        gains = lax.psum_scatter(
            out["gains_out"], ("dp", "context"), scatter_dimension=1, tiled=True
        )
        sent_wdown = weight_grad(out["hid_out"], g, 1)
        sent_gateup = weight_grad(out["n2_out"], out["gg_out"], 0)
        sent_wout = weight_grad(out["low_out"], out["gb_out"], 1)
        sent_wqkv = weight_grad(out["n1_out"], out["gqkv_out"], 0)
        sent_wq, sent_wkv = sent_wqkv[:, :width_q], sent_wqkv[:, width_q:]
        sent_gateup = sent_gateup.reshape(-1, units // 128, 2, 128).transpose(0, 2, 1, 3)
        grad_tokens, mixed = out["tokens_out"].astype(jnp.float32), out["mixed_out"]
    return (
        mixed.reshape(tokens.shape),
        grad_tokens.reshape(tokens.shape),
        gains[0].reshape(-1),
        sent_wq,
        sent_wkv.reshape(-1, heads_kv, 2 * HD),
        sent_wout,
        gains[1].reshape(-1),
        sent_gateup.reshape(-1, 2, units),
        sent_wdown,
    )


def solution(mesh):
    return jax.shard_map(
        shards,
        mesh=mesh,
        in_specs=(
            P("dp", "context", None),
            P("dp", "context"),
            P(),
            P(None, "tensor"),
            P(None, "tensor", None),
            P("tensor", None),
            P(),
            P(None, None, "tensor"),
            P("tensor", None),
            P("dp", "context", None),
        ),
        out_specs=(
            P("dp", "context", None),
            P("dp", "context", None),
            P(("dp", "context")),
            P(("dp", "context"), "tensor"),
            P(("dp", "context"), "tensor", None),
            P("tensor", ("dp", "context")),
            P(("dp", "context")),
            P(("dp", "context"), None, "tensor"),
            P("tensor", ("dp", "context")),
        ),
        check_vma=False,
    )
```

```python
import functools
import types

import jax
import jax.numpy as jnp
import numpy as np
from jax import lax
from jax.experimental import pallas as pl
from jax.experimental.pallas import tpu as pltpu
from jax.sharding import PartitionSpec as P

HD = 64


epsilon = 1e-05
neg_large = -1e30


MESH = pl.DeviceIdType.MESH
MIB = 1 << 20
log2_e = 1.4426950408889634


def dot(left, right):
    return jnp.dot(left, right, preferred_element_type=jnp.float32)


def dot_t(left, right):
    return lax.dot_general(left, right, (((1,), (1,)), ((), ())), preferred_element_type=jnp.float32)


def lanes(shape):
    return lax.broadcasted_iota(jnp.int32, shape, len(shape) - 1)


def turn_of(n, size):
    return n % size if isinstance(n, int) else lax.rem(n, size)


def aligned(index, size):
    if isinstance(index, int):
        return pl.ds(index * size, size)
    return pl.ds(pl.multiple_of(index * size, size), size)


def turn(values, cosine, sine):
    low_half = lax.rem(lanes(values.shape), 64) < 32
    swapped = jnp.where(low_half, pltpu.roll(values, 96, 1), pltpu.roll(values, 32, 1))
    return values * cosine + swapped * sine


def cos_sin(phase):
    count = jnp.floor(phase * 0.6366197723675814 + 0.5)
    rest = phase - count * 1.5703125
    rest = rest - count * 0.0004837512969970703
    rest = rest - count * 7.549789954e-08
    square = rest * rest
    sine = rest + rest * square * (
        -0.16666666666 + square * (0.0083333333333 + square * -0.0001984126984)
    )
    cosine = 1.0 + square * (
        -0.5 + square * (0.041666666666 + square * (-0.0013888888889 + square * 2.48015873e-05))
    )
    place = count - 4.0 * jnp.floor(count * 0.25)
    odd = (place == 1.0) | (place == 3.0)
    first, second = jnp.where(odd, sine, cosine), jnp.where(odd, cosine, sine)
    return (
        jnp.where((place == 1.0) | (place == 2.0), -first, first),
        jnp.where(place >= 2.0, -second, second),
    )


def layer_kernel(names, swap, *refs):
    r = types.SimpleNamespace(**dict(zip(names, refs, strict=True)))
    rows, width = r.x_n2.shape
    quarter = rows // 4
    units = r.hid.shape[1]
    heads_width = r.q.shape[1]
    f32, bf16 = jnp.float32, jnp.bfloat16
    tensor = lax.axis_index("tensor")
    place = lax.axis_index("context")
    core, chip = lax.rem(tensor, 2), lax.div(tensor, 2)
    core_mate = {"tensor": chip * 2 + 1 - core}
    chip_mate = {"tensor": (1 - chip) * 2 + core}
    tensor_mates = (core_mate, chip_mate, {"tensor": (1 - chip) * 2 + 1 - core})
    mates = [*tensor_mates, *({"context": lax.rem(place + k, 4)} for k in (1, 2, 3))]
    if swap:
        side = lax.axis_index("dp")
        dp_mate = {"dp": 1 - side}
        mates += [dp_mate]
        mates += [{"dp": 1 - side, "context": lax.rem(place + k, 4)} for k in (1, 2, 3)]
    mine = aligned(tensor, quarter)
    key_lane = lanes((rows, 128)) < 64
    qkv = heads_width + 128
    bf = lambda *shape: pltpu.VMEM(shape, bf16)
    fl = lambda *shape: pltpu.VMEM(shape, f32)

    barrier = pltpu.get_barrier_semaphore()
    for mate in mates:
        pl.semaphore_signal(barrier, inc=1, device_id=mate, device_id_type=MESH)

    def remote(src, dst, send, recv, mate):
        return pltpu.make_async_remote_copy(
            src_ref=src, dst_ref=dst, send_sem=send, recv_sem=recv, device_id=mate,
            device_id_type=MESH,
        )

    loads, stores = [], []

    def load(src, dst, now=True):
        copy = pltpu.make_async_copy(src, dst, r.load_sem.at[len(loads)])
        loads.append(copy)
        if now:
            copy.start()
        return copy

    def store_copy(i):
        return pltpu.make_async_copy(*stores[i], r.store_sem.at[i])

    def store(src, dst):
        stores.append((src, dst))
        store_copy(len(stores) - 1).start()

    swaps = []

    def swap_copy(src, dst):
        i = len(swaps)
        swaps.append(remote(src, dst, r.dp_send.at[i], r.dp_recv.at[i], dp_mate))
        return swaps[i]

    if swap:
        half = width // 2
        theirs_cols, mine_cols = aligned(1 - side, half), aligned(side, half)
        swap_n1 = swap_copy(r.n1_gb.at[:, theirs_cols], r.n1_o)
        swap_low = swap_copy(r.att_low, r.low_o)
        swap_gb = swap_copy(r.n1_gb.at[:, theirs_cols], r.gb_o)
        swap_gqkv = swap_copy(r.gqkv, r.gqkv_o)

    is_end = (place == 0) | (place == 3)
    is_mid = jnp.logical_not(is_end)
    low_side = place < 2
    beside = place + 1 - 2 * lax.rem(place, 2)
    peers = (beside, jnp.where(low_side, 2, 1), jnp.where(low_side, 3, 0))
    other_quarter = aligned(chip_mate["tensor"], quarter)

    def line_parts(i):
        return (mine, other_quarter) if i == 0 else (mine,)

    def line_sent(a, i, part):
        src, dst = ((r.g_hbm, r.g_z), (r.n2_z.at[place], r.n2_z))[a]
        step = lax.rem(peers[i] - place + 4, 4)
        at = line_parts(i)[part]
        return remote(
            src.at[at, :], dst.at[place, at, :], r.line_send.at[a, step, part],
            r.line_recv.at[a, step, part], {"context": peers[i]},
        )

    def line_got(a, i, part):
        dst = (r.g_z, r.n2_z)[a].at[peers[i], line_parts(i)[part], :]
        step = lax.rem(place - peers[i] + 4, 4)
        return remote(
            dst, dst, r.line_send.at[a, step, part], r.line_recv.at[a, step, part],
            {"context": peers[i]},
        )

    def handed_on(a, i):
        block = (r.g_z, r.n2_z)[a].at[peers[i], mine, :]
        return remote(
            block, block, r.hand_send.at[a, i - 1], r.hand_recv.at[a, i - 1], {"context": beside}
        )

    def hand_on(a, i):
        @pl.when(is_mid)
        def _():
            line_got(a, i, 0).wait_recv()
            handed_on(a, i).start()

    def spread(a, i):
        block = (r.g_z, r.n2_z)[a].at[peers[i]]
        slot = 4 + a * 3 + i
        if i > 0:
            return gather(slot, block.at[mine, :], block)
        return tuple(
            remote(
                block.at[at, :], block.at[at, :], r.ag_send.at[slot, part],
                r.ag_recv.at[slot, part], core_mate,
            )
            for part, at in enumerate(line_parts(0))
        )

    def spread_start(a, i):
        copies = spread(a, i)
        if i > 0:
            pl.when(is_end)(handed_on(a, i).wait_recv)
        else:
            for part in range(2):
                line_got(a, 0, part).wait_recv()
        for copy in copies[:2]:
            copy.start()

    def spread_onward(a, i):
        if i > 0:
            copies = spread(a, i)
            copies[0].wait_recv()
            copies[2].start()

    def spread_wait(a, i):
        copies = spread(a, i)
        for copy in copies[1:] if i > 0 else copies:
            copy.wait_recv()

    chunks = r.own_fin.shape[1]
    span = r.own_fin.shape[3]

    def core_copy(b, c):
        return remote(
            r.stage_core.at[b, c], r.got_core.at[b, c], r.core_send.at[b, c],
            r.core_recv.at[b, c], core_mate,
        )

    def x_copy(b, c):
        return remote(
            r.stage_x.at[b, c], r.got_x.at[b, c], r.x_send.at[b, c], r.x_recv.at[b, c], chip_mate
        )

    def start_sum(b, tile, product, first=False):
        if not first:
            pl.semaphore_wait(r.core_credit, 1)
            pl.semaphore_wait(r.x_credit, 1)

        def put(ref, index, at, value):
            ref[(*index, slice(None), at)] = value.astype(ref.dtype)

        routes = (
            ((1 - chip) * 2 + 1 - core, lambda c, at, v: put(r.stage_core, (b, c, 0), at, v)),
            (chip * 2 + 1 - core, lambda c, at, v: put(r.stage_core, (b, c, 1), at, v)),
            ((1 - chip) * 2 + core, lambda c, at, v: put(r.own_fwd, (c,), at, v)),
            (chip * 2 + core, lambda c, at, v: put(r.own_fin, (b, c), at, v)),
        )

        def forward_chunk(c):
            core_copy(b, c).wait_recv()
            total = r.own_fwd[c].astype(f32) + r.got_core[b, c, 0].astype(f32)
            r.stage_x[b, c] = total.astype(bf16)
            x_copy(b, c).start()

        @pl.loop(0, chunks)
        def _(c):
            for t in range(span // 256):
                n = c * (span // 256) + t
                if tile is not None:
                    tile(n).wait()
                r.tmp[...] = product(n)
                for owner, route in routes:
                    route(c, slice(t * 256, t * 256 + 256), r.tmp[aligned(owner, quarter), :])
                if tile is not None:

                    @pl.when(n + 3 < width // 256)
                    def _():
                        tile(n + 3).start()

            core_copy(b, c).start()
            pl.when(c > 1)(lambda: forward_chunk(c - 2))

        forward_chunk(chunks - 2)
        forward_chunk(chunks - 1)

    def finish_sum(b, last=False):
        for c in range(chunks):
            x_copy(b, c).wait_recv()
            r.own_fin[b, c] = (
                r.own_fin[b, c] + r.got_core[b, c, 1].astype(f32) + r.got_x[b, c].astype(f32)
            )
        for c in range(chunks):
            core_copy(b, c).wait_send()
            x_copy(b, c).wait_send()
        if not last:
            pl.semaphore_signal(r.core_credit, inc=1, device_id=core_mate, device_id_type=MESH)
            pl.semaphore_signal(r.x_credit, inc=1, device_id=chip_mate, device_id_type=MESH)

    def gather(i, src, dst):
        def copy(slot, src, owner, mate):
            return remote(
                src, dst.at[aligned(owner, quarter), :], r.ag_send.at[i, slot],
                r.ag_recv.at[i, slot], mate,
            )

        other = chip_mate["tensor"]
        return (
            copy(0, src, tensor, chip_mate),
            copy(1, src, tensor, core_mate),
            copy(2, dst.at[aligned(other, quarter), :], other, core_mate),
        )

    def mask(bias, k, first):
        key_index = (place - k) * rows + lax.broadcasted_iota(jnp.int32, (rows, rows), 0)
        allowed = key_index >= r.seg[...]
        if first:
            query_index = place * rows + lax.broadcasted_iota(jnp.int32, (rows, rows), 1)
            allowed = allowed & (key_index <= query_index)
        bias[...] = jnp.where(allowed, 0.0, neg_large)

    def pad_keys(keys, block):
        keys[0] = jnp.where(key_lane, block, 0.0).astype(bf16)
        keys[1] = jnp.where(key_lane, 0.0, pltpu.roll(block, 64, 1)).astype(bf16)

    def kv_copy(k):
        return remote(
            r.kv.at[0], r.kv.at[k], r.kv_send.at[k], r.kv_recv.at[k],
            {"context": lax.rem(place + k, 4)},
        )

    def dkv_copy(k, mate):
        return remote(
            r.kv.at[k], r.got_kv.at[k], r.dkv_send.at[k], r.dkv_recv.at[k], {"context": mate}
        )

    def attention(wgu, raw, wq, wkv, keys, vals_t, bias):
        load_x = load(r.x_hbm, r.x_n2)
        load_wkv = load(r.wkv_hbm, wkv)
        load_wq = load(r.wq_hbm, wq)
        ring = raw.shape[0]

        def raw_copy(i):
            slot = turn_of(i, ring)
            return pltpu.make_async_copy(
                r.wgateup_hbm.at[aligned(i, 128)], raw.at[slot], r.raw_sem.at[slot]
            )

        for i in range(ring):
            raw_copy(i).start()

        for copy in (load_wout, load_x_own, load_g_own):
            copy.start()

        position = place * rows + lanes((1, rows)) - r.seg[...]
        cosine, sine = cos_sin(r.freqs[...] * position.astype(f32))
        r.cos[...] = jnp.concatenate([cosine] * 4, 0).T
        r.sin[...] = jnp.concatenate([-sine, sine] * 2, 0).T

        load_x.wait()

        @pl.loop(0, rows // 64)
        def _(i):
            at = aligned(i, 64)
            values = r.x_n2[at, :].astype(f32)
            inverse = lax.rsqrt(jnp.mean(values * values, -1, keepdims=True) + epsilon)
            r.n1_gb[at, :] = (values * inverse * r.gain_one[...]).astype(bf16)

        store(r.n1_gb, r.n1_out)

        load_wkv.wait()
        r.kv[0] = turn(
            dot(r.n1_gb[...], wkv[...]),
            jnp.where(key_lane, r.cos[...], 1.0),
            jnp.where(key_lane, r.sin[...], 0.0),
        ).astype(bf16)
        pl.semaphore_wait(barrier, len(mates))
        for k in (1, 2, 3):
            pl.when(place + k < 4)(kv_copy(k).start)
        if swap:
            swap_n1.start()
            for i, part in ((0, 0), (0, 1), (1, 0)):
                line_sent(0, i, part).start()

        load_wq.wait()

        @pl.loop(0, heads_width // 256)
        def _(i):
            wide = dot(r.n1_gb[...], wq[:, aligned(i, 256)])
            for part in range(2):
                turned = turn(wide[:, 128 * part : 128 * part + 128], r.cos[...], r.sin[...])
                at = pl.ds(pl.multiple_of(i * 256 + 128 * part, 128), 128)
                r.q[:, at] = (turned * (0.125 * log2_e)).astype(bf16)

        def attend_block(k, first):
            mask(bias, k, first)
            block = r.kv[k].astype(f32)
            pad_keys(keys, block)
            vals_t[...] = block.T[64:].astype(bf16)

            @pl.loop(0, heads_width // 128)
            def _(pair):
                pair_q = r.q[:, aligned(pair, 128)]
                for e in range(2):
                    head = pair * 2 + e
                    scores = dot_t(keys[e], pair_q) + bias[...]
                    top = jnp.max(scores, 0, keepdims=True)
                    at = aligned(head, 64)
                    if first:
                        weights = jnp.exp2(scores - top)
                        r.run_sum[head] = jnp.sum(weights, 0, keepdims=True)
                        r.att[at, :] = dot(vals_t[...], weights.astype(bf16))
                    else:
                        old = r.lse[head]
                        top = jnp.maximum(top, old)
                        fade = jnp.exp2(old - top)
                        weights = jnp.exp2(scores - top)
                        r.run_sum[head] = r.run_sum[head] * fade + jnp.sum(weights, 0, keepdims=True)
                        r.att[at, :] = r.att[at, :] * fade + dot(vals_t[...], weights.astype(bf16))
                    r.lse[head] = top

        attend_block(0, True)

        row = lax.broadcasted_iota(jnp.int32, (256, 256), 0)
        column = lax.broadcasted_iota(jnp.int32, (256, 256), 1)
        source = jnp.where(row < 128, 2 * row, 2 * row - 255)
        order = (column == source).astype(bf16)

        @pl.loop(0, width // 128)
        def _(i):
            raw_copy(i).wait()
            at = aligned(i, 128)
            split = dot(order, raw[turn_of(i, ring)].reshape(256, units)).astype(bf16)
            for b in range(units // 128):
                wgu[at, 256 * b : 256 * b + 128] = split[:128, 128 * b : 128 * b + 128]
                wgu[at, 256 * b + 128 : 256 * b + 256] = split[128:, 128 * b : 128 * b + 128]

            @pl.when(i + ring < width // 128)
            def _():
                raw_copy(i + ring).start()

        @pl.loop(1, place + 1)
        def _(k):
            kv_copy(k).wait_recv()
            attend_block(k, False)

        for k in (1, 2, 3):
            pl.when(place + k < 4)(kv_copy(k).wait_send)

        @pl.loop(0, heads_width // 128)
        def _(pair):
            for e in range(2):
                head = pair * 2 + e
                at = aligned(head, 64)
                r.att[at, :] = r.att[at, :] * (1.0 / r.run_sum[head])
                r.lse[head] = r.lse[head] + jnp.log2(r.run_sum[head])
            at = aligned(pair, 128)
            r.att_low[:, at] = r.att[at, :].T.astype(bf16)

    def feed_forward(wgu, g, wdown, acc_gu, acc_down, t_n2, t_g):
        gh = acc_down
        r.t_n2 = t_n2
        load_g = load(r.g_hbm, g)
        load_wdown = load(r.wdown_hbm, wdown)
        load_wout.wait()
        start_sum(0, None, lambda n: dot(r.att_low[...], r.wout[:, aligned(n, 256)]), first=True)
        if swap:
            swap_low.start()

        load_g.wait()
        load_wdown.wait()

        @pl.loop(0, units // 128)
        def _(b):
            at = aligned(b, 128)
            gh[:, at] = dot_t(g[...], wdown[at, :])

        if swap:
            hand_on(0, 1)

        finish_sum(0)
        load_x_own.wait()
        square = jnp.zeros((quarter, 1), f32)
        for c in range(chunks):
            at = slice(c * span, (c + 1) * span)
            part = r.own_fin[0, c] + r.x_own[:, at].astype(f32)
            r.resid[:, at] = part
            square = square + jnp.sum(part * part, -1, keepdims=True)
        inverse = lax.rsqrt(square / width + epsilon)
        r.x_n2[mine, :] = (r.resid[...] * inverse * r.gain_two[...]).astype(bf16)
        to_chip, to_core, onward = gather(3, r.x_n2.at[mine, :], r.x_n2)
        to_chip.start()
        to_core.start()

        def own_to_line(part):
            at = line_parts(0)[part]
            return pltpu.make_async_copy(
                r.x_n2.at[at, :], r.n2_z.at[place, at, :], r.own_sem.at[part]
            )

        if swap:
            own_to_line(0).start()
            own_to_line(0).wait()
            line_sent(1, 0, 0).start()
            pl.when(is_mid)(line_sent(1, 1, 0).start)

        def activations(gate, up, grad):
            sigmoid = 0.5 * jnp.tanh(0.5 * gate) + 0.5
            active = gate * sigmoid
            grad_gate = (grad * up) * (sigmoid + active * (1.0 - sigmoid))
            both = jnp.concatenate([grad_gate, grad * active], 1)
            return (active * up).astype(bf16), both.astype(bf16)

        def units_of(at):
            @pl.loop(0, units // 128)
            def _(b):
                wide = dot(r.x_n2[at, :], wgu[:, aligned(b, 256)])
                hid, gg = activations(wide[:, :128], wide[:, 128:], gh[at, aligned(b, 128)])
                r.hid[at, aligned(b, 128)] = hid
                r.gg[at, aligned(b, 256)] = gg

        to_core.wait_recv()
        units_of(aligned(chip, 2 * quarter))
        to_chip.wait_recv()
        onward.start()
        if swap:
            own_to_line(1).start()
            own_to_line(1).wait()
            line_sent(1, 0, 1).start()
            pl.when(is_end)(line_sent(1, 1, 0).start)
        onward.wait_recv()
        units_of(aligned(1 - chip, 2 * quarter))
        if not swap:
            store(r.x_n2, r.n2_out)
            store(r.hid, r.hid_out)
            store(r.gg, r.gg_out)
            store(r.att_low, r.low_out)
        for copy in (to_chip, to_core, onward):
            copy.wait_send()
        if swap:
            hand_on(0, 2)

        steps = [(at, min(256, units - at)) for at in range(0, units, 256)]
        whole = units // 256

        def each_step(body, pause=None):
            first = 0
            if pause is not None:
                first = (whole + 1) // 2

                @pl.loop(0, first)
                def _(step):
                    body(pl.multiple_of(step * 256, 256), 256, step)

                pause()

            @pl.loop(first, whole)
            def _(step):
                body(pl.multiple_of(step * 256, 256), 256, step)

            if units % 256:
                body(whole * 256, units - whole * 256, whole)

        def turn_block():
            for t, ref in ((t_n2, r.x_n2), (t_g, g)):
                for i, owner in enumerate((side, 1 - side)):
                    columns = aligned(owner * 4 + place, 256)
                    t[i * 256 : i * 256 + 256, :] = ref[:, columns].astype(f32).T.astype(bf16)

        def own_block():
            turn_block()

            def body(offset, size, step):
                gu, down = pl.ds(2 * offset, 2 * size), pl.ds(offset, size)
                acc_gu[:, gu] = dot(t_n2[...], r.gg[:, gu])
                acc_down[:, down] = dot(t_g[...], r.hid[:, down])

            each_step(body)

        def block_loads(i):
            return (
                pltpu.make_async_copy(r.n2_z.at[peers[i]], r.x_n2, r.block_sem.at[0]),
                pltpu.make_async_copy(r.g_z.at[peers[i]], g, r.block_sem.at[1]),
            )

        def exchange(step, size):
            offset = step * 256
            gu, down = pl.ds(2 * offset, 2 * size), pl.ds(offset, size)
            return tuple(
                remote(
                    ref.at[0:256, at], ref.at[256:512, at], r.side_send.at[step, i],
                    r.side_recv.at[step, i], dp_mate,
                )
                for i, (ref, at) in enumerate(((r.gg, gu), (r.hid, down)))
            )

        def block_start(i):
            for a in range(2):
                spread_wait(a, i)
            for copy in block_loads(i):
                copy.start()

        def other_block(i, last=False, pause=None):
            for copy in block_loads(i):
                copy.wait()
            turn_block()
            if last:
                pl.semaphore_wait(r.side_credit, 1)

            def body(offset, size, step):
                gu, down = pl.ds(2 * offset, 2 * size), pl.ds(offset, size)
                terms = []
                for h in range(2):
                    at = slice(h * 256, h * 256 + 256)
                    wide = dot(r.x_n2[at, :], wgu[:, gu])
                    grad = dot_t(g[at, :], wdown[down, :])
                    parts = [
                        activations(
                            wide[:, 2 * q : 2 * q + 128],
                            wide[:, 2 * q + 128 : 2 * q + 256],
                            grad[:, q : q + 128],
                        )
                        for q in range(0, size, 128)
                    ]
                    hid = jnp.concatenate([part[0] for part in parts], 1)
                    gg = jnp.concatenate([part[1] for part in parts], 1)
                    terms.append((dot(t_n2[:, at], gg), dot(t_g[:, at], hid)))
                acc_gu[:, gu] += terms[0][0] + terms[1][0]
                acc_down[:, down] += terms[0][1] + terms[1][1]
                if last:
                    r.gg[0:256, gu] = acc_gu[256:512, gu].astype(bf16)
                    r.hid[0:256, down] = acc_down[256:512, down].astype(bf16)

                    @pl.when(step < len(steps) - 1)
                    def _():
                        for copy in exchange(step, size):
                            copy.start()

            each_step(body, pause)

        def last_exchange():
            for copy in exchange(len(steps) - 1, steps[-1][1]):
                copy.start()

        def own_share(first, stop):
            for step in range(first, stop):
                offset, size = steps[step]
                for copy in exchange(step, size):
                    copy.wait_recv()
                gu, down = slice(2 * offset, 2 * (offset + size)), slice(offset, offset + size)
                acc_gu[0:256, gu] += r.gg[256:512, gu].astype(f32)
                acc_down[0:256, down] += r.hid[256:512, down].astype(f32)
                for copy in share_stores(step, offset, size):
                    copy.start()

        def share_stores(step, offset, size):
            gu, down = pl.ds(2 * offset, 2 * size), pl.ds(offset, size)
            return (
                pltpu.make_async_copy(
                    acc_gu.at[0:256, gu], r.dgu_out.at[:, gu], r.share_sem.at[step, 0]
                ),
                pltpu.make_async_copy(
                    acc_down.at[0:256, down], r.dwdown_out.at[:, down], r.share_sem.at[step, 1]
                ),
            )

        def finish_shares():
            for step, (offset, size) in enumerate(steps):
                for copy in exchange(step, size):
                    copy.wait_send()
                for copy in share_stores(step, offset, size):
                    copy.wait()

        store_copy(0).wait()
        if swap:
            swap_n1.wait_send()
        start_sum(0, None, lambda n: dot_t(r.gg[...], wgu[aligned(n, 256), :]))
        if swap:
            own_block()
            hand_on(1, 1)
            spread_start(0, 0)
        r.share_tools = (last_exchange, own_share, finish_shares, len(steps) - 1)
        rest(wdown, block_start, other_block)

    def first_half(wgu):
        pl.run_scoped(
            functools.partial(attention, wgu),
            raw=bf(4, 128, 2, units),
            wq=bf(width, heads_width),
            wkv=bf(width, 128),
            keys=bf(2, rows, 128),
            vals_t=bf(64, rows),
            bias=pltpu.VMEM((rows, rows), f32),
        )
        pl.run_scoped(
            functools.partial(feed_forward, wgu),
            g=bf(rows, width),
            wdown=bf(units, width),
            acc_gu=pltpu.VMEM((rows, 2 * units), f32),
            acc_down=pltpu.VMEM((rows, units), f32),
            t_n2=bf(512, rows),
            t_g=bf(512, rows),
        )

    def slot_qkv(n):
        return pl.multiple_of(turn_of(n, 3) * qkv, 128)

    def tile_qkv(n):
        at, first = aligned(n, 256), slot_qkv(n)
        copies = (
            pltpu.make_async_copy(
                r.wq_hbm.at[at],
                r.wout.at[0:256, pl.ds(first, heads_width)],
                r.w_rows_sem.at[turn_of(n, 3)],
            ),
            pltpu.make_async_copy(
                r.wkv_hbm.at[at],
                r.wout.at[0:256, pl.ds(pl.multiple_of(first + heads_width, 128), 128)],
                r.w_kv_sem.at[turn_of(n, 3)],
            ),
        )
        return types.SimpleNamespace(
            start=lambda: [copy.start() for copy in copies],
            wait=lambda: [copy.wait() for copy in copies],
        )

    def back_through_norm(b, values, gain_ref, gain_row, emit):
        square = jnp.zeros((quarter, 1), f32)
        inner = jnp.zeros((quarter, 1), f32)
        for c in range(chunks):
            at = slice(c * span, (c + 1) * span)
            v = values[:, at].astype(f32)
            square = square + jnp.sum(v * v, -1, keepdims=True)
            inner = inner + jnp.sum(r.own_fin[b, c] * gain_ref[:, at] * v, -1, keepdims=True)
        inverse = lax.rsqrt(square / width + epsilon)
        slope = inner / width * (inverse * inverse * inverse)
        for c in range(chunks):
            at = slice(c * span, (c + 1) * span)
            v = values[:, at].astype(f32)
            dn = r.own_fin[b, c]
            r.gain_sum[0, gain_row : gain_row + 1, at] = jnp.sum(
                dn * v * inverse, 0, keepdims=True
            )
            emit(at, inverse * dn * gain_ref[:, at] - v * slope)

    if swap:
        io_mate, across_mate = {"context": beside}, {"context": 3 - place}
        sets = 2

        def unit(u):
            if u == 0:
                cut = (r.n1_gb.at[:, mine_cols], r.gb_o)
                other = r.other_kept.at[:, 0:heads_width]
                return (cut, r.att_low, other, heads_width, r.dwout_out)
            cut = (r.n1_out.at[:, mine_cols], r.n1_o)
            return (cut, r.gqkv, r.other_kept, qkv, r.dwqkv_out)

        def cut_loads(u):
            own, other = unit(u)[0]
            return (
                pltpu.make_async_copy(own, r.cut.at[0:rows], r.cut_sem.at[0]),
                pltpu.make_async_copy(other, r.cut.at[rows : 2 * rows], r.cut_sem.at[1]),
            )

        def piece(ref, s, j, u):
            return ref.at[s, j, :, 0 : unit(u)[3]]

        def line_copy(u, j, slot, mate):
            s = u % sets
            return remote(
                piece(r.stage, s, j, u), (r.got_out, r.got_qkv)[u].at[slot], r.unit_send.at[s, j],
                r.unit_recv.at[s, slot], mate,
            )

        def result(u):
            return pltpu.make_async_copy(
                r.sums.at[u % sets, :, 0 : unit(u)[3]], unit(u)[4], r.sums_sem.at[u % sets]
            )

        def prepare(u):
            s = u % sets
            own, other, width_u = unit(u)[1], unit(u)[2], unit(u)[3]
            for copy in cut_loads(u):
                copy.wait()

            @pl.loop(0, 4)
            def _(j):
                chunk = jnp.where(
                    j == 0,
                    jnp.where(low_side, 3, 0),
                    jnp.where(
                        j == 1, jnp.where(low_side, 2, 1), jnp.where(j == 2, beside, place)
                    ),
                )
                for i in range(2):
                    cut = r.cut[i * rows : (i + 1) * rows, aligned(chunk, 256)]
                    r.t_n2[i * 256 : i * 256 + 256, :] = cut.astype(f32).T.astype(bf16)

                def block(at):
                    term = dot(r.t_n2[0:256], own[:, at]) + dot(
                        r.t_n2[256:512], other[:, at]
                    )

                    @pl.when(j < 3)
                    def _():
                        r.stage[s, j, :, at] = term.astype(bf16)

                    @pl.when(j == 3)
                    def _():
                        r.sums[s, :, at] = term

                @pl.loop(0, width_u // 256)
                def _(tile):
                    block(aligned(tile, 256))

                if width_u % 256:
                    block(slice(width_u - width_u % 256, width_u))

                @pl.when((j < 3) & is_end)
                def _():
                    line_copy(u, j, j, io_mate).start()

        def add_in(u, j, slot):
            width_u, s = unit(u)[3], u % sets
            line_copy(u, 0, slot, io_mate).wait_recv()

            @pl.loop(0, 4)
            def _(i):
                at = aligned(i, 64)
                total = r.stage[s, j, at, 0:width_u].astype(f32)
                total = total + (r.got_out, r.got_qkv)[u][slot, at, :].astype(f32)
                r.stage[s, j, at, 0:width_u] = total.astype(bf16)

        def pass_on(u, step):
            @pl.when(is_mid)
            def _():
                if step < 2:
                    add_in(u, step, step)
                    line_copy(u, step, 3 + step, across_mate).start()
                else:
                    add_in(u, 2, 3)
                    line_copy(u, 2, 0, io_mate).start()

        def complete(u):
            width_u, s = unit(u)[3], u % sets

            def take(slots):
                for slot in slots:
                    line_copy(u, 0, slot, io_mate).wait_recv()

                @pl.loop(0, 4)
                def _(i):
                    at = aligned(i, 64)
                    total = r.sums[s, at, 0:width_u]
                    for slot in slots:
                        total = total + (r.got_out, r.got_qkv)[u][slot, at, :].astype(f32)
                    r.sums[s, at, 0:width_u] = total

            @pl.when(is_end)
            def _():
                take((0,))

            @pl.when(is_mid)
            def _():
                take((2, 4))

            result(u).start()

    def rest(wdown, block_start, other_block):
        r.wdown = wdown
        r.gain_sum[...] = jnp.zeros_like(r.gain_sum)

        finish_sum(0)
        load_g_own.wait()
        for i in range(1, len(stores)):
            store_copy(i).wait()

        def keep_resid(at, grad):
            r.n1_gb[mine, at] = (r.g_own[:, at].astype(f32) + grad).astype(bf16)

        back_through_norm(0, r.resid, r.gain_two, 1, keep_resid)
        gb_chip, gb_core, gb_onward = gather(0, r.n1_gb.at[mine, :], r.n1_gb)
        gb_chip.start()
        gb_core.start()
        if swap:
            spread_start(1, 0)
        start_sum(0, None, lambda n: dot(r.hid[...], r.wdown[:, aligned(n, 256)]))
        if swap:
            pl.semaphore_signal(r.side_credit, inc=1, device_id=dp_mate, device_id_type=MESH)
            block_start(0)

            def pause():
                gb_chip.wait_recv()
                gb_onward.start()
                spread_start(0, 1)
                spread_start(1, 1)

            other_block(0, pause=pause)
            hand_on(1, 2)
            spread_start(0, 2)
        else:
            gb_chip.wait_recv()
            gb_onward.start()
        gb_core.wait_recv()
        gb_onward.wait_recv()
        if swap:
            swap_gb.start()
        else:
            gb_store = pltpu.make_async_copy(r.n1_gb, r.gb_out, r.cut_sem.at[0])
            gb_store.start()
        pl.run_scoped(
            attention_back,
            ga=bf(rows, heads_width),
            bias=fl(rows, rows),
            delta=fl(heads_width // HD, 1, rows),
            keys=bf(2, rows, 128),
            vals=bf(2, rows, 128),
            keys_t=bf(HD, rows),
            dk=fl(2, rows, 128),
            dv=fl(2, rows, 128),
        )
        for n in range(3):
            tile_qkv(n).start()
        last_part = functools.partial(
            closing, block_start, other_block, gb_chip, gb_core, gb_onward
        )
        if swap:
            pl.run_scoped(
                last_part,
                other_kept=bf(rows, qkv),
                cut=bf(2 * rows, width // 2),
                stage=bf(2, 3, 256, qkv),
                sums=fl(2, 256, qkv),
            )
        else:
            last_part()
            gb_store.wait()

    def attention_back(**scoped):
        vars(r).update(scoped)

        for i in range(heads_width // 256):
            at = slice(i * 256, i * 256 + 256)
            r.ga[:, at] = dot_t(r.n1_gb[...], r.wout[at, :]).astype(bf16)

        @pl.loop(0, heads_width // 128)
        def _(pair):
            at = aligned(pair, 128)
            product = r.ga[:, at].astype(f32).T * r.att[at, :]
            for e in range(2):
                r.delta[pair * 2 + e] = jnp.sum(product[64 * e : 64 * e + 64], 0, keepdims=True)

        r.att[...] = jnp.zeros_like(r.att)

        def back_block(k, first):
            mask(r.bias, k, first)
            block = r.kv[k].astype(f32)
            rolled = pltpu.roll(block, 64, 1)
            pad_keys(r.keys, block)
            r.vals[0] = jnp.where(key_lane, rolled, 0.0).astype(bf16)
            r.vals[1] = jnp.where(key_lane, 0.0, block).astype(bf16)
            r.keys_t[...] = block.T[:64].astype(bf16)
            r.dk[...] = jnp.zeros_like(r.dk)
            r.dv[...] = jnp.zeros_like(r.dv)

            @pl.loop(0, heads_width // 128)
            def _(pair):
                pair_q = r.q[:, aligned(pair, 128)]
                pair_ga = r.ga[:, aligned(pair, 128)]
                for e in range(2):
                    head = pair * 2 + e
                    probs = jnp.exp2(dot_t(r.keys[e], pair_q) + r.bias[...] - r.lse[head])
                    grad_probs = dot_t(r.vals[e], pair_ga)
                    grad_scores = (probs * (grad_probs - r.delta[head])).astype(bf16)
                    r.dv[e] += dot(probs.astype(bf16), pair_ga)
                    r.dk[e] += dot(grad_scores, pair_q)
                    r.att[aligned(head, 64), :] += dot(r.keys_t[...], grad_scores)

            return jnp.where(
                key_lane,
                (r.dk[0] + pltpu.roll(r.dk[1], 64, 1)) * (1.0 / log2_e),
                r.dv[1] + pltpu.roll(r.dv[0], 64, 1),
            )

        @pl.loop(0, place)
        def _(i):
            k = place - i
            r.kv[k] = back_block(k, False).astype(bf16)
            dkv_copy(k, i).start()

        r.tmp[:, 0:128] = back_block(0, True)

    def closing(block_start, other_block, gb_chip, gb_core, gb_onward, **scoped):
        vars(r).update(scoped)
        last_exchange, own_share, finish_shares, last_step = r.share_tools
        if swap:
            spread_onward(0, 1)
            spread_start(1, 2)
            swap_low.wait_recv()
            low_load = pltpu.make_async_copy(
                r.low_o, r.other_kept.at[:, 0:heads_width], r.late_sem
            )

        @pl.loop(0, heads_width // 128)
        def _(pair):
            at = aligned(pair, 128)
            turned = turn(r.att[at, :].T * 0.125, r.cos[...], -r.sin[...])
            r.gqkv[:, at] = turned.astype(bf16)

        for k in (1, 2, 3):

            @pl.when(place + k < 4)
            def _():
                dkv_copy(k, 0).wait_recv()
                r.tmp[:, 0:128] += r.got_kv[k].astype(f32)

        r.gqkv[:, heads_width : heads_width + 128] = turn(
            r.tmp[:, 0:128],
            jnp.where(key_lane, r.cos[...], 1.0),
            jnp.where(key_lane, -r.sin[...], 0.0),
        ).astype(bf16)
        if swap:
            swap_gqkv.start()
        else:
            gqkv_store = pltpu.make_async_copy(r.gqkv, r.gqkv_out, r.cut_sem.at[1])
            gqkv_store.start()

        finish_sum(0)
        for c in range(chunks):
            at = slice(c * span, (c + 1) * span)
            r.g_own[:, at] = (r.resid[:, at] + r.own_fin[0, c]).astype(bf16)
        mixed_chip, mixed_core, mixed_onward = gather(1, r.g_own, r.mixed_out)
        mixed_store = pltpu.make_async_copy(r.g_own, r.mixed_out.at[mine, :], r.out_sem.at[0])

        start_sum(0, tile_qkv, lambda n: dot_t(r.gqkv[...], r.wout[0:256, pl.ds(slot_qkv(n), qkv)]))
        if swap:
            spread_onward(1, 1)
            swap_n1.wait_recv()
            for copy in cut_loads(1):
                copy.start()
            block_start(1)
            spread_onward(0, 2)
            other_block(1)
            spread_onward(1, 2)
            swap_gqkv.wait_recv()
            gqkv_load = pltpu.make_async_copy(r.gqkv_o, r.other_kept, r.late_sem)
            gqkv_load.start()
            gqkv_load.wait()
            block_start(2)
            prepare(1)
            swap_gb.wait_recv()
            for copy in (*cut_loads(0), low_load):
                copy.start()
            other_block(2, last=True)
            low_load.wait()
            prepare(0)
            pass_on(1, 0)
            pass_on(1, 1)

        finish_sum(0, last=True)

        def keep_tokens(at, grad):
            r.x_own[:, at] = (r.n1_gb[mine, at].astype(f32) + grad).astype(bf16)

        back_through_norm(0, r.x_own, r.gain_one, 0, keep_tokens)
        tokens_chip, tokens_core, tokens_onward = gather(2, r.x_own, r.tokens_out)
        tokens_store = pltpu.make_async_copy(r.x_own, r.tokens_out.at[mine, :], r.out_sem.at[1])

        across_tensor = [
            remote(
                r.gain_sum.at[0], r.gain_got.at[i], r.gain_send.at[i], r.gain_recv.at[i], mate
            )
            for i, mate in enumerate(tensor_mates)
        ]
        for copy in across_tensor:
            copy.start()
        for copy in (tokens_chip, tokens_core, tokens_store, mixed_chip, mixed_core, mixed_store):
            copy.start()
        if swap:
            pass_on(0, 0)
        for copy in across_tensor:
            copy.wait()
        r.gain_sum[1] = (r.gain_sum[0] + r.gain_got[0]) + (r.gain_got[1] + r.gain_got[2])
        if swap:
            part = width // 8
            pieces = []
            for i in range(1, 8):
                to_side = side if i < 4 else 1 - side
                to_place = lax.rem(place + i, 4)
                pieces.append(
                    remote(
                        r.gain_sum.at[1, :, aligned(to_side * 4 + to_place, part)],
                        r.gain_piece.at[i], r.gain_send.at[2 + i], r.gain_recv.at[2 + i],
                        {"dp": to_side, "context": to_place},
                    )
                )
            for copy in pieces:
                copy.start()
            last_exchange()
            pass_on(1, 2)
        else:
            r.gains_out[...] = r.gain_sum[1]
        tokens_chip.wait_recv()
        tokens_onward.start()
        if swap:
            pass_on(0, 1)
            complete(1)
        mixed_chip.wait_recv()
        mixed_onward.start()
        if swap:
            own_share(0, 1)
            pass_on(0, 2)
            own_share(1, 3)
            complete(0)
            own_share(3, last_step + 1)
            for copy in pieces:
                copy.wait()
            total = r.gain_sum[1, :, aligned(side * 4 + place, part)]
            for i in range(1, 8):
                total = total + r.gain_piece[i]
            r.gains_out[...] = total

        for copy in (mixed_core, mixed_onward, tokens_core, tokens_onward):
            copy.wait_recv()
        for copy in (
            gb_chip, gb_core, gb_onward, mixed_chip, mixed_core, mixed_onward, tokens_chip,
            tokens_core, tokens_onward,
        ):
            copy.wait_send()
        mixed_store.wait()
        tokens_store.wait()
        for k in (1, 2, 3):
            pl.when(place >= k)(dkv_copy(k, 0).wait_send)
        if swap:
            for copy in (swap_low, swap_gb, swap_gqkv):
                copy.wait_send()
            for a in range(2):
                for i in range(3):
                    for copy in spread(a, i):
                        copy.wait_send()
                for i, part in ((0, 0), (0, 1), (1, 0)):
                    line_sent(a, i, part).wait_send()
                for i in (1, 2):
                    pl.when(is_mid)(handed_on(a, i).wait_send)
            finish_shares()
            for u in range(2):
                for j in range(3):
                    line_copy(u, j, 0, io_mate).wait_send()
                result(u).wait()
        else:
            gqkv_store.wait()

    load_wout = load(r.wout_hbm, r.wout, False)
    load_x_own = load(r.x_hbm.at[mine, :], r.x_own, False)
    load_g_own = load(r.g_hbm.at[mine, :], r.g_own, False)
    pl.run_scoped(first_half, pltpu.VMEM((width, 2 * units), bf16))


def layer(swap, inputs, rows, width, units, heads):
    bf16, f32 = jnp.bfloat16, jnp.float32
    quarter = rows // 4
    chunks = 4
    span = width // chunks
    wide = heads * HD
    qkv = wide + 2 * HD
    outs = {
        "mixed_out": ((rows, width), bf16),
        "tokens_out": ((rows, width), bf16),
        "gains_out": ((8, width // 8 if swap else width), f32),
        "n1_out": ((rows, width), bf16),
    }
    if swap:
        outs |= {
            "dwdown_out": ((width // 8, units), f32),
            "dgu_out": ((width // 8, 2 * units), f32),
            "dwout_out": ((width // 8, wide), f32),
            "dwqkv_out": ((width // 8, qkv), f32),
            "g_z": ((4, rows, width), bf16),
            "n2_z": ((4, rows, width), bf16),
            "low_o": ((rows, wide), bf16),
            "gqkv_o": ((rows, qkv), bf16),
            "gb_o": ((rows, width // 2), bf16),
            "n1_o": ((rows, width // 2), bf16),
        }
    else:
        outs |= {
            "gb_out": ((rows, width), bf16),
            "gqkv_out": ((rows, qkv), bf16),
            "n2_out": ((rows, width), bf16),
            "hid_out": ((rows, units), bf16),
            "gg_out": ((rows, 2 * units), bf16),
            "low_out": ((rows, wide), bf16),
        }
    scratch = {
        "x_n2": ((rows, width), bf16),
        "n1_gb": ((rows, width), bf16),
        "wout": ((wide, width), bf16),
        "q": ((rows, wide), bf16),
        "kv": ((4, rows, 2 * HD), bf16),
        "att": ((wide, rows), f32),
        "att_low": ((rows, wide), bf16),
        "lse": ((heads, 1, rows), f32),
        "run_sum": ((heads, 1, rows), f32),
        "cos": ((rows, 2 * HD), f32),
        "sin": ((rows, 2 * HD), f32),
        "resid": ((quarter, width), f32),
        "g_own": ((quarter, width), bf16),
        "x_own": ((quarter, width), bf16),
        "hid": ((rows, units), bf16),
        "gg": ((rows, 2 * units), bf16),
        "tmp": ((rows, 256), f32),
        "stage_core": ((1, chunks, 2, quarter, span), bf16),
        "got_core": ((1, chunks, 2, quarter, span), bf16),
        "own_fwd": ((chunks, quarter, span), bf16),
        "own_fin": ((1, chunks, quarter, span), f32),
        "stage_x": ((1, chunks, quarter, span), bf16),
        "got_x": ((1, chunks, quarter, span), bf16),
        "got_kv": ((4, rows, 2 * HD), bf16),
        "gqkv": ((rows, qkv), bf16),
        "gain_sum": ((2, 8, width), f32),
        "gain_got": ((3, 8, width), f32),
    }
    if swap:
        scratch |= {
            "got_out": ((5, width // 8, wide), bf16),
            "got_qkv": ((5, width // 8, qkv), bf16),
            "gain_piece": ((8, 8, width // 8), f32),
        }
    sems = {
        "load_sem": (8,),
        "store_sem": (5,),
        "raw_sem": (4,),
        "w_rows_sem": (3,),
        "w_kv_sem": (3,),
        "core_send": (1, chunks),
        "core_recv": (1, chunks),
        "x_send": (1, chunks),
        "x_recv": (1, chunks),
        "ag_send": (10, 3),
        "ag_recv": (10, 3),
        "kv_send": (4,),
        "kv_recv": (4,),
        "dkv_send": (4,),
        "dkv_recv": (4,),
        "gain_send": (10,),
        "gain_recv": (10,),
        "out_sem": (2,),
        "cut_sem": (2,),
        "late_sem": (),
    }
    if swap:
        sems |= {
            "dp_send": (4,),
            "dp_recv": (4,),
            "line_send": (2, 4, 2),
            "line_recv": (2, 4, 2),
            "hand_send": (2, 2),
            "hand_recv": (2, 2),
            "own_sem": (2,),
            "block_sem": (2,),
            "side_send": (-(-units // 256), 2),
            "side_recv": (-(-units // 256), 2),
            "share_sem": (-(-units // 256), 2),
            "unit_send": (2, 3),
            "unit_recv": (2, 5),
            "sums_sem": (2,),
        }
    credits = ["core_credit", "x_credit", *(["side_credit"] if swap else [])]
    names = [*inputs, *outs, *scratch, *sems, *credits]
    anywhere = pl.BlockSpec(memory_space=pl.ANY)
    inside = pl.BlockSpec(memory_space=pltpu.VMEM)
    results = pl.pallas_call(
        functools.partial(layer_kernel, names, swap),
        out_shape=[jax.ShapeDtypeStruct(*out) for out in outs.values()],
        in_specs=[anywhere if name.endswith("_hbm") else inside for name in inputs],
        out_specs=[inside if name == "gains_out" else anywhere for name in outs],
        scratch_shapes=[
            *(pltpu.VMEM(*shape) for shape in scratch.values()),
            *(pltpu.SemaphoreType.DMA(shape) for shape in sems.values()),
            *(pltpu.SemaphoreType.REGULAR for _ in credits),
        ],
        compiler_params=pltpu.CompilerParams(
            collective_id=0, has_side_effects=True, vmem_limit_bytes=int(63.5 * MIB)
        ),
        name="layer",
    )(*inputs.values())
    return dict(zip(outs, results, strict=True))


def finish_kernel(
    down_hbm, gateup_hbm, out_hbm, qkv_hbm, tokens_hbm, mixed_hbm, gains,
    down_o, gateup_o, out_o, q_o, kv_o, tokens_o, mixed_o, gain_one_o, gain_two_o,
    down, gateup, out, qkv, tokens, mixed, down_t, gateup_t, out_t, kv_t, tokens_t,
    load_sem, store_sem,
):
    wide = q_o.shape[1]
    parts = 4
    loads, stores = [], []

    def load(src, dst):
        copy = pltpu.make_async_copy(src, dst, load_sem.at[len(loads)])
        copy.start()
        loads.append(copy)
        return copy

    def store(src, dst):
        copy = pltpu.make_async_copy(src, dst, store_sem.at[len(stores)])
        copy.start()
        stores.append(copy)

    def piece(ref, i):
        size = ref.shape[0] // parts
        return ref.at[i * size : (i + 1) * size]

    gain_one_o[...] = gains[0:1, :]
    gain_two_o[...] = gains[1:2, :]
    token_loads = [load(piece(tokens_hbm, i), piece(tokens, i)) for i in range(parts)]
    gateup_loads = [load(piece(gateup_hbm, i), piece(gateup, i)) for i in range(parts)]
    load_mixed = load(mixed_hbm, mixed)
    load_down = load(down_hbm, down)
    load_qkv = load(qkv_hbm, qkv)
    load_out = load(out_hbm, out)
    for i in range(parts):
        token_loads[i].wait()
        piece(tokens_t, i)[...] = piece(tokens, i)[...].astype(jnp.float32)
        store(piece(tokens_t, i), piece(tokens_o, i))
    for i in range(parts):
        gateup_loads[i].wait()
        values, target = piece(gateup, i), piece(gateup_t, i)
        for b in range(gateup.shape[1] // 256):
            at = slice(b * 128, b * 128 + 128)
            target[:, 0, at] = values[:, b * 256 : b * 256 + 128]
            target[:, 1, at] = values[:, b * 256 + 128 : b * 256 + 256]
        store(target, piece(gateup_o, i))
    load_mixed.wait()
    store(mixed, mixed_o)
    load_down.wait()
    for i in range(down.shape[1] // 128):
        at = slice(i * 128, i * 128 + 128)
        down_t[at, :] = down[:, at].T
    store(down_t, down_o)
    load_qkv.wait()
    store(qkv.at[:, 0:wide], q_o)
    kv_t[:, 0, :] = qkv[:, wide:]
    store(kv_t, kv_o)
    load_out.wait()
    for i in range(wide // 128):
        at = slice(i * 128, i * 128 + 128)
        out_t[at, :] = out[:, at].T
    store(out_t, out_o)
    for copy in stores:
        copy.wait()


def finish(down, gateup, out, qkv, tokens, mixed, gains):
    depth, units = down.shape
    wide = out.shape[1]
    rows, width = tokens.shape
    bf16, f32 = jnp.bfloat16, jnp.float32
    outs = [
        ((units, depth), f32),
        ((depth, 2, units), f32),
        ((wide, depth), f32),
        ((depth, wide), f32),
        ((depth, 1, 2 * HD), f32),
        ((rows, width), f32),
        ((rows, width), bf16),
        ((1, depth), f32),
        ((1, depth), f32),
    ]
    scratch = [
        *((array.shape, array.dtype) for array in (down, gateup, out, qkv, tokens, mixed)),
        *outs[:3],
        *outs[4:6],
    ]
    anywhere = pl.BlockSpec(memory_space=pl.ANY)
    inside = pl.BlockSpec(memory_space=pltpu.VMEM)
    return pl.pallas_call(
        finish_kernel,
        out_shape=[jax.ShapeDtypeStruct(*entry) for entry in outs],
        in_specs=[*[anywhere] * 6, inside],
        out_specs=[*[anywhere] * 7, inside, inside],
        scratch_shapes=[
            *(pltpu.VMEM(*entry) for entry in scratch),
            pltpu.SemaphoreType.DMA((12,)),
            pltpu.SemaphoreType.DMA((13,)),
        ],
        compiler_params=pltpu.CompilerParams(vmem_limit_bytes=62 * MIB),
        name="finish",
    )(down, gateup, out, qkv, tokens, mixed, gains)


def pick(array, index, axis):
    return lax.dynamic_index_in_dim(array, index, axis, keepdims=False)


def line_sum(part):
    place = lax.axis_index("context")
    order = jnp.array([[3, 2, 1, 0], [3, 2, 0, 1], [0, 1, 3, 2], [0, 1, 2, 3]], jnp.int32)[place]
    first, second, third, own = (part(order[i]) for i in range(4))

    def inward(array):
        return lax.ppermute(array.astype(jnp.bfloat16), "context", [(0, 1), (3, 2)])

    def across(array):
        return lax.ppermute(array.astype(jnp.bfloat16), "context", [(1, 2), (2, 1)])

    def outward(array):
        return lax.ppermute(array.astype(jnp.bfloat16), "context", [(1, 0), (2, 3)])

    in_one, in_two, in_three = inward(first), inward(second), inward(third)
    over_two = across(first + in_one.astype(jnp.float32))
    over_three = across(second + in_two.astype(jnp.float32))
    out_three = outward(third + over_two.astype(jnp.float32))
    return (
        own
        + in_three.astype(jnp.float32)
        + over_three.astype(jnp.float32)
        + out_three.astype(jnp.float32)
    )


def weight_grad(left, right, axis):
    whole = lax.dot_general(
        left, right, (((0,), (0,)), ((), ())), preferred_element_type=jnp.float32
    )
    mine = lax.psum_scatter(
        whole.astype(jnp.bfloat16), "dp", scatter_dimension=axis, tiled=True
    )
    step = mine.shape[axis] // 4
    return line_sum(
        lambda chunk: lax.dynamic_slice_in_dim(mine, chunk * step, step, axis).astype(jnp.float32)
    )


def shards(
    tokens, segments, gain_one, w_query, w_keyval, w_out, gain_two, w_gateup, w_down, cotangent
):
    num_seqs, tok_count, model_width = tokens.shape
    heads_kv = w_keyval.shape[1]
    width_q = w_query.shape[1]
    units = w_down.shape[0]
    swap = lax.axis_size("dp") == 2
    freqs = 10000.0 ** (-(np.arange(HD // 2, dtype=np.float32) * 2.0) / HD)
    g = cotangent.reshape(tok_count, model_width)
    inputs = {
        "seg": segments,
        "freqs": jnp.asarray(freqs.astype(np.float32)[:, None]),
        "gain_one": gain_one[None],
        "gain_two": gain_two[None],
        "x_hbm": tokens.reshape(tok_count, model_width),
        "g_hbm": g,
        "wq_hbm": w_query,
        "wkv_hbm": w_keyval.reshape(model_width, 2 * HD),
        "wout_hbm": w_out,
        "wgateup_hbm": w_gateup,
        "wdown_hbm": w_down,
    }
    out = layer(swap, inputs, tok_count, model_width, units, width_q // HD)
    if swap:
        sent_wdown, sent_gateup, sent_wout, sent_wq, sent_wkv, grad_tokens, mixed, *gains = finish(
            *(out[name] for name in ("dwdown_out", "dgu_out", "dwout_out", "dwqkv_out")),
            *(out[name] for name in ("tokens_out", "mixed_out", "gains_out")),
        )
    else:
        gains = lax.psum_scatter(
            out["gains_out"], ("dp", "context"), scatter_dimension=1, tiled=True
        )
        sent_wdown = weight_grad(out["hid_out"], g, 1)
        sent_gateup = weight_grad(out["n2_out"], out["gg_out"], 0)
        sent_wout = weight_grad(out["low_out"], out["gb_out"], 1)
        sent_wqkv = weight_grad(out["n1_out"], out["gqkv_out"], 0)
        sent_wq, sent_wkv = sent_wqkv[:, :width_q], sent_wqkv[:, width_q:]
        sent_gateup = sent_gateup.reshape(-1, units // 128, 2, 128).transpose(0, 2, 1, 3)
        grad_tokens, mixed = out["tokens_out"].astype(jnp.float32), out["mixed_out"]
    return (
        mixed.reshape(tokens.shape),
        grad_tokens.reshape(tokens.shape),
        gains[0].reshape(-1),
        sent_wq,
        sent_wkv.reshape(-1, heads_kv, 2 * HD),
        sent_wout,
        gains[1].reshape(-1),
        sent_gateup.reshape(-1, 2, units),
        sent_wdown,
    )


def solution(mesh):
    return jax.shard_map(
        shards,
        mesh=mesh,
        in_specs=(
            P("dp", "context", None),
            P("dp", "context"),
            P(),
            P(None, "tensor"),
            P(None, "tensor", None),
            P("tensor", None),
            P(),
            P(None, None, "tensor"),
            P("tensor", None),
            P("dp", "context", None),
        ),
        out_specs=(
            P("dp", "context", None),
            P("dp", "context", None),
            P(("dp", "context")),
            P(("dp", "context"), "tensor"),
            P(("dp", "context"), "tensor", None),
            P("tensor", ("dp", "context")),
            P(("dp", "context")),
            P(("dp", "context"), None, "tensor"),
            P("tensor", ("dp", "context")),
        ),
        check_vma=False,
    )
```
